32 devices in a mesh: seq: 16 (over z, y, x), tp: 2 (over core).
Axes of the slice: x: 2, y: 2, z: 4, core: 2. Of those that a mesh axis runs over, the one named last changes fastest.
Arguments:
- tokens: bfloat16 [24576, 768], P('seq'), may hold values from -6 to 6
- short_lengths: int32 [16, 3], P('seq'), may hold values from 1 to 512, 1024 in all within a row
- query_weight: bfloat16 [768, 768], P(None, 'tp'), may hold values from -0.21875 to 0.21875
- key_weight: bfloat16 [768, 768], P(None, 'tp'), may hold values from -0.21875 to 0.21875
- value_weight: bfloat16 [768, 768], P(None, 'tp'), may hold values from -0.21875 to 0.21875
- conv_kernel: float32 [12, 33], P('tp'), may hold values from -0.3 to 0.3
- out_weight: bfloat16 [768, 768], P('tp'), may hold values from -0.625 to 0.625
- gain_one: float32 [768], replicated, may hold values from 0.5 to 1.5
- bias_one: float32 [768], replicated, may hold values from -1 to 1
- inner_weight: bfloat16 [768, 3072], P(None, 'tp'), may hold values from -0.21875 to 0.21875
- outer_weight: bfloat16 [3072, 768], P('tp'), may hold values from -0.109375 to 0.109375
- gain_two: float32 [768], replicated, may hold values from 0.5 to 1.5
- bias_two: float32 [768], replicated, may hold values from -1 to 1
- cotangent: bfloat16 [24576, 768], P('seq'), may hold values from -6 to 6
Outputs:
- output: bfloat16 [24576, 768], P('seq')
- token_grad: float32 [24576, 768], P('seq')
- query_grad: float32 [768, 768], P(None, 'tp')
- key_grad: float32 [768, 768], P(None, 'tp')
- value_grad: float32 [768, 768], P(None, 'tp')
- kernel_grad: float32 [12, 33], P('tp')
- out_grad: float32 [768, 768], P('tp')
- gain_one_grad: float32 [768], replicated
- bias_one_grad: float32 [768], replicated
- inner_grad: float32 [768, 3072], P(None, 'tp')
- outer_grad: float32 [3072, 768], P('tp')
- gain_two_grad: float32 [768], replicated
- bias_two_grad: float32 [768], replicated
The draws below stay inside these ranges and needn't reach their ends.
Inputs may be any that keep to these rules, and one draw needn't show every extreme that they name: `short_lengths`: row d lists the lengths of device d's short items in order; they sum to 1024, and the largest of each row is exactly 512.
All inputs are finite; a program needn't handle non-finite values.
Results may differ from the reference program's by a relative error of at most 0.013.
Values may be sent and summed in bfloat16 or wider, within the bound.
No kernel may reach another device: no remote copies, remote signals or barrier semaphores. Data moves between devices by JAX's collectives and lax.ppermute only.
A program may use at most 320 MiB of HBM per device.

```python
import math
from functools import partial
import jax
import jax.numpy as jnp
import numpy as np
from jax import lax

D = 768
HEADS = 12
HEAD_DIM = 64
FF = 3072
TAU = 8
CONV_WIDTH = 33
HALF_WIDTH = 16
GROUP = 16
PIECE = 256
SHORT_DEV = 1024
SHORT_MOST = 512
SHORT_ITEMS = 3
LONG_LEN = 4096
LONG_ITEMS = 2
TOK_DEV = 1536
TOKENS = 24576
N_SEQ = 16


def shard_levels(own_key, extent, split, low, high):
    def one(axis_at, parts):
        heights = jax.random.uniform(jax.random.fold_in(jax.random.fold_in(own_key, 6), axis_at), (parts,), jnp.float32, low / len(split), high / len(split))
        return jnp.repeat(jnp.exp(heights), extent[axis_at] // parts).reshape((-1,) + (1,) * (len(extent) - axis_at - 1))

    factor_of = one(*split[0])
    for cut in split[1:]:
        factor_of = factor_of * one(*cut)
    return factor_of


def split_up(amount, total, limit, skew):
    portions = [(1 << 20) // math.isqrt(rank ** skew) + 1 for rank in range(2, amount + 1)]
    rest, given = total - limit - (amount - 1), [1] * (amount - 1)
    while rest > 0:
        free = [i for i in range(amount - 1) if given[i] < limit]
        pool, remaining = sum([portions[i] for i in free]), rest
        for i in free:
            addition = min(limit - given[i], max(1, remaining * portions[i] // pool), rest)
            given[i] = given[i] + addition
            rest = rest - addition
    return np.array([limit] + given)


def uneven(key, amount, total, reach, lean):
    if amount == 2:
        one = jax.random.randint(key, (), max(1, total - reach), min(reach, total - 1) + 1)
        return jnp.stack([one, total - one])
    tallies = jnp.asarray(split_up(amount, total, reach, lean), jnp.int32)
    twos = (amount - 1) // 2
    giver, sink = tallies[1:1 + 2 * twos:2], tallies[2:2 + 2 * twos:2]
    room = jnp.minimum(giver - 1, reach - sink)
    passed = jax.random.randint(jax.random.fold_in(key, 1), (twos,), 0, 1 << 20) % (room + 1)
    tallies = tallies.at[1:1 + 2 * twos:2].set(giver - passed).at[2:2 + 2 * twos:2].set(sink + passed)
    return tallies[jax.random.permutation(jax.random.fold_in(key, 2), amount)]


def centred(own_key, dims, scale, limit, pieces=(), held_as=jnp.bfloat16):
    level = shard_levels(own_key, dims, pieces, -0.22, 0.18) if pieces else 1.0
    values = jax.random.normal(own_key, dims, jnp.float32) * scale * level
    return jnp.minimum(jnp.maximum(values, -limit), limit).astype(held_as)


def setup_inputs(seed: int = 0) -> dict:
    key_list = jax.random.split(jax.random.key(seed), 15)
    return {
        "tokens": centred(key_list[0], (TOKENS, D), 1.0, 6.0, ((0, 16),)),
        "short_lengths": jax.vmap(lambda own: uneven(own, SHORT_ITEMS, SHORT_DEV, SHORT_MOST, 2))(jax.random.split(key_list[1], N_SEQ)).reshape((N_SEQ, SHORT_ITEMS)).astype(jnp.int32),
        "query_weight": centred(key_list[2], (D, D), D ** -0.5, 0.21875, ((1, 2),)),
        "key_weight": centred(key_list[3], (D, D), D ** -0.5, 0.21875, ((1, 2),)),
        "value_weight": centred(key_list[4], (D, D), D ** -0.5, 0.21875, ((1, 2),)),
        "conv_kernel": centred(key_list[5], (HEADS, CONV_WIDTH), 0.05, 0.3, ((0, 2),), jnp.float32),
        "out_weight": centred(key_list[6], (D, D), (D // 8) ** -0.5, 0.625, ((0, 2),)),
        "gain_one": jnp.clip(1.0 + 0.1 * jax.random.normal(key_list[7], (D,), jnp.float32), 0.5, 1.5),
        "bias_one": centred(key_list[8], (D,), 0.2, 1.0, (), jnp.float32),
        "inner_weight": centred(key_list[9], (D, FF), D ** -0.5, 0.21875, ((1, 2),)),
        "outer_weight": centred(key_list[10], (FF, D), FF ** -0.5, 0.109375, ((0, 2),)),
        "gain_two": jnp.clip(1.0 + 0.1 * jax.random.normal(key_list[11], (D,), jnp.float32), 0.5, 1.5),
        "bias_two": centred(key_list[12], (D,), 0.2, 1.0, (), jnp.float32),
        "cotangent": centred(key_list[13], (TOKENS, D), 1.0, 6.0, ((0, 16),)),
    }


@jax.custom_vjp
def low(v):
    return lax.optimization_barrier(v.astype(jnp.bfloat16)).astype(jnp.float32)

@jax.custom_vjp
def low_back(v):
    return v

def low_keep(v):
    return (low(v), None)

def low_pass(kept, grad):
    return (grad,)

def back_keep(v):
    return (v, None)

def back_low(kept, grad):
    return (low(grad),)
low.defvjp(low_keep, low_pass)
low_back.defvjp(back_keep, back_low)
HIGHEST = lax.Precision.HIGHEST
COS_SCALE = 0.98
EPS_UNIT = 1e-06
EPS_NORM = 1e-05

def unit_rows(values):
    return values * lax.rsqrt(lax.optimization_barrier(jnp.sum(values * values, axis=-1, keepdims=True)) + EPS_UNIT)

def layer_norm(values, gain, bias):
    row_mean = lax.optimization_barrier(jnp.mean(values, axis=-1, keepdims=True))
    centered = values - row_mean
    variance = lax.optimization_barrier(jnp.mean(centered * centered, axis=-1, keepdims=True))
    return centered * lax.rsqrt(variance + EPS_NORM) * gain + bias

def weigh_block(queries, key_rows, values, same_item):
    cosine = low_back(COS_SCALE * jnp.einsum('qhe,khe->hqk', queries, key_rows, precision=HIGHEST))
    weights = low((1.0 - jnp.arccos(cosine) / math.pi) ** TAU) * same_item[None]
    return jnp.einsum('hqk,khe->qhe', weights, values, precision=HIGHEST)

def convolve(values, item_ids, kernel):
    length = values.shape[0]
    padded = jnp.pad(values, ((HALF_WIDTH, HALF_WIDTH), (0, 0), (0, 0)))
    padded_ids = jnp.pad(item_ids, (HALF_WIDTH, HALF_WIDTH), constant_values=-1)
    running = jnp.zeros(values.shape, jnp.float32)
    for tap_index in range(CONV_WIDTH):
        same_item = (padded_ids[tap_index:tap_index + length] == item_ids).astype(jnp.float32)
        running = running + kernel[:, tap_index][None, :, None] * padded[tap_index:tap_index + length] * same_item[:, None, None]
    return running

def long_item(kernel, packed):
    queries, key_rows, values = packed
    length = queries.shape[0]
    block_rows = math.gcd(length, 512)
    all_ones = jnp.ones((block_rows, length), jnp.float32)
    blocks = queries.reshape(length // block_rows, block_rows, HEADS, HEAD_DIM)
    attended = lax.map(jax.checkpoint(lambda query_block: weigh_block(query_block, key_rows, values, all_ones)), blocks)
    item_ids = jnp.zeros((length,), jnp.int32)
    return attended.reshape(length, HEADS, HEAD_DIM) + jax.checkpoint(convolve)(values, item_ids, kernel)

def short_block(queries, key_rows, values, item_ids, kernel):
    same_item = (item_ids[:, None] == item_ids[None, :]).astype(jnp.float32)
    return weigh_block(queries, key_rows, values, same_item) + convolve(values, item_ids, kernel)

def short_pack(kernel, packed):
    return short_block(packed[0], packed[1], packed[2], packed[3], kernel)

def to_items(array):
    device_grid = array.reshape(N_SEQ, TOK_DEV, HEADS, HEAD_DIM)
    long_part = device_grid[:, :2 * PIECE].reshape(N_SEQ // GROUP, GROUP, PIECE, 2, HEADS, HEAD_DIM)
    long_part = jnp.transpose(long_part, (0, 3, 1, 2, 4, 5)).reshape(LONG_ITEMS, LONG_LEN, HEADS, HEAD_DIM)
    return (long_part, device_grid[:, 2 * PIECE:])

def forward(short_ids, tokens, query_weight, key_weight, value_weight, conv_kernel, out_weight, gain_one, bias_one, inner_weight, outer_weight, gain_two, bias_two):
    queries = low_back(jnp.dot(tokens, query_weight, precision=HIGHEST)).reshape(TOKENS, HEADS, HEAD_DIM)
    key_rows = low_back(jnp.dot(tokens, key_weight, precision=HIGHEST)).reshape(TOKENS, HEADS, HEAD_DIM)
    values = low(low_back(jnp.dot(tokens, value_weight, precision=HIGHEST))).reshape(TOKENS, HEADS, HEAD_DIM)
    query_unit = low(unit_rows(queries))
    key_unit = low(unit_rows(key_rows))
    long_query, short_query = to_items(query_unit)
    long_key, short_key = to_items(key_unit)
    long_value, short_value = to_items(values)
    long_out = lax.map(partial(long_item, conv_kernel), (long_query, long_key, long_value))
    short_out = lax.map(jax.checkpoint(partial(short_pack, conv_kernel)), (short_query, short_key, short_value, short_ids))
    long_rows = long_out.reshape(N_SEQ // GROUP, 2, GROUP, PIECE, HEADS, HEAD_DIM)
    long_rows = jnp.transpose(long_rows, (0, 2, 3, 1, 4, 5)).reshape(N_SEQ, 2 * PIECE, HEADS, HEAD_DIM)
    attention = jnp.concatenate([long_rows, short_out], axis=1).reshape(TOKENS, D)
    mixed_low = low(low_back(attention))
    projected = low_back(jnp.dot(mixed_low, out_weight, precision=HIGHEST))

    def finish(packed):
        hidden = packed[0] + packed[1]
        normed = layer_norm(hidden, gain_one, bias_one)
        pre_act = low_back(jnp.dot(low(normed), inner_weight, precision=HIGHEST))
        act_low = low(jax.nn.gelu(pre_act, approximate=False))
        ffn_out = low_back(jnp.dot(act_low, outer_weight, precision=HIGHEST))
        return layer_norm(normed + ffn_out, gain_two, bias_two)
    finished = lax.map(jax.checkpoint(finish), (tokens.reshape(N_SEQ, TOK_DEV, D), projected.reshape(N_SEQ, TOK_DEV, D)))
    return finished.reshape(TOKENS, D)

def reference(tokens, short_lengths, query_weight, key_weight, value_weight, conv_kernel, out_weight, gain_one, bias_one, inner_weight, outer_weight, gain_two, bias_two, cotangent):
    item_ends = jnp.cumsum(short_lengths, axis=1).astype(jnp.int32)
    positions = jnp.arange(SHORT_DEV, dtype=jnp.int32)
    short_ids = lax.optimization_barrier(jnp.sum((positions[None, :, None] >= item_ends[:, None, :]).astype(jnp.int32), axis=2)).astype(jnp.int32)
    floats = tuple((argument.astype(jnp.float32) for argument in (tokens, query_weight, key_weight, value_weight, conv_kernel, out_weight, gain_one, bias_one, inner_weight, outer_weight, gain_two, bias_two)))
    result, pullback = jax.vjp(partial(forward, short_ids), floats[0], floats[1], floats[2], floats[3], floats[4], floats[5], floats[6], floats[7], floats[8], floats[9], floats[10], floats[11])
    gradients = pullback(cotangent.astype(jnp.float32))
    return (result.astype(jnp.bfloat16), gradients[0], gradients[1], gradients[2], gradients[3], gradients[4], gradients[5], gradients[6], gradients[7], gradients[8], gradients[9], gradients[10], gradients[11])
```

```python
import math

import jax
import jax.numpy as jnp
from jax import lax
from jax.experimental import pallas as pl
from jax.experimental.pallas import tpu as pltpu
from jax.sharding import PartitionSpec as P

TAU = 8
CONV_WIDTH = 33
HALF_WIDTH = 16
GROUP = 16
PIECE = 256
ITEMS = 2
REACH = 128

COS_SCALE = 0.98
EPS_UNIT = 1e-06
EPS_NORM = 1e-05
NEAR_POLY = (1.158024787902832, -0.36302468180656433, 0.09245320409536362, -0.011449637822806835)
SLOPE_SCALE = TAU / math.pi
VMEM_BYTES = 60 * 2**20

F32 = jnp.float32
BF16 = jnp.bfloat16


def layer_norm(values, gain, bias):
    row_mean = jnp.mean(values, axis=-1, keepdims=True)
    centered = values - row_mean
    variance = jnp.mean(centered * centered, axis=-1, keepdims=True)
    return centered * lax.rsqrt(variance + EPS_NORM) * gain + bias


def exact_gelu(values):
    return jax.nn.gelu(values, approximate=False)


def contract(left, right, left_dim, right_dim):
    return lax.dot_general(
        left, right, (((left_dim,), (right_dim,)), ((), ())), preferred_element_type=F32
    )


def pair_terms(dots, same=None):
    upper = 1.0 / COS_SCALE + dots
    lower = 1.0 / COS_SCALE - dots
    upper_inv = lax.rsqrt(upper)
    lower_inv = lax.rsqrt(lower)
    wide = 1.0 / 0.7 + lower * lower_inv
    wide_inv = lax.rsqrt(wide)
    root = wide * wide_inv
    ratio = NEAR_POLY[3] * root + NEAR_POLY[2]
    ratio = ratio * root + NEAR_POLY[1]
    ratio = ratio * root + NEAR_POLY[0]
    near = ratio * ((upper * upper_inv) * wide_inv)
    if same is not None:
        near = jnp.where(same, near, 0.0)
    near_2 = near * near
    near_4 = near_2 * near_2
    weights = (near_4 * near_4).astype(BF16)
    slopes = ((near_4 * near_2) * (near * (upper_inv * lower_inv))).astype(BF16)
    return weights, slopes


def pad_lanes(dst, src, length):
    dst[:, pl.ds(0, REACH)] = jnp.zeros((dst.shape[0], REACH), dst.dtype)
    dst[:, pl.ds(REACH, length)] = src
    dst[:, pl.ds(REACH + length, REACH)] = jnp.zeros((dst.shape[0], REACH), dst.dtype)


def rows_of(dst, src, length):
    for start in range(0, length, PIECE):
        dst[pl.ds(start, PIECE), :] = src[:, pl.ds(start, PIECE)].T


def long_forward(query, key, value, band):
    head_dim, length = query.shape
    blocks = length // PIECE
    step = 512

    def body(q_ref, k_ref, v_ref, band_ref, o_ref, w_ref, s_ref, key_rows, value_pad):
        block = pl.program_id(0)

        @pl.when(block == 0)
        def _():
            rows_of(key_rows, k_ref, length)
            pad_lanes(value_pad, v_ref[...], length)

        q = q_ref[...]
        start = pl.multiple_of(block * PIECE, PIECE)
        total = contract(value_pad[:, pl.ds(start, PIECE + 2 * REACH)], band_ref[...], 1, 1)
        for at in range(0, length, step):
            dots = contract(key_rows[pl.ds(at, step), :], q, 1, 0)
            weights, slopes = pair_terms(dots)
            w_ref[pl.ds(at, step), :] = weights
            s_ref[pl.ds(at, step), :] = slopes
            total = total + contract(v_ref[:, pl.ds(at, step)], weights, 1, 0)
        o_ref[...] = total.astype(BF16)

    whole = pl.BlockSpec((head_dim, length), lambda i: (0, 0))
    large = pl.BlockSpec((None, length, PIECE), lambda i: (i, 0, 0))
    large_shape = jax.ShapeDtypeStruct((blocks, length, PIECE), BF16)
    return pl.pallas_call(
        body,
        grid=(blocks,),
        in_specs=[
            pl.BlockSpec((head_dim, PIECE), lambda i: (0, i)),
            whole,
            whole,
            pl.BlockSpec((PIECE, PIECE + 2 * REACH), lambda i: (0, 0)),
        ],
        out_specs=[pl.BlockSpec((None, head_dim, PIECE), lambda i: (i, 0, 0)), large, large],
        out_shape=[jax.ShapeDtypeStruct((blocks, head_dim, PIECE), BF16), large_shape, large_shape],
        scratch_shapes=[
            pltpu.VMEM((length, head_dim), BF16),
            pltpu.VMEM((head_dim, length + 2 * REACH), BF16),
        ],
        compiler_params=pltpu.CompilerParams(vmem_limit_bytes=VMEM_BYTES),
        cost_estimate=pl.CostEstimate(
            flops=length * length * 300, bytes_accessed=length * length * 4, transcendentals=0
        ),
    )(query, key, value, band)


def long_backward(query, key, value, grad, band, weights, slopes):
    head_dim, length = query.shape
    blocks = length // PIECE
    step = 1024

    def body(
        q_ref, k_ref, v_ref, g_ref, band_ref, w_ref, s_ref,
        dq_ref, dk_ref, dv_ref, taps_ref, value_rows, value_pad, grad_pad, key_sum, value_sum,
    ):
        block = pl.program_id(0)

        @pl.when(block == 0)
        def _():
            rows_of(value_rows, v_ref, length)
            pad_lanes(value_pad, v_ref[...], length)
            pad_lanes(grad_pad, g_ref[...], length)
            key_sum[...] = jnp.zeros_like(key_sum)
            value_sum[...] = jnp.zeros_like(value_sum)
            taps_ref[...] = jnp.zeros_like(taps_ref)

        start = pl.multiple_of(block * PIECE, PIECE)
        q = q_ref[...]
        g = g_ref[:, pl.ds(start, PIECE)]
        near_values = value_pad[:, pl.ds(start, PIECE + 2 * REACH)]
        near_grads = grad_pad[:, pl.ds(start, PIECE + 2 * REACH)]
        taps_ref[...] += contract(g.T, near_values, 1, 0)
        value_sum[:, pl.ds(start, PIECE)] += contract(near_grads, band_ref[...], 1, 1)
        total = jnp.zeros((head_dim, PIECE), F32)
        for at in range(0, length, step):
            grad_weights = contract(value_rows[pl.ds(at, step), :], g, 1, 0)
            terms = grad_weights.astype(BF16) * s_ref[pl.ds(at, step), :]
            total = total + contract(k_ref[:, pl.ds(at, step)], terms, 1, 0)
            key_sum[:, pl.ds(at, step)] += contract(q, terms, 1, 1)
            value_sum[:, pl.ds(at, step)] += contract(g, w_ref[pl.ds(at, step), :], 1, 1)
        dq_ref[...] = (total * SLOPE_SCALE).astype(BF16)

        @pl.when(block == blocks - 1)
        def _():
            for index in range(blocks):
                piece = pl.ds(index * PIECE, PIECE)
                dk_ref[index] = (key_sum[:, piece] * SLOPE_SCALE).astype(BF16)
                dv_ref[index] = value_sum[:, piece].astype(BF16)

    whole = pl.BlockSpec((head_dim, length), lambda i: (0, 0))
    large = pl.BlockSpec((None, length, PIECE), lambda i: (i, 0, 0))
    pieces = pl.BlockSpec((blocks, head_dim, PIECE), lambda i: (0, 0, 0))
    pieces_shape = jax.ShapeDtypeStruct((blocks, head_dim, PIECE), BF16)
    wide = PIECE + 2 * REACH
    return pl.pallas_call(
        body,
        grid=(blocks,),
        in_specs=[
            pl.BlockSpec((head_dim, PIECE), lambda i: (0, i)),
            whole,
            whole,
            whole,
            pl.BlockSpec((PIECE, wide), lambda i: (0, 0)),
            large,
            large,
        ],
        out_specs=[
            pl.BlockSpec((None, head_dim, PIECE), lambda i: (i, 0, 0)),
            pieces,
            pieces,
            pl.BlockSpec((PIECE, wide), lambda i: (0, 0)),
        ],
        out_shape=[pieces_shape] * 3 + [jax.ShapeDtypeStruct((PIECE, wide), F32)],
        scratch_shapes=[
            pltpu.VMEM((length, head_dim), BF16),
            pltpu.VMEM((head_dim, length + 2 * REACH), BF16),
            pltpu.VMEM((head_dim, length + 2 * REACH), BF16),
            pltpu.VMEM((head_dim, length), F32),
            pltpu.VMEM((head_dim, length), F32),
        ],
        compiler_params=pltpu.CompilerParams(vmem_limit_bytes=VMEM_BYTES),
        cost_estimate=pl.CostEstimate(
            flops=length * length * 300, bytes_accessed=length * length * 4, transcendentals=0
        ),
    )(query, key, value, grad, band, weights, slopes)


def short_forward(reach, ids_row, ids_col, query, key, value, band):
    heads, head_dim, length = query.shape
    blocks = length // PIECE
    wide = PIECE + 2 * REACH

    def body(
        reach_ref, row_ref, col_ref, q_ref, k_ref, v_ref, band_ref,
        o_ref, w_ref, s_ref, key_rows, value_pad, total,
    ):
        block = pl.program_id(0)

        @pl.when(block == 0)
        def _():
            for h in range(heads):
                rows_of(key_rows.at[h], k_ref.at[h], length)
                pad_lanes(value_pad.at[h], v_ref[h], length)

        start = pl.multiple_of(block * PIECE, PIECE)
        near = (col_ref[pl.ds(start, PIECE), :] == row_ref[:, pl.ds(start, wide)]).astype(F32)
        for h in range(heads):
            masked = (band_ref[h] * near).astype(BF16)
            total[h] = contract(value_pad[h, :, pl.ds(start, wide)], masked, 1, 1)

        own_ids = row_ref[:, pl.ds(start + REACH, PIECE)]

        def turn(step, carry):
            at = pl.multiple_of(step * PIECE, PIECE)
            same = col_ref[pl.ds(at, PIECE), :] == own_ids
            for h in range(heads):
                dots = contract(key_rows[h, pl.ds(at, PIECE), :], q_ref[h], 1, 0)
                weights, slopes = pair_terms(dots, same)
                w_ref[h, pl.ds(at, PIECE), :] = weights
                s_ref[h, pl.ds(at, PIECE), :] = slopes
                total[h] += contract(v_ref[h, :, pl.ds(at, PIECE)], weights, 1, 0)
            return carry

        lax.fori_loop(reach_ref[0, block], reach_ref[1, block], turn, 0)
        o_ref[...] = total[...].astype(BF16)

    whole = pl.BlockSpec((heads, head_dim, length), lambda i: (0, 0, 0))
    block_spec = pl.BlockSpec((heads, head_dim, PIECE), lambda i: (0, 0, i))
    large = pl.BlockSpec((None, heads, length, PIECE), lambda i: (i, 0, 0, 0))
    large_shape = jax.ShapeDtypeStruct((blocks, heads, length, PIECE), BF16)
    return pl.pallas_call(
        body,
        grid=(blocks,),
        in_specs=[
            pl.BlockSpec(memory_space=pltpu.SMEM),
            pl.BlockSpec((1, length + 2 * REACH), lambda i: (0, 0)),
            pl.BlockSpec((length, 1), lambda i: (0, 0)),
            block_spec,
            whole,
            whole,
            pl.BlockSpec((heads, PIECE, wide), lambda i: (0, 0, 0)),
        ],
        out_specs=[block_spec, large, large],
        out_shape=[jax.ShapeDtypeStruct((heads, head_dim, length), BF16), large_shape, large_shape],
        scratch_shapes=[
            pltpu.VMEM((heads, length, head_dim), BF16),
            pltpu.VMEM((heads, head_dim, length + 2 * REACH), BF16),
            pltpu.VMEM((heads, head_dim, PIECE), F32),
        ],
        compiler_params=pltpu.CompilerParams(vmem_limit_bytes=VMEM_BYTES),
        cost_estimate=pl.CostEstimate(
            flops=heads * length * length * 200,
            bytes_accessed=heads * length * length * 4,
            transcendentals=0,
        ),
    )(reach, ids_row, ids_col, query, key, value, band)


def short_backward(reach, ids_row, ids_col, query, key, value, grad, band, weights, slopes):
    heads, head_dim, length = query.shape
    blocks = length // PIECE
    wide = PIECE + 2 * REACH

    def body(
        reach_ref, row_ref, col_ref, q_ref, k_ref, v_ref, g_ref, band_ref, w_ref, s_ref,
        dq_ref, dk_ref, dv_ref, taps_ref, value_rows, value_pad, grad_pad,
    ):
        block = pl.program_id(0)

        @pl.when(block == 0)
        def _():
            for h in range(heads):
                rows_of(value_rows.at[h], v_ref.at[h], length)
                pad_lanes(value_pad.at[h], v_ref[h], length)
                pad_lanes(grad_pad.at[h], g_ref[h], length)
            dk_ref[...] = jnp.zeros_like(dk_ref)
            dv_ref[...] = jnp.zeros_like(dv_ref)
            taps_ref[...] = jnp.zeros_like(taps_ref)

        start = pl.multiple_of(block * PIECE, PIECE)
        near = (col_ref[pl.ds(start, PIECE), :] == row_ref[:, pl.ds(start, wide)]).astype(F32)
        for h in range(heads):
            masked = (band_ref[h] * near).astype(BF16)
            own = g_ref[h, :, pl.ds(start, PIECE)]
            taps_ref[h] += contract(own.T, value_pad[h, :, pl.ds(start, wide)], 1, 0) * near
            dv_ref[h, :, pl.ds(start, PIECE)] += contract(
                grad_pad[h, :, pl.ds(start, wide)], masked, 1, 1
            )
        dq_ref[...] = jnp.zeros_like(dq_ref)

        def turn(step, carry):
            at = pl.multiple_of(step * PIECE, PIECE)
            for h in range(heads):
                own = g_ref[h, :, pl.ds(start, PIECE)]
                grad_weights = contract(value_rows[h, pl.ds(at, PIECE), :], own, 1, 0)
                terms = grad_weights.astype(BF16) * s_ref[h, pl.ds(at, PIECE), :]
                dq_ref[h] += contract(k_ref[h, :, pl.ds(at, PIECE)], terms, 1, 0) * SLOPE_SCALE
                dk_ref[h, :, pl.ds(at, PIECE)] += contract(q_ref[h], terms, 1, 1) * SLOPE_SCALE
                dv_ref[h, :, pl.ds(at, PIECE)] += contract(own, w_ref[h, pl.ds(at, PIECE), :], 1, 1)
            return carry

        lax.fori_loop(reach_ref[0, block], reach_ref[1, block], turn, 0)

    whole = pl.BlockSpec((heads, head_dim, length), lambda i: (0, 0, 0))
    block_spec = pl.BlockSpec((heads, head_dim, PIECE), lambda i: (0, 0, i))
    large = pl.BlockSpec((None, heads, length, PIECE), lambda i: (i, 0, 0, 0))
    bands = pl.BlockSpec((heads, PIECE, wide), lambda i: (0, 0, 0))
    whole_shape = jax.ShapeDtypeStruct((heads, head_dim, length), F32)
    return pl.pallas_call(
        body,
        grid=(blocks,),
        in_specs=[
            pl.BlockSpec(memory_space=pltpu.SMEM),
            pl.BlockSpec((1, length + 2 * REACH), lambda i: (0, 0)),
            pl.BlockSpec((length, 1), lambda i: (0, 0)),
            block_spec,
            whole,
            whole,
            whole,
            bands,
            large,
            large,
        ],
        out_specs=[block_spec, whole, whole, bands],
        out_shape=[whole_shape] * 3 + [jax.ShapeDtypeStruct((heads, PIECE, wide), F32)],
        scratch_shapes=[
            pltpu.VMEM((heads, length, head_dim), BF16),
            pltpu.VMEM((heads, head_dim, length + 2 * REACH), BF16),
            pltpu.VMEM((heads, head_dim, length + 2 * REACH), BF16),
        ],
        compiler_params=pltpu.CompilerParams(vmem_limit_bytes=VMEM_BYTES),
        cost_estimate=pl.CostEstimate(
            flops=heads * length * length * 200,
            bytes_accessed=heads * length * length * 4,
            transcendentals=0,
        ),
    )(reach, ids_row, ids_col, query, key, value, grad, band, weights, slopes)


def band_of(taps):
    wide = PIECE + 2 * REACH
    first = REACH - HALF_WIDTH
    line = jnp.pad(taps, ((0, 0), (first, wide + 1 - first - CONV_WIDTH)))
    flat = jnp.tile(line, (1, PIECE))[:, : PIECE * wide]
    return flat.reshape(taps.shape[0], PIECE, wide)


def band_sums(products):
    heads, rows, wide = products.shape
    first = REACH - HALF_WIDTH
    flat = jnp.pad(products.reshape(heads, rows * wide), ((0, 0), (0, rows)))
    return jnp.sum(flat.reshape(heads, rows, wide + 1), axis=1)[:, first : first + CONV_WIDTH]


def across_tp(part):
    own = part.astype(BF16)
    other = lax.ppermute(own, "tp", [(0, 1), (1, 0)])
    return own.astype(F32) + other.astype(F32)


def sum_all(parts, axis):
    peers = lax.axis_size(axis)
    flat = jnp.concatenate([part.reshape(peers, -1, 768).astype(BF16) for part in parts], axis=1)
    pieces = lax.all_to_all(flat, axis, 0, 0)
    own = jnp.sum(pieces.astype(F32), axis=0).astype(BF16)
    gathered = lax.all_gather(own, axis, axis=0).astype(F32)
    sums, at = [], 0
    for part in parts:
        rows = part.size // peers // 768
        sums.append(gathered[:, at : at + rows].reshape(part.shape))
        at += rows
    return sums


def shards(
    tokens,
    short_lengths,
    query_weight,
    key_weight,
    value_weight,
    conv_kernel,
    out_weight,
    gain_one,
    bias_one,
    inner_weight,
    outer_weight,
    gain_two,
    bias_two,
    cotangent,
):
    row_total, width = tokens.shape
    heads_dev = conv_kernel.shape[0]
    head_cols = query_weight.shape[1]
    head_dim = head_cols // heads_dev
    long_rows = ITEMS * PIECE
    short_rows = row_total - long_rows
    units = ITEMS * heads_dev
    place = lax.axis_index("seq") % GROUP
    groups = [
        [first + i for i in range(GROUP)] for first in range(0, lax.axis_size("seq"), GROUP)
    ]

    def by_item(rows):
        long_part = rows[:long_rows].reshape(PIECE, ITEMS, rows.shape[1]).swapaxes(0, 1)
        return jnp.concatenate(
            [long_part.reshape(long_rows, rows.shape[1]), rows[long_rows:]], axis=0
        )

    def by_place(rows):
        long_part = rows[:long_rows].reshape(ITEMS, PIECE, rows.shape[1]).swapaxes(0, 1)
        return jnp.concatenate(
            [long_part.reshape(long_rows, rows.shape[1]), rows[long_rows:]], axis=0
        )

    def to_owner(parts):
        count = parts.shape[0]
        split = parts.reshape(count, heads_dev, head_dim, ITEMS, PIECE)
        split = jnp.transpose(split, (3, 1, 0, 2, 4)).reshape(units, count * head_dim, PIECE)
        split = jnp.pad(split, ((0, GROUP - units), (0, 0), (0, 0)))
        moved = lax.all_to_all(split, "seq", 0, 0, axis_index_groups=groups)
        return jnp.transpose(moved, (1, 0, 2)).reshape(count, head_dim, GROUP * PIECE)

    def from_owner(pieces):
        count = pieces.shape[1]
        moved = lax.all_to_all(pieces, "seq", 0, 0, axis_index_groups=groups)[:units]
        moved = moved.reshape(ITEMS, heads_dev, count, head_dim, PIECE)
        return jnp.transpose(moved, (2, 1, 3, 0, 4)).reshape(count, heads_dev, head_dim, long_rows)

    tokens = by_item(tokens)
    cotangent = by_item(cotangent)

    item_ends = jnp.cumsum(short_lengths[0])
    positions = jnp.arange(short_rows, dtype=jnp.int32)
    item_ids = jnp.sum((positions[:, None] >= item_ends[None, :]).astype(jnp.int32), axis=1)
    ids_row = jnp.pad(item_ids, (REACH, REACH), constant_values=-1)[None, :]
    ids_col = item_ids[:, None]
    item_starts = jnp.concatenate([jnp.zeros((1,), jnp.int32), item_ends[:-1]])
    block_first = jnp.arange(0, short_rows, PIECE, dtype=jnp.int32)
    block_last = block_first + (PIECE - 1)
    inside = (item_starts[None, :] <= block_last[:, None]) & (
        item_ends[None, :] > block_first[:, None]
    )
    lowest = jnp.min(jnp.where(inside, item_starts[None, :], short_rows), axis=1)
    highest = jnp.max(jnp.where(inside, item_ends[None, :], 0), axis=1)
    reach = jnp.stack([lowest // PIECE, (highest + PIECE - 1) // PIECE]).astype(jnp.int32)

    band = band_of(conv_kernel)
    band_back = band_of(conv_kernel[:, ::-1])
    unit_head = place % heads_dev
    long_band = lax.dynamic_index_in_dim(band, unit_head, 0, False).astype(BF16)
    long_band_back = lax.dynamic_index_in_dim(band_back, unit_head, 0, False).astype(BF16)

    weight_all = jnp.concatenate([query_weight, key_weight, value_weight], axis=1)
    projected = contract(weight_all, tokens, 0, 1).reshape(3, heads_dev, head_dim, row_total)
    raw = projected[:2]
    inverse = lax.rsqrt(jnp.sum(raw * raw, axis=2, keepdims=True) + EPS_UNIT)
    unit = raw * inverse
    packed = jnp.concatenate([unit.astype(BF16), projected[2:].astype(BF16)], axis=0)
    long_pack = to_owner(packed[..., :long_rows])
    short_pack = packed[..., long_rows:]

    short_att, short_w, short_s = short_forward(
        reach, ids_row, ids_col, short_pack[0], short_pack[1], short_pack[2], band
    )
    long_att, long_w, long_s = long_forward(long_pack[0], long_pack[1], long_pack[2], long_band)
    long_home = from_owner(long_att[:, None])[0]
    mixed = jnp.concatenate([long_home, short_att], axis=2).reshape(head_cols, row_total)

    hidden = tokens.astype(F32) + across_tp(contract(mixed, out_weight, 0, 0))
    normed, norm_one_back = jax.vjp(layer_norm, hidden, gain_one, bias_one)
    normed_low = normed.astype(BF16)
    pre_act = jnp.dot(normed_low, inner_weight, preferred_element_type=F32)
    act_rows, gelu_back = jax.vjp(exact_gelu, pre_act)
    act_low = act_rows.astype(BF16)
    ffn_out = across_tp(jnp.dot(act_low, outer_weight, preferred_element_type=F32))
    output, norm_two_back = jax.vjp(layer_norm, normed + ffn_out, gain_two, bias_two)
    grad_sum, gain_two_grad, bias_two_grad = norm_two_back(cotangent.astype(F32))
    grad_ffn_low = grad_sum.astype(BF16)
    outer_grad = contract(act_low, grad_ffn_low, 0, 0)
    grad_pre_low = gelu_back(contract(grad_ffn_low, outer_weight, 1, 1))[0].astype(BF16)
    inner_grad = contract(normed_low, grad_pre_low, 0, 0)
    grad_normed = grad_sum + across_tp(contract(grad_pre_low, inner_weight, 1, 1))
    grad_hidden, gain_one_grad, bias_one_grad = norm_one_back(grad_normed)
    grad_proj_low = grad_hidden.astype(BF16)
    grad_att = contract(out_weight, grad_proj_low, 1, 1).astype(BF16)
    grad_att = grad_att.reshape(heads_dev, head_dim, row_total)
    out_grad = contract(mixed, grad_proj_low, 1, 0)

    long_grad = to_owner(grad_att[None, ..., :long_rows])[0]
    short_dq, short_dk, short_dv, short_taps = short_backward(
        reach,
        ids_row,
        ids_col,
        short_pack[0],
        short_pack[1],
        short_pack[2],
        grad_att[..., long_rows:],
        band_back,
        short_w,
        short_s,
    )
    long_dq, long_dk, long_dv, long_taps = long_backward(
        long_pack[0], long_pack[1], long_pack[2], long_grad, long_band_back, long_w, long_s
    )
    owner = (jnp.arange(heads_dev) == unit_head) & (place < units)
    kernel_grad = band_sums(short_taps) + jnp.where(
        owner[:, None], band_sums(long_taps[None]), 0.0
    )
    long_back = from_owner(jnp.stack([long_dq, long_dk, long_dv], axis=1)).astype(F32)
    grads = jnp.concatenate(
        [long_back, jnp.stack([short_dq, short_dk, short_dv], axis=0)], axis=3
    )
    unit_grads = grads[:2]
    along = jnp.sum(unit * unit_grads, axis=2, keepdims=True)
    raw_grads = (unit_grads - unit * along) * inverse
    grads_low = jnp.concatenate([raw_grads, grads[2:]], axis=0).astype(BF16)
    grads_low = grads_low.reshape(3 * head_cols, row_total)
    weight_grads = contract(tokens, grads_low, 0, 1)
    token_grad = grad_hidden + across_tp(contract(grads_low, weight_all, 0, 1))

    inner_sum, outer_sum, out_sum = sum_all([inner_grad, outer_grad, out_grad], "seq")
    (qkv_sum,) = sum_all([weight_grads], "seq")
    small = lax.psum(
        (kernel_grad, gain_one_grad, bias_one_grad, gain_two_grad, bias_two_grad), "seq"
    )
    return (
        by_place(output.astype(BF16)),
        by_place(token_grad),
        qkv_sum[:, :head_cols],
        qkv_sum[:, head_cols : 2 * head_cols],
        qkv_sum[:, 2 * head_cols :],
        small[0],
        out_sum,
        small[1],
        small[2],
        inner_sum,
        outer_sum,
        small[3],
        small[4],
    )


def solution(mesh):
    rows = P("seq", None)
    columns = P(None, "tp")
    split_rows = P("tp", None)
    return jax.shard_map(
        shards,
        mesh=mesh,
        in_specs=(
            rows, rows, columns, columns, columns, split_rows, split_rows,
            P(), P(), columns, split_rows, P(), P(), rows,
        ),
        out_specs=(
            rows, rows, columns, columns, columns, split_rows, split_rows,
            P(), P(), columns, split_rows, P(), P(),
        ),
        check_vma=False,
    )
```

```python
import math

import jax
import jax.numpy as jnp
from jax import lax
from jax.experimental import pallas as pl
from jax.experimental.pallas import tpu as pltpu
from jax.sharding import PartitionSpec as P

TAU = 8
CONV_WIDTH = 33
HALF_WIDTH = 16
GROUP = 16
PIECE = 256
ITEMS = 2
REACH = 128

COS_SCALE = 0.98
EPS_UNIT = 1e-06
EPS_NORM = 1e-05
NEAR_POLY = (1.158024787902832, -0.36302468180656433, 0.09245320409536362, -0.011449637822806835)
TAIL_POLY = tuple(
    0.5 * a for a in (0.254829592, -0.284496736, 1.421413741, -1.453152027, 1.061405429)
)
SLOPE_SCALE = TAU / math.pi
VMEM_BYTES = 60 * 2**20

F32 = jnp.float32
BF16 = jnp.bfloat16


def norm_terms(values):
    centered = values - jnp.mean(values, axis=-1, keepdims=True)
    inverse = lax.rsqrt(jnp.mean(centered * centered, axis=-1, keepdims=True) + EPS_NORM)
    return centered * inverse, inverse


def norm_back(scaled, unit, inverse):
    along = jnp.mean(scaled * unit, axis=-1, keepdims=True)
    return inverse * (scaled - jnp.mean(scaled, axis=-1, keepdims=True) - unit * along)


def gelu_terms(values):
    share = 1.0 / (1.0 + (0.3275911 * math.sqrt(0.5)) * jnp.abs(values))
    bell = jnp.exp(-0.5 * (values * values))
    poly = TAIL_POLY[4] * share + TAIL_POLY[3]
    for coefficient in TAIL_POLY[2::-1]:
        poly = poly * share + coefficient
    tail = poly * (share * bell)
    below = jnp.where(values < 0.0, tail, 1.0 - tail)
    return values * below, below + values * (bell * (1.0 / math.sqrt(2.0 * math.pi)))


def place_of_item(rows):
    item_at = lax.broadcasted_iota(jnp.int32, (rows, rows), 0)
    place_at = lax.broadcasted_iota(jnp.int32, (rows, rows), 1)
    hit = item_at == (place_at & 1) * PIECE + (place_at >> 1)
    return jnp.where(hit, 1.0, 0.0).astype(BF16)


def lasting(microseconds):
    return pl.CostEstimate(flops=microseconds * 1_150_000_000, bytes_accessed=0, transcendentals=0)


def contract(left, right, left_dim, right_dim):
    return lax.dot_general(
        left, right, (((left_dim,), (right_dim,)), ((), ())), preferred_element_type=F32
    )


def pair_terms(dots, same=None):
    upper = 1.0 / COS_SCALE + dots
    lower = 1.0 / COS_SCALE - dots
    upper_inv = lax.rsqrt(upper)
    lower_inv = lax.rsqrt(lower)
    wide = 1.0 / 0.7 + lower * lower_inv
    wide_inv = lax.rsqrt(wide)
    root = wide * wide_inv
    ratio = NEAR_POLY[3] * root + NEAR_POLY[2]
    ratio = ratio * root + NEAR_POLY[1]
    ratio = ratio * root + NEAR_POLY[0]
    near = ratio * ((upper * upper_inv) * wide_inv)
    if same is not None:
        near = jnp.where(same, near, 0.0)
    near_2 = near * near
    near_4 = near_2 * near_2
    weights = (near_4 * near_4).astype(BF16)
    slopes = ((near_4 * near_2) * (near * (upper_inv * lower_inv))).astype(BF16)
    return weights, slopes


def banded(line):
    return pltpu.roll(
        jnp.broadcast_to(line, (PIECE, line.shape[1])), 0, 1, stride=1, stride_axis=0
    )


def reversed_rows(columns):
    at = lax.broadcasted_iota(jnp.int32, (PIECE, PIECE), 0)
    to = lax.broadcasted_iota(jnp.int32, (PIECE, PIECE), 1)
    flip = jnp.where(at + to == PIECE - 1, 1.0, 0.0).astype(BF16)
    return contract(flip, columns, 1, 1).astype(BF16)


def unbanded(products):
    wide = products.shape[1]
    turned = pltpu.roll(products, wide - (PIECE - 1), 1, stride=1, stride_axis=0)
    return jnp.sum(turned, axis=0, keepdims=True)


def pad_lanes(dst, src, length):
    dst[:, pl.ds(0, REACH)] = jnp.zeros((dst.shape[0], REACH), dst.dtype)
    dst[:, pl.ds(REACH, length)] = src
    dst[:, pl.ds(REACH + length, REACH)] = jnp.zeros((dst.shape[0], REACH), dst.dtype)


def rows_of(dst, src, length):
    for start in range(0, length, PIECE):
        dst[pl.ds(start, PIECE), :] = src[:, pl.ds(start, PIECE)].T


def long_forward(query, key, value, line):
    head_dim, length = query.shape
    blocks = length // PIECE
    step = 512

    def body(q_ref, k_ref, v_ref, line_ref, o_ref, w_ref, s_ref, key_rows, value_pad, band_ref):
        block = pl.program_id(0)

        @pl.when(block == 0)
        def _():
            rows_of(key_rows, k_ref, length)
            pad_lanes(value_pad, v_ref[...], length)
            band_ref[...] = banded(line_ref[...]).astype(BF16)

        q = q_ref[...]
        start = pl.multiple_of(block * PIECE, PIECE)
        total = contract(value_pad[:, pl.ds(start, PIECE + 2 * REACH)], band_ref[...], 1, 1)
        for at in range(0, length, step):
            dots = contract(key_rows[pl.ds(at, step), :], q, 1, 0)
            weights, slopes = pair_terms(dots)
            w_ref[pl.ds(at, step), :] = weights
            s_ref[pl.ds(at, step), :] = slopes
            total = total + contract(v_ref[:, pl.ds(at, step)], weights, 1, 0)
        o_ref[...] = total.astype(BF16)

    whole = pl.BlockSpec((head_dim, length), lambda i: (0, 0))
    large = pl.BlockSpec((None, length, PIECE), lambda i: (i, 0, 0))
    large_shape = jax.ShapeDtypeStruct((blocks, length, PIECE), BF16)
    return pl.pallas_call(
        body,
        grid=(blocks,),
        in_specs=[
            pl.BlockSpec((head_dim, PIECE), lambda i: (0, i)),
            whole,
            whole,
            pl.BlockSpec((1, PIECE + 2 * REACH), lambda i: (0, 0)),
        ],
        out_specs=[pl.BlockSpec((None, head_dim, PIECE), lambda i: (i, 0, 0)), large, large],
        out_shape=[jax.ShapeDtypeStruct((blocks, head_dim, PIECE), BF16), large_shape, large_shape],
        scratch_shapes=[
            pltpu.VMEM((length, head_dim), BF16),
            pltpu.VMEM((head_dim, length + 2 * REACH), BF16),
            pltpu.VMEM((PIECE, PIECE + 2 * REACH), BF16),
        ],
        compiler_params=pltpu.CompilerParams(vmem_limit_bytes=VMEM_BYTES),
        cost_estimate=lasting(70),
    )(query, key, value, line)


def long_back_values(value, grad, line, weights):
    head_dim, length = value.shape
    blocks = length // PIECE
    step = 1024
    wide = PIECE + 2 * REACH

    def body(
        v_ref, g_ref, line_ref, w_ref, dv_ref, taps_ref,
        value_pad, grad_pad, value_sum, band_ref, products,
    ):
        block = pl.program_id(0)

        @pl.when(block == 0)
        def _():
            pad_lanes(value_pad, v_ref[...], length)
            pad_lanes(grad_pad, g_ref[...], length)
            value_sum[...] = jnp.zeros_like(value_sum)
            products[...] = jnp.zeros_like(products)
            band_ref[...] = banded(line_ref[...]).astype(BF16)

        start = pl.multiple_of(block * PIECE, PIECE)
        g = g_ref[:, pl.ds(start, PIECE)]
        near_values = value_pad[:, pl.ds(start, wide)]
        near_grads = grad_pad[:, pl.ds(start, wide)]
        products[...] += contract(reversed_rows(g), near_values, 1, 0)
        value_sum[:, pl.ds(start, PIECE)] += contract(near_grads, band_ref[...], 1, 1)
        for at in range(0, length, step):
            value_sum[:, pl.ds(at, step)] += contract(g, w_ref[pl.ds(at, step), :], 1, 1)

        @pl.when(block == blocks - 1)
        def _():
            for index in range(blocks):
                dv_ref[index] = value_sum[:, pl.ds(index * PIECE, PIECE)].astype(BF16)
            taps_ref[...] = unbanded(products[...])

    whole = pl.BlockSpec((head_dim, length), lambda i: (0, 0))
    return pl.pallas_call(
        body,
        grid=(blocks,),
        in_specs=[
            whole,
            whole,
            pl.BlockSpec((1, wide), lambda i: (0, 0)),
            pl.BlockSpec((None, length, PIECE), lambda i: (i, 0, 0)),
        ],
        out_specs=[
            pl.BlockSpec((blocks, head_dim, PIECE), lambda i: (0, 0, 0)),
            pl.BlockSpec((1, wide), lambda i: (0, 0)),
        ],
        out_shape=[
            jax.ShapeDtypeStruct((blocks, head_dim, PIECE), BF16),
            jax.ShapeDtypeStruct((1, wide), F32),
        ],
        scratch_shapes=[
            pltpu.VMEM((head_dim, length + 2 * REACH), BF16),
            pltpu.VMEM((head_dim, length + 2 * REACH), BF16),
            pltpu.VMEM((head_dim, length), F32),
            pltpu.VMEM((PIECE, wide), BF16),
            pltpu.VMEM((PIECE, wide), F32),
        ],
        compiler_params=pltpu.CompilerParams(vmem_limit_bytes=VMEM_BYTES),
        cost_estimate=lasting(16),
    )(value, grad, line, weights)


def long_back_pairs(query, key, value, grad, slopes):
    head_dim, length = query.shape
    blocks = length // PIECE
    step = 1024

    def body(q_ref, k_ref, v_ref, g_ref, s_ref, dq_ref, dk_ref, value_rows, key_sum):
        block = pl.program_id(0)

        @pl.when(block == 0)
        def _():
            rows_of(value_rows, v_ref, length)
            key_sum[...] = jnp.zeros_like(key_sum)

        q = q_ref[...]
        g = g_ref[...]
        total = jnp.zeros((head_dim, PIECE), F32)
        for at in range(0, length, step):
            grad_weights = contract(value_rows[pl.ds(at, step), :], g, 1, 0)
            terms = grad_weights.astype(BF16) * s_ref[pl.ds(at, step), :]
            total = total + contract(k_ref[:, pl.ds(at, step)], terms, 1, 0)
            key_sum[:, pl.ds(at, step)] += contract(q, terms, 1, 1)
        dq_ref[...] = (total * SLOPE_SCALE).astype(BF16)

        @pl.when(block == blocks - 1)
        def _():
            for index in range(blocks):
                piece = key_sum[:, pl.ds(index * PIECE, PIECE)]
                dk_ref[index] = (piece * SLOPE_SCALE).astype(BF16)

    whole = pl.BlockSpec((head_dim, length), lambda i: (0, 0))
    piece = pl.BlockSpec((head_dim, PIECE), lambda i: (0, i))
    pieces_shape = jax.ShapeDtypeStruct((blocks, head_dim, PIECE), BF16)
    return pl.pallas_call(
        body,
        grid=(blocks,),
        in_specs=[
            piece,
            whole,
            whole,
            piece,
            pl.BlockSpec((None, length, PIECE), lambda i: (i, 0, 0)),
        ],
        out_specs=[
            pl.BlockSpec((None, head_dim, PIECE), lambda i: (i, 0, 0)),
            pl.BlockSpec((blocks, head_dim, PIECE), lambda i: (0, 0, 0)),
        ],
        out_shape=[pieces_shape] * 2,
        scratch_shapes=[
            pltpu.VMEM((length, head_dim), BF16),
            pltpu.VMEM((head_dim, length), F32),
        ],
        compiler_params=pltpu.CompilerParams(vmem_limit_bytes=VMEM_BYTES),
        cost_estimate=lasting(40),
    )(query, key, value, grad, slopes)


def short_forward(reach, ids_row, ids_col, pack, line):
    _, heads, head_dim, length = pack.shape
    blocks = length // PIECE
    wide = PIECE + 2 * REACH

    def body(
        reach_ref, row_ref, col_ref, q_ref, k_ref, v_ref, line_ref,
        o_ref, w_ref, s_ref, key_rows, value_pad, total, band_ref,
    ):
        block = pl.program_id(0)

        @pl.when(block == 0)
        def _():
            for h in range(heads):
                rows_of(key_rows.at[h], k_ref.at[h], length)
                pad_lanes(value_pad.at[h], v_ref[h], length)
                band_ref[h] = banded(line_ref[h])

        start = pl.multiple_of(block * PIECE, PIECE)
        near = (col_ref[pl.ds(start, PIECE), :] == row_ref[:, pl.ds(start, wide)]).astype(F32)
        for h in range(heads):
            masked = (band_ref[h] * near).astype(BF16)
            total[h] = contract(value_pad[h, :, pl.ds(start, wide)], masked, 1, 1)

        own_ids = row_ref[:, pl.ds(start + REACH, PIECE)]

        def turn(step, carry):
            at = pl.multiple_of(step * PIECE, PIECE)
            same = col_ref[pl.ds(at, PIECE), :] == own_ids
            for h in range(heads):
                dots = contract(key_rows[h, pl.ds(at, PIECE), :], q_ref[h], 1, 0)
                weights, slopes = pair_terms(dots, same)
                w_ref[h, pl.ds(at, PIECE), :] = weights
                s_ref[h, pl.ds(at, PIECE), :] = slopes
                total[h] += contract(v_ref[h, :, pl.ds(at, PIECE)], weights, 1, 0)
            return carry

        lax.fori_loop(reach_ref[0, block], reach_ref[1, block], turn, 0)
        o_ref[...] = total[...].astype(BF16)

    def packed(which):
        return pl.BlockSpec((None, heads, head_dim, length), lambda i: (which, 0, 0, 0))

    block_spec = pl.BlockSpec((heads, head_dim, PIECE), lambda i: (0, 0, i))
    large = pl.BlockSpec((None, heads, length, PIECE), lambda i: (i, 0, 0, 0))
    large_shape = jax.ShapeDtypeStruct((blocks, heads, length, PIECE), BF16)
    return pl.pallas_call(
        body,
        grid=(blocks,),
        in_specs=[
            pl.BlockSpec(memory_space=pltpu.SMEM),
            pl.BlockSpec((1, length + 2 * REACH), lambda i: (0, 0)),
            pl.BlockSpec((length, 1), lambda i: (0, 0)),
            pl.BlockSpec((None, heads, head_dim, PIECE), lambda i: (0, 0, 0, i)),
            packed(1),
            packed(2),
            pl.BlockSpec((heads, 1, wide), lambda i: (0, 0, 0)),
        ],
        out_specs=[block_spec, large, large],
        out_shape=[jax.ShapeDtypeStruct((heads, head_dim, length), BF16), large_shape, large_shape],
        scratch_shapes=[
            pltpu.VMEM((heads, length, head_dim), BF16),
            pltpu.VMEM((heads, head_dim, length + 2 * REACH), BF16),
            pltpu.VMEM((heads, head_dim, PIECE), F32),
            pltpu.VMEM((heads, PIECE, wide), F32),
        ],
        compiler_params=pltpu.CompilerParams(vmem_limit_bytes=VMEM_BYTES),
        cost_estimate=lasting(28),
    )(reach, ids_row, ids_col, pack, pack, pack, line)


def short_backward(
    part, parts, reach, ids_row, ids_col, pack, grad, line, weights, slopes
):
    _, all_heads, head_dim, length = pack.shape
    heads = all_heads // parts
    blocks = length // PIECE
    wide = PIECE + 2 * REACH

    def body(
        reach_ref, row_ref, col_ref, q_ref, k_ref, v_ref, g_ref, line_ref, w_ref, s_ref,
        dq_ref, dk_ref, dv_ref, taps_ref, value_rows, value_pad, grad_pad, band_ref, products,
    ):
        block = pl.program_id(0)

        @pl.when(block == 0)
        def _():
            for h in range(heads):
                rows_of(value_rows.at[h], v_ref.at[h], length)
                pad_lanes(value_pad.at[h], v_ref[h], length)
                pad_lanes(grad_pad.at[h], g_ref[h], length)
                band_ref[h] = banded(line_ref[h])
            dk_ref[...] = jnp.zeros_like(dk_ref)
            dv_ref[...] = jnp.zeros_like(dv_ref)
            products[...] = jnp.zeros_like(products)

        start = pl.multiple_of(block * PIECE, PIECE)
        near = (col_ref[pl.ds(start, PIECE), :] == row_ref[:, pl.ds(start, wide)]).astype(F32)
        at = lax.broadcasted_iota(jnp.int32, (PIECE, PIECE), 0)
        to = lax.broadcasted_iota(jnp.int32, (PIECE, PIECE), 1)
        flip = jnp.where(at + to == PIECE - 1, 1.0, 0.0).astype(BF16)
        near_flip = contract(flip, near.astype(BF16), 1, 0)
        for h in range(heads):
            masked = (band_ref[h] * near).astype(BF16)
            own = g_ref[h, :, pl.ds(start, PIECE)]
            products[h] += (
                contract(reversed_rows(own), value_pad[h, :, pl.ds(start, wide)], 1, 0) * near_flip
            )
            dv_ref[h, :, pl.ds(start, PIECE)] += contract(
                grad_pad[h, :, pl.ds(start, wide)], masked, 1, 1
            )
        dq_ref[...] = jnp.zeros_like(dq_ref)

        def turn(step, carry):
            at = pl.multiple_of(step * PIECE, PIECE)
            for h in range(heads):
                own = g_ref[h, :, pl.ds(start, PIECE)]
                grad_weights = contract(value_rows[h, pl.ds(at, PIECE), :], own, 1, 0)
                terms = grad_weights.astype(BF16) * s_ref[h, pl.ds(at, PIECE), :]
                dq_ref[h] += contract(k_ref[h, :, pl.ds(at, PIECE)], terms, 1, 0) * SLOPE_SCALE
                dk_ref[h, :, pl.ds(at, PIECE)] += contract(q_ref[h], terms, 1, 1) * SLOPE_SCALE
                dv_ref[h, :, pl.ds(at, PIECE)] += contract(own, w_ref[h, pl.ds(at, PIECE), :], 1, 1)
            return carry

        lax.fori_loop(reach_ref[0, block], reach_ref[1, block], turn, 0)

        @pl.when(block == blocks - 1)
        def _():
            for h in range(heads):
                taps_ref[h] = unbanded(products[h])

    def packed(which):
        return pl.BlockSpec((None, heads, head_dim, length), lambda i: (which, part, 0, 0))

    whole = pl.BlockSpec((heads, head_dim, length), lambda i: (0, 0, 0))
    large = pl.BlockSpec((None, heads, length, PIECE), lambda i: (i, part, 0, 0))
    whole_shape = jax.ShapeDtypeStruct((heads, head_dim, length), F32)
    return pl.pallas_call(
        body,
        grid=(blocks,),
        in_specs=[
            pl.BlockSpec(memory_space=pltpu.SMEM),
            pl.BlockSpec((1, length + 2 * REACH), lambda i: (0, 0)),
            pl.BlockSpec((length, 1), lambda i: (0, 0)),
            pl.BlockSpec((None, heads, head_dim, PIECE), lambda i: (0, part, 0, i)),
            packed(1),
            packed(2),
            pl.BlockSpec((heads, head_dim, length), lambda i: (part, 0, 0)),
            pl.BlockSpec((heads, 1, wide), lambda i: (part, 0, 0)),
            large,
            large,
        ],
        out_specs=[
            pl.BlockSpec((heads, head_dim, PIECE), lambda i: (0, 0, i)),
            whole,
            whole,
            pl.BlockSpec((heads, 1, wide), lambda i: (0, 0, 0)),
        ],
        out_shape=[whole_shape] * 3 + [jax.ShapeDtypeStruct((heads, 1, wide), F32)],
        scratch_shapes=[
            pltpu.VMEM((heads, length, head_dim), BF16),
            pltpu.VMEM((heads, head_dim, length + 2 * REACH), BF16),
            pltpu.VMEM((heads, head_dim, length + 2 * REACH), BF16),
            pltpu.VMEM((heads, PIECE, wide), F32),
            pltpu.VMEM((heads, PIECE, wide), F32),
        ],
        compiler_params=pltpu.CompilerParams(vmem_limit_bytes=VMEM_BYTES),
        cost_estimate=lasting(28),
    )(reach, ids_row, ids_col, pack, pack, pack, grad, line, weights, slopes)


def project_in(tokens, query_weight, key_weight, value_weight, heads):
    row_total, width = tokens.shape
    cols = query_weight.shape[1]
    head_dim = cols // heads
    blocks = row_total // PIECE
    long_rows = ITEMS * PIECE

    def body(t_ref, wq_ref, wk_ref, wv_ref, long_ref, short_ref, unit_ref, inv_ref, turned, rows):
        block = pl.program_id(0)

        @pl.when(block == 0)
        def _():
            for index, ref in enumerate((wq_ref, wk_ref, wv_ref)):
                turned[pl.ds(index * cols, cols), :] = ref[...].T
            long_ref[pl.ds(ITEMS * heads, GROUP - ITEMS * heads)] = jnp.zeros(
                (GROUP - ITEMS * heads, 3 * head_dim, PIECE), BF16
            )

        @pl.when(block < ITEMS)
        def _():
            item_at = lax.broadcasted_iota(jnp.int32, (PIECE, long_rows), 0)
            place_at = lax.broadcasted_iota(jnp.int32, (PIECE, long_rows), 1)
            pick = jnp.where(place_at == ITEMS * item_at + block, 1.0, 0.0).astype(BF16)
            rows[...] = contract(pick, t_ref[pl.ds(0, long_rows), :], 1, 0).astype(BF16)

        @pl.when(block >= ITEMS)
        def _():
            rows[...] = t_ref[pl.ds(pl.multiple_of(block * PIECE, PIECE), PIECE), :]

        parts = contract(turned[...], rows[...], 1, 1).reshape(3, heads, head_dim, PIECE)
        raw = parts[:2]
        inverse = lax.rsqrt(jnp.sum(raw * raw, axis=2, keepdims=True) + EPS_UNIT)
        unit = raw * inverse
        unit_ref[...] = unit
        inv_ref[...] = inverse
        low = unit.astype(BF16)
        short_ref[:2] = low
        short_ref[2] = parts[2].astype(BF16)

        @pl.when(block < ITEMS)
        def _():
            for h in range(heads):
                unit_at = block * heads + h
                long_ref[unit_at, pl.ds(0, head_dim), :] = low[0, h]
                long_ref[unit_at, pl.ds(head_dim, head_dim), :] = low[1, h]
                long_ref[unit_at, pl.ds(2 * head_dim, head_dim), :] = parts[2, h].astype(BF16)

    weight = pl.BlockSpec((width, cols), lambda i: (0, 0))
    return pl.pallas_call(
        body,
        grid=(blocks,),
        in_specs=[pl.BlockSpec((row_total, width), lambda i: (0, 0)), weight, weight, weight],
        out_specs=[
            pl.BlockSpec((GROUP, 3 * head_dim, PIECE), lambda i: (0, 0, 0)),
            pl.BlockSpec(
                (3, heads, head_dim, PIECE), lambda i: (0, 0, 0, jnp.maximum(i - ITEMS, 0))
            ),
            pl.BlockSpec((2, heads, head_dim, PIECE), lambda i: (0, 0, 0, i)),
            pl.BlockSpec((2, heads, 1, PIECE), lambda i: (0, 0, 0, i)),
        ],
        out_shape=[
            jax.ShapeDtypeStruct((GROUP, 3 * head_dim, PIECE), BF16),
            jax.ShapeDtypeStruct((3, heads, head_dim, row_total - long_rows), BF16),
            jax.ShapeDtypeStruct((2, heads, head_dim, row_total), F32),
            jax.ShapeDtypeStruct((2, heads, 1, row_total), F32),
        ],
        scratch_shapes=[pltpu.VMEM((3 * cols, width), BF16), pltpu.VMEM((PIECE, width), BF16)],
        compiler_params=pltpu.CompilerParams(vmem_limit_bytes=VMEM_BYTES),
        cost_estimate=lasting(10),
    )(tokens, query_weight, key_weight, value_weight)


def project_out(moved, short_att, out_weight):
    heads, head_dim, short_rows = short_att.shape
    cols, width = out_weight.shape
    span = ITEMS * PIECE
    blocks = 1 + short_rows // span

    def body(m_ref, a_ref, w_ref, mixed_ref, part_ref, items):
        block = pl.program_id(0)

        @pl.when(block == 0)
        def _():
            for h in range(heads):
                for item in range(ITEMS):
                    items[pl.ds(h * head_dim, head_dim), pl.ds(item * PIECE, PIECE)] = m_ref[
                        item * heads + h
                    ]
            mixed_ref[...] = contract(items[...], place_of_item(span), 1, 0).astype(BF16)

        @pl.when(block > 0)
        def _():
            mixed_ref[...] = a_ref[...].reshape(cols, span)

        part_ref[...] = contract(mixed_ref[...], w_ref[...], 0, 0).astype(BF16)

    return pl.pallas_call(
        body,
        grid=(blocks,),
        in_specs=[
            pl.BlockSpec((GROUP, head_dim, PIECE), lambda i: (0, 0, 0)),
            pl.BlockSpec((heads, head_dim, span), lambda i: (0, 0, jnp.maximum(i - 1, 0))),
            pl.BlockSpec((cols, width), lambda i: (0, 0)),
        ],
        out_specs=[
            pl.BlockSpec((cols, span), lambda i: (0, i)),
            pl.BlockSpec((span, width), lambda i: (i, 0)),
        ],
        out_shape=[
            jax.ShapeDtypeStruct((cols, span * blocks), BF16),
            jax.ShapeDtypeStruct((span * blocks, width), BF16),
        ],
        scratch_shapes=[pltpu.VMEM((cols, span), BF16)],
        compiler_params=pltpu.CompilerParams(vmem_limit_bytes=VMEM_BYTES),
        cost_estimate=lasting(5),
    )(moved, short_att, out_weight)


def feed_forward(tokens, own, other, gain, bias, inner_weight, outer_weight):
    row_total, width = tokens.shape
    hidden_units = inner_weight.shape[1]

    def body(
        t_ref, own_ref, other_ref, gain_ref, bias_ref, inner_ref, outer_ref,
        unit_ref, inv_ref, low_ref, act_ref, slope_ref, part_ref,
    ):
        hidden = t_ref[...].astype(F32) + (
            own_ref[...].astype(F32) + other_ref[...].astype(F32)
        )
        unit, inverse = norm_terms(hidden)
        unit_ref[...] = unit
        inv_ref[...] = inverse
        low = (unit * gain_ref[...] + bias_ref[...]).astype(BF16)
        low_ref[...] = low
        act, slope = gelu_terms(contract(low, inner_ref[...], 1, 0))
        act = act.astype(BF16)
        act_ref[...] = act
        slope_ref[...] = slope.astype(BF16)
        part_ref[...] = contract(act, outer_ref[...], 1, 0).astype(BF16)

    rows = pl.BlockSpec((PIECE, width), lambda i: (i, 0))
    units = pl.BlockSpec((PIECE, hidden_units), lambda i: (i, 0))
    line = pl.BlockSpec((1, width), lambda i: (0, 0))
    return pl.pallas_call(
        body,
        grid=(row_total // PIECE,),
        in_specs=[
            rows, rows, rows, line, line,
            pl.BlockSpec((width, hidden_units), lambda i: (0, 0)),
            pl.BlockSpec((hidden_units, width), lambda i: (0, 0)),
        ],
        out_specs=[rows, pl.BlockSpec((PIECE, 1), lambda i: (i, 0)), rows, units, units, rows],
        out_shape=[
            jax.ShapeDtypeStruct((row_total, width), F32),
            jax.ShapeDtypeStruct((row_total, 1), F32),
            jax.ShapeDtypeStruct((row_total, width), BF16),
            jax.ShapeDtypeStruct((row_total, hidden_units), BF16),
            jax.ShapeDtypeStruct((row_total, hidden_units), BF16),
            jax.ShapeDtypeStruct((row_total, width), BF16),
        ],
        compiler_params=pltpu.CompilerParams(vmem_limit_bytes=VMEM_BYTES),
        cost_estimate=lasting(20),
    )(tokens, own, other, gain, bias, inner_weight, outer_weight)


def feed_back(
    unit_one, own, other, gain_one, bias_one, gain_two, bias_two, cotangent, slope,
    inner_weight, outer_weight,
):
    row_total, width = unit_one.shape
    hidden_units = inner_weight.shape[1]

    def body(
        unit_ref, own_ref, other_ref, gain_one_ref, bias_one_ref, gain_ref, bias_ref, g_ref,
        slope_ref, inner_ref, outer_ref,
        out_ref, sum_ref, low_ref, pre_ref, part_ref, gain_grad_ref, bias_grad_ref,
    ):
        @pl.when(pl.program_id(0) == 0)
        def _():
            gain_grad_ref[...] = jnp.zeros_like(gain_grad_ref)
            bias_grad_ref[...] = jnp.zeros_like(bias_grad_ref)

        normed = unit_ref[...] * gain_one_ref[...] + bias_one_ref[...]
        unit, inverse = norm_terms(
            normed + (own_ref[...].astype(F32) + other_ref[...].astype(F32))
        )
        out_ref[...] = (unit * gain_ref[...] + bias_ref[...]).astype(BF16)
        g = g_ref[...].astype(F32)
        gain_grad_ref[...] += jnp.sum(g * unit, axis=0, keepdims=True)
        bias_grad_ref[...] += jnp.sum(g, axis=0, keepdims=True)
        grad_sum = norm_back(g * gain_ref[...], unit, inverse)
        sum_ref[...] = grad_sum
        low = grad_sum.astype(BF16)
        low_ref[...] = low
        pre = contract(low, outer_ref[...], 1, 1) * slope_ref[...].astype(F32)
        pre = pre.astype(BF16)
        pre_ref[...] = pre
        part_ref[...] = contract(pre, inner_ref[...], 1, 1).astype(BF16)

    rows = pl.BlockSpec((PIECE, width), lambda i: (i, 0))
    units = pl.BlockSpec((PIECE, hidden_units), lambda i: (i, 0))
    line = pl.BlockSpec((1, width), lambda i: (0, 0))
    return pl.pallas_call(
        body,
        grid=(row_total // PIECE,),
        in_specs=[
            rows, rows, rows, line, line, line, line, rows, units,
            pl.BlockSpec((width, hidden_units), lambda i: (0, 0)),
            pl.BlockSpec((hidden_units, width), lambda i: (0, 0)),
        ],
        out_specs=[rows, rows, rows, units, rows, line, line],
        out_shape=[
            jax.ShapeDtypeStruct((row_total, width), BF16),
            jax.ShapeDtypeStruct((row_total, width), F32),
            jax.ShapeDtypeStruct((row_total, width), BF16),
            jax.ShapeDtypeStruct((row_total, hidden_units), BF16),
            jax.ShapeDtypeStruct((row_total, width), BF16),
            jax.ShapeDtypeStruct((1, width), F32),
            jax.ShapeDtypeStruct((1, width), F32),
        ],
        compiler_params=pltpu.CompilerParams(vmem_limit_bytes=VMEM_BYTES),
        cost_estimate=lasting(18),
    )(
        unit_one, own, other, gain_one, bias_one, gain_two, bias_two, cotangent, slope,
        inner_weight, outer_weight,
    )


def project_back(unit, inverse, grad_sum, own, other, gain, out_weight, heads):
    row_total, width = unit.shape
    cols = out_weight.shape[0]
    head_dim = cols // heads
    span = ITEMS * PIECE
    blocks = row_total // span

    def body(
        unit_ref, inv_ref, sum_ref, own_ref, other_ref, gain_ref, w_ref,
        hidden_ref, low_ref, long_ref, short_ref, gain_grad_ref, bias_grad_ref,
    ):
        block = pl.program_id(0)

        @pl.when(block == 0)
        def _():
            gain_grad_ref[...] = jnp.zeros_like(gain_grad_ref)
            bias_grad_ref[...] = jnp.zeros_like(bias_grad_ref)

        unit = unit_ref[...]
        grad = sum_ref[...] + (own_ref[...].astype(F32) + other_ref[...].astype(F32))
        gain_grad_ref[...] += jnp.sum(grad * unit, axis=0, keepdims=True)
        bias_grad_ref[...] += jnp.sum(grad, axis=0, keepdims=True)
        hidden = norm_back(grad * gain_ref[...], unit, inv_ref[...])
        hidden_ref[...] = hidden
        low = hidden.astype(BF16)
        low_ref[...] = low
        att = contract(w_ref[...], low, 1, 1).astype(BF16)

        @pl.when(block == 0)
        def _():
            items = contract(att, place_of_item(span), 1, 1).astype(BF16)
            for h in range(heads):
                for item in range(ITEMS):
                    long_ref[item * heads + h] = items[
                        h * head_dim : (h + 1) * head_dim, item * PIECE : (item + 1) * PIECE
                    ]
            long_ref[pl.ds(ITEMS * heads, GROUP - ITEMS * heads)] = jnp.zeros(
                (GROUP - ITEMS * heads, head_dim, PIECE), BF16
            )

        short_ref[...] = att.reshape(heads, head_dim, span)

    rows = pl.BlockSpec((span, width), lambda i: (i, 0))
    line = pl.BlockSpec((1, width), lambda i: (0, 0))
    return pl.pallas_call(
        body,
        grid=(blocks,),
        in_specs=[
            rows, pl.BlockSpec((span, 1), lambda i: (i, 0)), rows, rows, rows, line,
            pl.BlockSpec((cols, width), lambda i: (0, 0)),
        ],
        out_specs=[
            rows,
            rows,
            pl.BlockSpec((GROUP, head_dim, PIECE), lambda i: (0, 0, 0)),
            pl.BlockSpec((heads, head_dim, span), lambda i: (0, 0, jnp.maximum(i - 1, 0))),
            line,
            line,
        ],
        out_shape=[
            jax.ShapeDtypeStruct((row_total, width), F32),
            jax.ShapeDtypeStruct((row_total, width), BF16),
            jax.ShapeDtypeStruct((GROUP, head_dim, PIECE), BF16),
            jax.ShapeDtypeStruct((heads, head_dim, row_total - span), BF16),
            jax.ShapeDtypeStruct((1, width), F32),
            jax.ShapeDtypeStruct((1, width), F32),
        ],
        compiler_params=pltpu.CompilerParams(vmem_limit_bytes=VMEM_BYTES),
        cost_estimate=lasting(12),
    )(unit, inverse, grad_sum, own, other, gain, out_weight)


def unit_back(moved_pairs, moved_values, short_parts, unit, inverse):
    heads, head_dim = unit.shape[1:3]
    short_heads, _, short_rows = short_parts[0][0].shape
    count = len(short_parts)
    span = ITEMS * PIECE
    blocks = 1 + short_rows // span
    cols = heads * head_dim

    def body(*refs):
        pairs_ref, values_ref = refs[:2]
        short_refs = refs[2 : 2 + 3 * count]
        unit_ref, inv_ref, out_ref, items = refs[2 + 3 * count :]
        block = pl.program_id(0)

        def short_part(which):
            return jnp.concatenate([short_refs[3 * at + which][...] for at in range(count)], axis=0)

        def back(which, grad):
            unit = unit_ref[which]
            along = jnp.sum(unit * grad, axis=1, keepdims=True)
            return ((grad - unit * along) * inv_ref[which]).astype(BF16).reshape(cols, span)

        @pl.when(block == 0)
        def _():
            def long_part(ref, at):
                part = pl.ds(at, head_dim)
                heads_of = [
                    jnp.concatenate([ref[h, part, :], ref[heads + h, part, :]], axis=1)
                    for h in range(heads)
                ]
                return jnp.stack(heads_of, axis=0)

            for which in range(2):
                items[pl.ds(which * cols, cols), :] = back(
                    which, long_part(pairs_ref, which * head_dim).astype(F32)
                )
            items[pl.ds(2 * cols, cols), :] = long_part(values_ref, 0).reshape(cols, span)
            out_ref[...] = contract(items[...], place_of_item(span), 1, 0).astype(BF16)

        @pl.when(block > 0)
        def _():
            out_ref[pl.ds(0, cols), :] = back(0, short_part(0))
            out_ref[pl.ds(cols, cols), :] = back(1, short_part(1))
            out_ref[pl.ds(2 * cols, cols), :] = short_part(2).astype(BF16).reshape(
                cols, span
            )

    short = pl.BlockSpec(
        (short_heads, head_dim, span), lambda i: (0, 0, jnp.maximum(i - 1, 0))
    )
    return pl.pallas_call(
        body,
        grid=(blocks,),
        in_specs=[
            pl.BlockSpec((GROUP, moved_pairs.shape[1], PIECE), lambda i: (0, 0, 0)),
            pl.BlockSpec((GROUP, head_dim, PIECE), lambda i: (0, 0, 0)),
        ]
        + [short] * (3 * count)
        + [
            pl.BlockSpec((2, heads, head_dim, span), lambda i: (0, 0, 0, i)),
            pl.BlockSpec((2, heads, 1, span), lambda i: (0, 0, 0, i)),
        ],
        out_specs=pl.BlockSpec((3 * cols, span), lambda i: (0, i)),
        out_shape=jax.ShapeDtypeStruct((3 * cols, span * blocks), BF16),
        scratch_shapes=[pltpu.VMEM((3 * cols, span), BF16)],
        compiler_params=pltpu.CompilerParams(vmem_limit_bytes=VMEM_BYTES),
        cost_estimate=lasting(8),
    )(moved_pairs, moved_values, *sum(map(tuple, short_parts), ()), unit, inverse)


def other_half(part):
    return lax.ppermute(part, "tp", [(0, 1), (1, 0)])


def halves(part, bits, bit):
    mine = (lax.axis_index("seq") >> bit) & 1
    axis = bits.index(bit)
    return tuple(
        lax.dynamic_index_in_dim(part, side, axis, False) for side in (1 - mine, mine)
    )


def across_bit(sent, kept, bit):
    peers = lax.axis_size("seq")
    came = lax.ppermute(sent, "seq", [(i, i ^ (1 << bit)) for i in range(peers)])
    return (kept.astype(F32) + came.astype(F32)).astype(BF16)


def after(first, second):
    return lax.optimization_barrier((first, second))


def shards(
    tokens,
    short_lengths,
    query_weight,
    key_weight,
    value_weight,
    conv_kernel,
    out_weight,
    gain_one,
    bias_one,
    inner_weight,
    outer_weight,
    gain_two,
    bias_two,
    cotangent,
):
    row_total, width = tokens.shape
    heads_dev = conv_kernel.shape[0]
    head_cols = query_weight.shape[1]
    head_dim = head_cols // heads_dev
    short_rows = row_total - ITEMS * PIECE
    units = ITEMS * heads_dev
    place = lax.axis_index("seq") % GROUP
    groups = [
        [first + i for i in range(GROUP)] for first in range(0, lax.axis_size("seq"), GROUP)
    ]

    def exchange(pieces):
        return lax.all_to_all(pieces, "seq", 0, 0, axis_index_groups=groups)

    def by_position(moved, count):
        return jnp.transpose(moved, (1, 0, 2)).reshape(count, head_dim, GROUP * PIECE)

    item_ends = jnp.cumsum(short_lengths[0])
    positions = jnp.arange(short_rows, dtype=jnp.int32)
    item_ids = jnp.sum((positions[:, None] >= item_ends[None, :]).astype(jnp.int32), axis=1)
    ids_row = jnp.pad(item_ids, (REACH, REACH), constant_values=-1)[None, :]
    ids_col = item_ids[:, None]
    item_starts = jnp.concatenate([jnp.zeros((1,), jnp.int32), item_ends[:-1]])
    block_first = jnp.arange(0, short_rows, PIECE, dtype=jnp.int32)
    block_last = block_first + (PIECE - 1)
    inside = (item_starts[None, :] <= block_last[:, None]) & (
        item_ends[None, :] > block_first[:, None]
    )
    lowest = jnp.min(jnp.where(inside, item_starts[None, :], short_rows), axis=1)
    highest = jnp.max(jnp.where(inside, item_ends[None, :], 0), axis=1)
    reach = jnp.stack([lowest // PIECE, (highest + PIECE - 1) // PIECE]).astype(jnp.int32)

    first_tap = REACH - HALF_WIDTH
    tap_pad = ((0, 0), (first_tap, PIECE + 2 * REACH - first_tap - CONV_WIDTH))
    lines = jnp.pad(conv_kernel, tap_pad)[:, None, :]
    lines_back = jnp.pad(conv_kernel[:, ::-1], tap_pad)[:, None, :]
    unit_head = place % heads_dev
    long_line = lax.dynamic_index_in_dim(lines, unit_head, 0, False)
    long_line_back = lax.dynamic_index_in_dim(lines_back, unit_head, 0, False)

    long_send, short_pack, unit, inverse = project_in(
        tokens, query_weight, key_weight, value_weight, heads_dev
    )
    long_moved = exchange(long_send)
    short_att, short_w, short_s = short_forward(reach, ids_row, ids_col, short_pack, lines)
    long_moved, short_att = after(long_moved, short_att)
    long_pack = by_position(long_moved, 3)
    long_att, long_w, long_s = long_forward(long_pack[0], long_pack[1], long_pack[2], long_line)
    mixed, proj_own = project_out(exchange(long_att), short_att, out_weight)

    gain_one, bias_one, gain_two, bias_two = (
        line[None, :] for line in (gain_one, bias_one, gain_two, bias_two)
    )
    norm_unit, norm_inverse, normed_low, act_low, act_slope, ffn_own = feed_forward(
        tokens, proj_own, other_half(proj_own), gain_one, bias_one, inner_weight, outer_weight
    )
    output, grad_sum, grad_ffn_low, grad_pre_low, back_own, gain_two_grad, bias_two_grad = (
        feed_back(
            norm_unit, ffn_own, other_half(ffn_own), gain_one, bias_one, gain_two, bias_two,
            cotangent, act_slope, inner_weight, outer_weight,
        )
    )
    grad_hidden, grad_proj_low, long_grad, short_grad, gain_one_grad, bias_one_grad = project_back(
        norm_unit, norm_inverse, grad_sum, back_own, other_half(back_own), gain_one, out_weight,
        heads_dev,
    )

    long_grad = exchange(long_grad)
    outer_grad = contract(act_low, grad_ffn_low, 0, 0)
    inner_grad = contract(normed_low, grad_pre_low, 0, 0)
    out_grad = contract(mixed, grad_proj_low, 1, 0)
    peers = lax.axis_size("seq")
    every_bit = list(range(peers.bit_length() - 1))[::-1]
    orders = [[0, 1] + every_bit[:-2], [1, 0] + every_bit[:-2], [1, 0] + every_bit[:-2]]
    left = [list(every_bit) for _ in orders]
    parts = [
        grad.astype(BF16).reshape([2] * len(every_bit) + [-1, grad.shape[1]])
        for grad in (outer_grad, inner_grad, out_grad)
    ]

    def split(turn):
        return [halves(part, has, order[turn]) for part, has, order in zip(parts, left, orders)]

    def join(pairs, turn):
        for has, order in zip(left, orders):
            has.remove(order[turn])
        return [across_bit(*pair, order[turn]) for pair, order in zip(pairs, orders)]

    def short_half(half, grad):
        return short_backward(
            half, 2, reach, ids_row, ids_col, short_pack, grad, lines_back, short_w, short_s
        )

    pairs, short_grad = after(split(0), short_grad)
    *short_first, first_taps = short_half(0, short_grad)
    long_grad, short_first = after(long_grad, short_first)
    long_grad = by_position(long_grad, 1)[0]
    long_dv, long_taps = long_back_values(long_pack[2], long_grad, long_line_back, long_w)
    parts = join(pairs, 0)
    pairs, long_dv, long_grad = lax.optimization_barrier((split(1), long_dv, long_grad))
    norm_lines = jnp.concatenate(
        [gain_one_grad, bias_one_grad, gain_two_grad, bias_two_grad], axis=0
    ).reshape(-1, PIECE)
    norm_count = norm_lines.shape[0]
    norm_lines = jnp.pad(norm_lines, ((0, 16 - norm_count), (0, 0))).astype(BF16)
    long_dv = exchange(
        jnp.concatenate([long_dv, jnp.broadcast_to(norm_lines[None], (GROUP, 16, PIECE))], axis=1)
    )
    long_dq, long_dk = long_back_pairs(
        long_pack[0], long_pack[1], long_pack[2], long_grad, long_s
    )
    parts = join(pairs, 1)
    pairs, long_dv, long_dq, short_grad = lax.optimization_barrier(
        (split(2), long_dv, long_dq, short_grad)
    )
    *short_last, last_taps = short_half(1, short_grad)
    short_taps = jnp.concatenate([first_taps, last_taps], axis=0)
    long_back = exchange(jnp.concatenate([long_dq, long_dk], axis=1))
    parts = join(pairs, 2)
    for turn in range(3, len(every_bit)):
        parts = join(split(turn), turn)
    norm_sums = jnp.sum(long_dv[:, head_dim : head_dim + norm_count].astype(F32), axis=0)
    norm_sums = norm_sums.reshape(4, width)
    taps = slice(first_tap, first_tap + CONV_WIDTH)
    owner = (jnp.arange(heads_dev) == unit_head) & (place < units)
    kernel_part = short_taps[:, 0, taps] + jnp.where(owner[:, None], long_taps[:, taps], 0.0)
    if len(groups) > 1:
        same_place = [list(pick) for pick in zip(*groups)]
        norm_sums = lax.psum(norm_sums, "seq", axis_index_groups=same_place)
    parts, long_back, short_last = lax.optimization_barrier((parts, long_back, short_last))
    outer_part, inner_part, out_part = parts
    joined = jnp.concatenate(
        [outer_part, inner_part[:, :width], inner_part[:, width:], out_part], axis=0
    )
    joined = lax.all_gather(joined, "seq", axis=0)
    grads_low = unit_back(long_back, long_dv, [short_first, short_last], unit, inverse)
    weight_part = contract(tokens, grads_low, 0, 1).astype(BF16).reshape(peers, -1, 3 * head_cols)
    taps_line = kernel_part.reshape(1, 1, -1).astype(BF16)
    taps_line = jnp.pad(taps_line, ((0, 0), (0, 15), (0, 3 * head_cols - taps_line.shape[2])))
    weight_pieces = lax.all_to_all(
        jnp.concatenate([weight_part, jnp.broadcast_to(taps_line, (peers, 16, 3 * head_cols))], axis=1),
        "seq", 0, 0,
    )
    weight_all = jnp.concatenate([query_weight, key_weight, value_weight], axis=1)
    token_own = contract(grads_low, weight_all, 0, 1).astype(BF16)
    weight_pieces, token_own, joined = lax.optimization_barrier((weight_pieces, token_own, joined))
    joined = joined.astype(F32)
    marks = [outer_part.shape[0]]
    marks += [marks[0] + inner_part.shape[0], marks[0] + 2 * inner_part.shape[0]]
    outer_sum = joined[:, : marks[0]].reshape(outer_weight.shape)
    inner_sum = jnp.concatenate(
        [joined[:, marks[0] : marks[1]], joined[:, marks[1] : marks[2]]], axis=2
    ).reshape(inner_weight.shape)
    out_sum = joined[:, marks[2] :].reshape(out_weight.shape)
    pieces = jnp.sum(weight_pieces.astype(F32), axis=0)
    own_rows = weight_part.shape[1]
    kernel_sum = pieces[own_rows, : heads_dev * CONV_WIDTH].reshape(heads_dev, CONV_WIDTH)
    weight_sum = lax.all_gather(pieces[:own_rows].astype(BF16), "seq", axis=0, tiled=True)
    token_grad = grad_hidden + (token_own.astype(F32) + other_half(token_own).astype(F32))
    return (
        output,
        token_grad,
        weight_sum[:, :head_cols].astype(F32),
        weight_sum[:, head_cols : 2 * head_cols].astype(F32),
        weight_sum[:, 2 * head_cols :].astype(F32),
        kernel_sum,
        out_sum,
        norm_sums[0],
        norm_sums[1],
        inner_sum,
        outer_sum,
        norm_sums[2],
        norm_sums[3],
    )


def solution(mesh):
    rows = P("seq", None)
    columns = P(None, "tp")
    split_rows = P("tp", None)
    return jax.shard_map(
        shards,
        mesh=mesh,
        in_specs=(
            rows, rows, columns, columns, columns, split_rows, split_rows,
            P(), P(), columns, split_rows, P(), P(), rows,
        ),
        out_specs=(
            rows, rows, columns, columns, columns, split_rows, split_rows,
            P(), P(), columns, split_rows, P(), P(),
        ),
        check_vma=False,
    )
```

```python
import math

import jax
import jax.numpy as jnp
from jax import lax
from jax.experimental import pallas as pl
from jax.experimental.pallas import tpu as pltpu
from jax.sharding import PartitionSpec as P

TAU = 8
CONV_WIDTH = 33
HALF_WIDTH = 16
GROUP = 16
PIECE = 256
ITEMS = 2
REACH = 128

COS_SCALE = 0.98
EPS_UNIT = 1e-06
EPS_NORM = 1e-05
NEAR_POLY = (1.158024787902832, -0.36302468180656433, 0.09245320409536362, -0.011449637822806835)
TAIL_POLY = tuple(
    0.5 * a for a in (0.254829592, -0.284496736, 1.421413741, -1.453152027, 1.061405429)
)
SLOPE_SCALE = TAU / math.pi
VMEM_BYTES = 60 * 2**20

F32 = jnp.float32
BF16 = jnp.bfloat16


def norm_terms(values):
    centered = values - jnp.mean(values, axis=-1, keepdims=True)
    inverse = lax.rsqrt(jnp.mean(centered * centered, axis=-1, keepdims=True) + EPS_NORM)
    return centered * inverse, inverse


def norm_back(scaled, unit, inverse):
    along = jnp.mean(scaled * unit, axis=-1, keepdims=True)
    return inverse * (scaled - jnp.mean(scaled, axis=-1, keepdims=True) - unit * along)


def gelu_terms(values):
    share = 1.0 / (1.0 + (0.3275911 * math.sqrt(0.5)) * jnp.abs(values))
    bell = jnp.exp(-0.5 * (values * values))
    poly = TAIL_POLY[4] * share + TAIL_POLY[3]
    for coefficient in TAIL_POLY[2::-1]:
        poly = poly * share + coefficient
    tail = poly * (share * bell)
    below = jnp.where(values < 0.0, tail, 1.0 - tail)
    return values * below, below + values * (bell * (1.0 / math.sqrt(2.0 * math.pi)))


def place_of_item(rows):
    item_at = lax.broadcasted_iota(jnp.int32, (rows, rows), 0)
    place_at = lax.broadcasted_iota(jnp.int32, (rows, rows), 1)
    hit = item_at == (place_at & 1) * PIECE + (place_at >> 1)
    return jnp.where(hit, 1.0, 0.0).astype(BF16)


def lasting(microseconds):
    return pl.CostEstimate(flops=microseconds * 1_150_000_000, bytes_accessed=0, transcendentals=0)


def contract(left, right, left_dim, right_dim):
    return lax.dot_general(
        left, right, (((left_dim,), (right_dim,)), ((), ())), preferred_element_type=F32
    )


def pair_terms(dots, same=None):
    upper = 1.0 / COS_SCALE + dots
    lower = 1.0 / COS_SCALE - dots
    upper_inv = lax.rsqrt(upper)
    lower_inv = lax.rsqrt(lower)
    wide = 1.0 / 0.7 + lower * lower_inv
    wide_inv = lax.rsqrt(wide)
    root = wide * wide_inv
    ratio = NEAR_POLY[3] * root + NEAR_POLY[2]
    ratio = ratio * root + NEAR_POLY[1]
    ratio = ratio * root + NEAR_POLY[0]
    near = ratio * ((upper * upper_inv) * wide_inv)
    if same is not None:
        near = jnp.where(same, near, 0.0)
    near_2 = near * near
    near_4 = near_2 * near_2
    weights = (near_4 * near_4).astype(BF16)
    slopes = ((near_4 * near_2) * (near * (upper_inv * lower_inv))).astype(BF16)
    return weights, slopes


def banded(line):
    return pltpu.roll(
        jnp.broadcast_to(line, (PIECE, line.shape[1])), 0, 1, stride=1, stride_axis=0
    )


def reversed_rows(columns):
    at = lax.broadcasted_iota(jnp.int32, (PIECE, PIECE), 0)
    to = lax.broadcasted_iota(jnp.int32, (PIECE, PIECE), 1)
    flip = jnp.where(at + to == PIECE - 1, 1.0, 0.0).astype(BF16)
    return contract(flip, columns, 1, 1).astype(BF16)


def unbanded(products):
    wide = products.shape[1]
    turned = pltpu.roll(products, wide - (PIECE - 1), 1, stride=1, stride_axis=0)
    return jnp.sum(turned, axis=0, keepdims=True)


def pad_lanes(dst, src, length):
    dst[:, pl.ds(0, REACH)] = jnp.zeros((dst.shape[0], REACH), dst.dtype)
    dst[:, pl.ds(REACH, length)] = src
    dst[:, pl.ds(REACH + length, REACH)] = jnp.zeros((dst.shape[0], REACH), dst.dtype)


def rows_of(dst, src, length):
    for start in range(0, length, PIECE):
        dst[pl.ds(start, PIECE), :] = src[:, pl.ds(start, PIECE)].T


def long_forward(query, key, value, line):
    head_dim, length = query.shape
    blocks = length // PIECE
    step = 512

    def body(q_ref, k_ref, v_ref, line_ref, o_ref, w_ref, s_ref, key_rows, value_pad, band_ref):
        block = pl.program_id(0)

        @pl.when(block == 0)
        def _():
            rows_of(key_rows, k_ref, length)
            pad_lanes(value_pad, v_ref[...], length)
            band_ref[...] = banded(line_ref[...]).astype(BF16)

        q = q_ref[...]
        start = pl.multiple_of(block * PIECE, PIECE)
        total = contract(value_pad[:, pl.ds(start, PIECE + 2 * REACH)], band_ref[...], 1, 1)
        for at in range(0, length, step):
            dots = contract(key_rows[pl.ds(at, step), :], q, 1, 0)
            weights, slopes = pair_terms(dots)
            w_ref[pl.ds(at, step), :] = weights
            s_ref[pl.ds(at, step), :] = slopes
            total = total + contract(v_ref[:, pl.ds(at, step)], weights, 1, 0)
        o_ref[...] = total.astype(BF16)

    whole = pl.BlockSpec((head_dim, length), lambda i: (0, 0))
    large = pl.BlockSpec((None, length, PIECE), lambda i: (i, 0, 0))
    large_shape = jax.ShapeDtypeStruct((blocks, length, PIECE), BF16)
    return pl.pallas_call(
        body,
        grid=(blocks,),
        in_specs=[
            pl.BlockSpec((head_dim, PIECE), lambda i: (0, i)),
            whole,
            whole,
            pl.BlockSpec((1, PIECE + 2 * REACH), lambda i: (0, 0)),
        ],
        out_specs=[pl.BlockSpec((None, head_dim, PIECE), lambda i: (i, 0, 0)), large, large],
        out_shape=[jax.ShapeDtypeStruct((blocks, head_dim, PIECE), BF16), large_shape, large_shape],
        scratch_shapes=[
            pltpu.VMEM((length, head_dim), BF16),
            pltpu.VMEM((head_dim, length + 2 * REACH), BF16),
            pltpu.VMEM((PIECE, PIECE + 2 * REACH), BF16),
        ],
        compiler_params=pltpu.CompilerParams(vmem_limit_bytes=VMEM_BYTES),
        cost_estimate=lasting(70),
    )(query, key, value, line)


def long_back_values(value, grad, line, weights):
    head_dim, length = value.shape
    blocks = length // PIECE
    step = 1024
    wide = PIECE + 2 * REACH

    def body(
        v_ref, g_ref, line_ref, w_ref, dv_ref, taps_ref,
        value_pad, grad_pad, value_sum, band_ref, products,
    ):
        block = pl.program_id(0)

        @pl.when(block == 0)
        def _():
            pad_lanes(value_pad, v_ref[...], length)
            pad_lanes(grad_pad, g_ref[...], length)
            value_sum[...] = jnp.zeros_like(value_sum)
            products[...] = jnp.zeros_like(products)
            band_ref[...] = banded(line_ref[...]).astype(BF16)

        start = pl.multiple_of(block * PIECE, PIECE)
        g = g_ref[:, pl.ds(start, PIECE)]
        near_values = value_pad[:, pl.ds(start, wide)]
        near_grads = grad_pad[:, pl.ds(start, wide)]
        products[...] += contract(reversed_rows(g), near_values, 1, 0)
        value_sum[:, pl.ds(start, PIECE)] += contract(near_grads, band_ref[...], 1, 1)
        for at in range(0, length, step):
            value_sum[:, pl.ds(at, step)] += contract(g, w_ref[pl.ds(at, step), :], 1, 1)

        @pl.when(block == blocks - 1)
        def _():
            for index in range(blocks):
                dv_ref[index] = value_sum[:, pl.ds(index * PIECE, PIECE)].astype(BF16)
            taps_ref[...] = unbanded(products[...])

    whole = pl.BlockSpec((head_dim, length), lambda i: (0, 0))
    return pl.pallas_call(
        body,
        grid=(blocks,),
        in_specs=[
            whole,
            whole,
            pl.BlockSpec((1, wide), lambda i: (0, 0)),
            pl.BlockSpec((None, length, PIECE), lambda i: (i, 0, 0)),
        ],
        out_specs=[
            pl.BlockSpec((blocks, head_dim, PIECE), lambda i: (0, 0, 0)),
            pl.BlockSpec((1, wide), lambda i: (0, 0)),
        ],
        out_shape=[
            jax.ShapeDtypeStruct((blocks, head_dim, PIECE), BF16),
            jax.ShapeDtypeStruct((1, wide), F32),
        ],
        scratch_shapes=[
            pltpu.VMEM((head_dim, length + 2 * REACH), BF16),
            pltpu.VMEM((head_dim, length + 2 * REACH), BF16),
            pltpu.VMEM((head_dim, length), F32),
            pltpu.VMEM((PIECE, wide), BF16),
            pltpu.VMEM((PIECE, wide), F32),
        ],
        compiler_params=pltpu.CompilerParams(vmem_limit_bytes=VMEM_BYTES),
        cost_estimate=lasting(16),
    )(value, grad, line, weights)


def long_back_pairs(query, key, value, grad, slopes):
    head_dim, length = query.shape
    blocks = length // PIECE
    step = 1024

    def body(q_ref, k_ref, v_ref, g_ref, s_ref, dq_ref, dk_ref, value_rows, key_sum):
        block = pl.program_id(0)

        @pl.when(block == 0)
        def _():
            rows_of(value_rows, v_ref, length)
            key_sum[...] = jnp.zeros_like(key_sum)

        q = q_ref[...]
        g = g_ref[...]
        total = jnp.zeros((head_dim, PIECE), F32)
        for at in range(0, length, step):
            grad_weights = contract(value_rows[pl.ds(at, step), :], g, 1, 0)
            terms = grad_weights.astype(BF16) * s_ref[pl.ds(at, step), :]
            total = total + contract(k_ref[:, pl.ds(at, step)], terms, 1, 0)
            key_sum[:, pl.ds(at, step)] += contract(q, terms, 1, 1)
        dq_ref[...] = (total * SLOPE_SCALE).astype(BF16)

        @pl.when(block == blocks - 1)
        def _():
            for index in range(blocks):
                piece = key_sum[:, pl.ds(index * PIECE, PIECE)]
                dk_ref[index] = (piece * SLOPE_SCALE).astype(BF16)

    whole = pl.BlockSpec((head_dim, length), lambda i: (0, 0))
    piece = pl.BlockSpec((head_dim, PIECE), lambda i: (0, i))
    pieces_shape = jax.ShapeDtypeStruct((blocks, head_dim, PIECE), BF16)
    return pl.pallas_call(
        body,
        grid=(blocks,),
        in_specs=[
            piece,
            whole,
            whole,
            piece,
            pl.BlockSpec((None, length, PIECE), lambda i: (i, 0, 0)),
        ],
        out_specs=[
            pl.BlockSpec((None, head_dim, PIECE), lambda i: (i, 0, 0)),
            pl.BlockSpec((blocks, head_dim, PIECE), lambda i: (0, 0, 0)),
        ],
        out_shape=[pieces_shape] * 2,
        scratch_shapes=[
            pltpu.VMEM((length, head_dim), BF16),
            pltpu.VMEM((head_dim, length), F32),
        ],
        compiler_params=pltpu.CompilerParams(vmem_limit_bytes=VMEM_BYTES),
        cost_estimate=lasting(40),
    )(query, key, value, grad, slopes)


def short_forward(reach, ids_row, ids_col, pack, line):
    _, heads, head_dim, length = pack.shape
    blocks = length // PIECE
    wide = PIECE + 2 * REACH

    def body(
        reach_ref, row_ref, col_ref, q_ref, k_ref, v_ref, line_ref,
        o_ref, w_ref, s_ref, key_rows, value_pad, total, band_ref,
    ):
        block = pl.program_id(0)

        @pl.when(block == 0)
        def _():
            for h in range(heads):
                rows_of(key_rows.at[h], k_ref.at[h], length)
                pad_lanes(value_pad.at[h], v_ref[h], length)
                band_ref[h] = banded(line_ref[h])

        start = pl.multiple_of(block * PIECE, PIECE)
        near = (col_ref[pl.ds(start, PIECE), :] == row_ref[:, pl.ds(start, wide)]).astype(F32)
        for h in range(heads):
            masked = (band_ref[h] * near).astype(BF16)
            total[h] = contract(value_pad[h, :, pl.ds(start, wide)], masked, 1, 1)

        own_ids = row_ref[:, pl.ds(start + REACH, PIECE)]

        def turn(step, carry):
            at = pl.multiple_of(step * PIECE, PIECE)
            same = col_ref[pl.ds(at, PIECE), :] == own_ids
            for h in range(heads):
                dots = contract(key_rows[h, pl.ds(at, PIECE), :], q_ref[h], 1, 0)
                weights, slopes = pair_terms(dots, same)
                w_ref[h, pl.ds(at, PIECE), :] = weights
                s_ref[h, pl.ds(at, PIECE), :] = slopes
                total[h] += contract(v_ref[h, :, pl.ds(at, PIECE)], weights, 1, 0)
            return carry

        lax.fori_loop(reach_ref[0, block], reach_ref[1, block], turn, 0)
        o_ref[...] = total[...].astype(BF16)

    def packed(which):
        return pl.BlockSpec((None, heads, head_dim, length), lambda i: (which, 0, 0, 0))

    block_spec = pl.BlockSpec((heads, head_dim, PIECE), lambda i: (0, 0, i))
    large = pl.BlockSpec((None, heads, length, PIECE), lambda i: (i, 0, 0, 0))
    large_shape = jax.ShapeDtypeStruct((blocks, heads, length, PIECE), BF16)
    return pl.pallas_call(
        body,
        grid=(blocks,),
        in_specs=[
            pl.BlockSpec(memory_space=pltpu.SMEM),
            pl.BlockSpec((1, length + 2 * REACH), lambda i: (0, 0)),
            pl.BlockSpec((length, 1), lambda i: (0, 0)),
            pl.BlockSpec((None, heads, head_dim, PIECE), lambda i: (0, 0, 0, i)),
            packed(1),
            packed(2),
            pl.BlockSpec((heads, 1, wide), lambda i: (0, 0, 0)),
        ],
        out_specs=[block_spec, large, large],
        out_shape=[jax.ShapeDtypeStruct((heads, head_dim, length), BF16), large_shape, large_shape],
        scratch_shapes=[
            pltpu.VMEM((heads, length, head_dim), BF16),
            pltpu.VMEM((heads, head_dim, length + 2 * REACH), BF16),
            pltpu.VMEM((heads, head_dim, PIECE), F32),
            pltpu.VMEM((heads, PIECE, wide), F32),
        ],
        compiler_params=pltpu.CompilerParams(vmem_limit_bytes=VMEM_BYTES),
        cost_estimate=lasting(28),
    )(reach, ids_row, ids_col, pack, pack, pack, line)


def short_backward(
    part, parts, reach, ids_row, ids_col, pack, grad, line, weights, slopes
):
    _, all_heads, head_dim, length = pack.shape
    heads = all_heads // parts
    blocks = length // PIECE
    wide = PIECE + 2 * REACH

    def body(
        reach_ref, row_ref, col_ref, q_ref, k_ref, v_ref, g_ref, line_ref, w_ref, s_ref,
        dq_ref, dk_ref, dv_ref, taps_ref, value_rows, value_pad, grad_pad, band_ref, products,
    ):
        block = pl.program_id(0)

        @pl.when(block == 0)
        def _():
            for h in range(heads):
                rows_of(value_rows.at[h], v_ref.at[h], length)
                pad_lanes(value_pad.at[h], v_ref[h], length)
                pad_lanes(grad_pad.at[h], g_ref[h], length)
                band_ref[h] = banded(line_ref[h])
            dk_ref[...] = jnp.zeros_like(dk_ref)
            dv_ref[...] = jnp.zeros_like(dv_ref)
            products[...] = jnp.zeros_like(products)

        start = pl.multiple_of(block * PIECE, PIECE)
        near = (col_ref[pl.ds(start, PIECE), :] == row_ref[:, pl.ds(start, wide)]).astype(F32)
        at = lax.broadcasted_iota(jnp.int32, (PIECE, PIECE), 0)
        to = lax.broadcasted_iota(jnp.int32, (PIECE, PIECE), 1)
        flip = jnp.where(at + to == PIECE - 1, 1.0, 0.0).astype(BF16)
        near_flip = contract(flip, near.astype(BF16), 1, 0)
        for h in range(heads):
            masked = (band_ref[h] * near).astype(BF16)
            own = g_ref[h, :, pl.ds(start, PIECE)]
            products[h] += (
                contract(reversed_rows(own), value_pad[h, :, pl.ds(start, wide)], 1, 0) * near_flip
            )
            dv_ref[h, :, pl.ds(start, PIECE)] += contract(
                grad_pad[h, :, pl.ds(start, wide)], masked, 1, 1
            )
        dq_ref[...] = jnp.zeros_like(dq_ref)

        def turn(step, carry):
            at = pl.multiple_of(step * PIECE, PIECE)
            for h in range(heads):
                own = g_ref[h, :, pl.ds(start, PIECE)]
                grad_weights = contract(value_rows[h, pl.ds(at, PIECE), :], own, 1, 0)
                terms = grad_weights.astype(BF16) * s_ref[h, pl.ds(at, PIECE), :]
                dq_ref[h] += contract(k_ref[h, :, pl.ds(at, PIECE)], terms, 1, 0) * SLOPE_SCALE
                dk_ref[h, :, pl.ds(at, PIECE)] += contract(q_ref[h], terms, 1, 1) * SLOPE_SCALE
                dv_ref[h, :, pl.ds(at, PIECE)] += contract(own, w_ref[h, pl.ds(at, PIECE), :], 1, 1)
            return carry

        lax.fori_loop(reach_ref[0, block], reach_ref[1, block], turn, 0)

        @pl.when(block == blocks - 1)
        def _():
            for h in range(heads):
                taps_ref[h] = unbanded(products[h])

    def packed(which):
        return pl.BlockSpec((None, heads, head_dim, length), lambda i: (which, part, 0, 0))

    whole = pl.BlockSpec((heads, head_dim, length), lambda i: (0, 0, 0))
    large = pl.BlockSpec((None, heads, length, PIECE), lambda i: (i, part, 0, 0))
    whole_shape = jax.ShapeDtypeStruct((heads, head_dim, length), F32)
    return pl.pallas_call(
        body,
        grid=(blocks,),
        in_specs=[
            pl.BlockSpec(memory_space=pltpu.SMEM),
            pl.BlockSpec((1, length + 2 * REACH), lambda i: (0, 0)),
            pl.BlockSpec((length, 1), lambda i: (0, 0)),
            pl.BlockSpec((None, heads, head_dim, PIECE), lambda i: (0, part, 0, i)),
            packed(1),
            packed(2),
            pl.BlockSpec((heads, head_dim, length), lambda i: (part, 0, 0)),
            pl.BlockSpec((heads, 1, wide), lambda i: (part, 0, 0)),
            large,
            large,
        ],
        out_specs=[
            pl.BlockSpec((heads, head_dim, PIECE), lambda i: (0, 0, i)),
            whole,
            whole,
            pl.BlockSpec((heads, 1, wide), lambda i: (0, 0, 0)),
        ],
        out_shape=[whole_shape] * 3 + [jax.ShapeDtypeStruct((heads, 1, wide), F32)],
        scratch_shapes=[
            pltpu.VMEM((heads, length, head_dim), BF16),
            pltpu.VMEM((heads, head_dim, length + 2 * REACH), BF16),
            pltpu.VMEM((heads, head_dim, length + 2 * REACH), BF16),
            pltpu.VMEM((heads, PIECE, wide), F32),
            pltpu.VMEM((heads, PIECE, wide), F32),
        ],
        compiler_params=pltpu.CompilerParams(vmem_limit_bytes=VMEM_BYTES),
        cost_estimate=lasting(28),
    )(reach, ids_row, ids_col, pack, pack, pack, grad, line, weights, slopes)


def project_in(tokens, query_weight, key_weight, value_weight, heads):
    row_total, width = tokens.shape
    cols = query_weight.shape[1]
    head_dim = cols // heads
    blocks = row_total // PIECE
    long_rows = ITEMS * PIECE

    def body(t_ref, wq_ref, wk_ref, wv_ref, long_ref, short_ref, unit_ref, inv_ref, turned, rows):
        block = pl.program_id(0)

        @pl.when(block == 0)
        def _():
            for index, ref in enumerate((wq_ref, wk_ref, wv_ref)):
                turned[pl.ds(index * cols, cols), :] = ref[...].T
            long_ref[pl.ds(ITEMS * heads, GROUP - ITEMS * heads)] = jnp.zeros(
                (GROUP - ITEMS * heads, 3 * head_dim, PIECE), BF16
            )

        @pl.when(block < ITEMS)
        def _():
            item_at = lax.broadcasted_iota(jnp.int32, (PIECE, long_rows), 0)
            place_at = lax.broadcasted_iota(jnp.int32, (PIECE, long_rows), 1)
            pick = jnp.where(place_at == ITEMS * item_at + block, 1.0, 0.0).astype(BF16)
            rows[...] = contract(pick, t_ref[pl.ds(0, long_rows), :], 1, 0).astype(BF16)

        @pl.when(block >= ITEMS)
        def _():
            rows[...] = t_ref[pl.ds(pl.multiple_of(block * PIECE, PIECE), PIECE), :]

        parts = contract(turned[...], rows[...], 1, 1).reshape(3, heads, head_dim, PIECE)
        raw = parts[:2]
        inverse = lax.rsqrt(jnp.sum(raw * raw, axis=2, keepdims=True) + EPS_UNIT)
        unit = raw * inverse
        unit_ref[...] = unit
        inv_ref[...] = inverse
        low = unit.astype(BF16)
        short_ref[:2] = low
        short_ref[2] = parts[2].astype(BF16)

        @pl.when(block < ITEMS)
        def _():
            for h in range(heads):
                unit_at = block * heads + h
                long_ref[unit_at, pl.ds(0, head_dim), :] = low[0, h]
                long_ref[unit_at, pl.ds(head_dim, head_dim), :] = low[1, h]
                long_ref[unit_at, pl.ds(2 * head_dim, head_dim), :] = parts[2, h].astype(BF16)

    weight = pl.BlockSpec((width, cols), lambda i: (0, 0))
    return pl.pallas_call(
        body,
        grid=(blocks,),
        in_specs=[pl.BlockSpec((row_total, width), lambda i: (0, 0)), weight, weight, weight],
        out_specs=[
            pl.BlockSpec((GROUP, 3 * head_dim, PIECE), lambda i: (0, 0, 0)),
            pl.BlockSpec(
                (3, heads, head_dim, PIECE), lambda i: (0, 0, 0, jnp.maximum(i - ITEMS, 0))
            ),
            pl.BlockSpec((2, heads, head_dim, PIECE), lambda i: (0, 0, 0, i)),
            pl.BlockSpec((2, heads, 1, PIECE), lambda i: (0, 0, 0, i)),
        ],
        out_shape=[
            jax.ShapeDtypeStruct((GROUP, 3 * head_dim, PIECE), BF16),
            jax.ShapeDtypeStruct((3, heads, head_dim, row_total - long_rows), BF16),
            jax.ShapeDtypeStruct((2, heads, head_dim, row_total), F32),
            jax.ShapeDtypeStruct((2, heads, 1, row_total), F32),
        ],
        scratch_shapes=[pltpu.VMEM((3 * cols, width), BF16), pltpu.VMEM((PIECE, width), BF16)],
        compiler_params=pltpu.CompilerParams(vmem_limit_bytes=VMEM_BYTES),
        cost_estimate=lasting(10),
    )(tokens, query_weight, key_weight, value_weight)


def row_blocks(first, count, cols, span=PIECE):
    return pl.BlockSpec((span, cols), lambda i: (i + first, 0))


ANYWHERE = pl.BlockSpec(memory_space=pl.ANY)


def project_out_short(short_att, out_weight, row_total):
    heads, head_dim, short_rows = short_att.shape
    cols, width = out_weight.shape
    span = ITEMS * PIECE

    def body(a_ref, w_ref, mixed_ref, part_ref):
        mixed = a_ref[...].reshape(cols, span)
        mixed_ref[...] = mixed
        part_ref[...] = contract(mixed, w_ref[...], 0, 0).astype(BF16)

    return pl.pallas_call(
        body,
        grid=(short_rows // span,),
        in_specs=[
            pl.BlockSpec((heads, head_dim, span), lambda i: (0, 0, i)),
            pl.BlockSpec((cols, width), lambda i: (0, 0)),
        ],
        out_specs=[
            pl.BlockSpec((cols, span), lambda i: (0, i + 1)),
            pl.BlockSpec((span, width), lambda i: (i, 0)),
        ],
        out_shape=[
            jax.ShapeDtypeStruct((cols, row_total), BF16),
            jax.ShapeDtypeStruct((short_rows, width), BF16),
        ],
        compiler_params=pltpu.CompilerParams(vmem_limit_bytes=VMEM_BYTES),
        cost_estimate=lasting(4),
    )(short_att, out_weight)


def project_out_long(moved_low, moved_high, out_weight, mixed):
    cols, width = out_weight.shape
    half = moved_low.shape[1]
    head_dim = 2 * half
    heads = cols // head_dim
    span = ITEMS * PIECE

    def body(low_ref, high_ref, w_ref, old_ref, mixed_ref, part_ref, items):
        for h in range(heads):
            for item in range(ITEMS):
                for at, ref in ((0, low_ref), (half, high_ref)):
                    items[pl.ds(h * head_dim + at, half), pl.ds(item * PIECE, PIECE)] = ref[
                        item * heads + h
                    ]
        placed = contract(items[...], place_of_item(span), 1, 0).astype(BF16)
        mixed_ref[...] = placed
        part_ref[...] = contract(placed, w_ref[...], 0, 0).astype(BF16)

    return pl.pallas_call(
        body,
        grid=(1,),
        in_specs=[
            pl.BlockSpec((GROUP, half, PIECE), lambda i: (0, 0, 0)),
            pl.BlockSpec((GROUP, half, PIECE), lambda i: (0, 0, 0)),
            pl.BlockSpec((cols, width), lambda i: (0, 0)),
            ANYWHERE,
        ],
        out_specs=[
            pl.BlockSpec((cols, span), lambda i: (0, 0)),
            pl.BlockSpec((span, width), lambda i: (0, 0)),
        ],
        out_shape=[
            jax.ShapeDtypeStruct(mixed.shape, BF16),
            jax.ShapeDtypeStruct((span, width), BF16),
        ],
        scratch_shapes=[pltpu.VMEM((cols, span), BF16)],
        input_output_aliases={3: 0},
        compiler_params=pltpu.CompilerParams(vmem_limit_bytes=VMEM_BYTES),
        cost_estimate=lasting(3),
    )(moved_low, moved_high, out_weight, mixed)


def feed_forward(first, tokens, own, other, gain, bias, inner_weight, outer_weight, into=()):
    row_total, width = tokens.shape
    count = own.shape[0] // PIECE
    hidden_units = inner_weight.shape[1]

    def body(t_ref, own_ref, other_ref, gain_ref, bias_ref, inner_ref, outer_ref, *rest):
        unit_ref, inv_ref, low_ref, act_ref, slope_ref, part_ref = rest[len(into) :]
        hidden = t_ref[...].astype(F32) + (
            own_ref[...].astype(F32) + other_ref[...].astype(F32)
        )
        unit, inverse = norm_terms(hidden)
        unit_ref[...] = unit
        inv_ref[...] = inverse
        low = (unit * gain_ref[...] + bias_ref[...]).astype(BF16)
        low_ref[...] = low
        act, slope = gelu_terms(contract(low, inner_ref[...], 1, 0))
        act = act.astype(BF16)
        act_ref[...] = act
        slope_ref[...] = slope.astype(BF16)
        part_ref[...] = contract(act, outer_ref[...], 1, 0).astype(BF16)

    own_rows = row_blocks(0, count, width)
    rows = row_blocks(first, count, width)
    units = row_blocks(first, count, hidden_units)
    line = pl.BlockSpec((1, width), lambda i: (0, 0))
    return pl.pallas_call(
        body,
        grid=(count,),
        in_specs=[
            rows, own_rows, own_rows, line, line,
            pl.BlockSpec((width, hidden_units), lambda i: (0, 0)),
            pl.BlockSpec((hidden_units, width), lambda i: (0, 0)),
        ]
        + [ANYWHERE] * len(into),
        out_specs=[rows, row_blocks(first, count, 1), rows, units, units, own_rows],
        out_shape=[
            jax.ShapeDtypeStruct((row_total, width), F32),
            jax.ShapeDtypeStruct((row_total, 1), F32),
            jax.ShapeDtypeStruct((row_total, width), BF16),
            jax.ShapeDtypeStruct((row_total, hidden_units), BF16),
            jax.ShapeDtypeStruct((row_total, hidden_units), BF16),
            jax.ShapeDtypeStruct((count * PIECE, width), BF16),
        ],
        input_output_aliases={7 + at: at for at in range(len(into))},
        compiler_params=pltpu.CompilerParams(vmem_limit_bytes=VMEM_BYTES),
        cost_estimate=lasting(3 * count),
    )(tokens, own, other, gain, bias, inner_weight, outer_weight, *into)


def feed_back(
    first, unit_one, own, other, gain_one, bias_one, gain_two, bias_two, cotangent, slope,
    inner_weight, outer_weight, into=(),
):
    row_total, width = unit_one.shape
    count = own.shape[0] // PIECE
    hidden_units = inner_weight.shape[1]

    def body(
        unit_ref, own_ref, other_ref, gain_one_ref, bias_one_ref, gain_ref, bias_ref, g_ref,
        slope_ref, inner_ref, outer_ref, *rest,
    ):
        out_ref, sum_ref, low_ref, pre_ref, part_ref, gain_grad_ref, bias_grad_ref = rest[
            len(into) :
        ]

        @pl.when(pl.program_id(0) == 0)
        def _():
            gain_grad_ref[...] = jnp.zeros_like(gain_grad_ref)
            bias_grad_ref[...] = jnp.zeros_like(bias_grad_ref)

        normed = unit_ref[...] * gain_one_ref[...] + bias_one_ref[...]
        unit, inverse = norm_terms(
            normed + (own_ref[...].astype(F32) + other_ref[...].astype(F32))
        )
        out_ref[...] = (unit * gain_ref[...] + bias_ref[...]).astype(BF16)
        g = g_ref[...].astype(F32)
        gain_grad_ref[...] += jnp.sum(g * unit, axis=0, keepdims=True)
        bias_grad_ref[...] += jnp.sum(g, axis=0, keepdims=True)
        grad_sum = norm_back(g * gain_ref[...], unit, inverse)
        sum_ref[...] = grad_sum
        low = grad_sum.astype(BF16)
        low_ref[...] = low
        pre = contract(low, outer_ref[...], 1, 1) * slope_ref[...].astype(F32)
        pre = pre.astype(BF16)
        pre_ref[...] = pre
        part_ref[...] = contract(pre, inner_ref[...], 1, 1).astype(BF16)

    own_rows = row_blocks(0, count, width)
    rows = row_blocks(first, count, width)
    units = row_blocks(first, count, hidden_units)
    line = pl.BlockSpec((1, width), lambda i: (0, 0))
    return pl.pallas_call(
        body,
        grid=(count,),
        in_specs=[
            rows, own_rows, own_rows, line, line, line, line, rows, units,
            pl.BlockSpec((width, hidden_units), lambda i: (0, 0)),
            pl.BlockSpec((hidden_units, width), lambda i: (0, 0)),
        ]
        + [ANYWHERE] * len(into),
        out_specs=[rows, rows, rows, units, own_rows, line, line],
        out_shape=[
            jax.ShapeDtypeStruct((row_total, width), BF16),
            jax.ShapeDtypeStruct((row_total, width), F32),
            jax.ShapeDtypeStruct((row_total, width), BF16),
            jax.ShapeDtypeStruct((row_total, hidden_units), BF16),
            jax.ShapeDtypeStruct((count * PIECE, width), BF16),
            jax.ShapeDtypeStruct((1, width), F32),
            jax.ShapeDtypeStruct((1, width), F32),
        ],
        input_output_aliases={11 + at: at for at in range(len(into))},
        compiler_params=pltpu.CompilerParams(vmem_limit_bytes=VMEM_BYTES),
        cost_estimate=lasting(3 * count),
    )(
        unit_one, own, other, gain_one, bias_one, gain_two, bias_two, cotangent, slope,
        inner_weight, outer_weight, *into,
    )


def project_back(first, unit, inverse, grad_sum, own, other, gain, out_weight, heads, into=()):
    row_total, width = unit.shape
    cols = out_weight.shape[0]
    head_dim = cols // heads
    span = ITEMS * PIECE
    count = own.shape[0] // span
    is_long = first == 0

    def body(unit_ref, inv_ref, sum_ref, own_ref, other_ref, gain_ref, w_ref, *rest):
        hidden_ref, low_ref, att_ref, gain_grad_ref, bias_grad_ref = rest[len(into) :]

        @pl.when(pl.program_id(0) == 0)
        def _():
            gain_grad_ref[...] = jnp.zeros_like(gain_grad_ref)
            bias_grad_ref[...] = jnp.zeros_like(bias_grad_ref)

        unit = unit_ref[...]
        grad = sum_ref[...] + (own_ref[...].astype(F32) + other_ref[...].astype(F32))
        gain_grad_ref[...] += jnp.sum(grad * unit, axis=0, keepdims=True)
        bias_grad_ref[...] += jnp.sum(grad, axis=0, keepdims=True)
        hidden = norm_back(grad * gain_ref[...], unit, inv_ref[...])
        hidden_ref[...] = hidden
        low = hidden.astype(BF16)
        low_ref[...] = low
        att = contract(w_ref[...], low, 1, 1).astype(BF16)
        if is_long:
            items = contract(att, place_of_item(span), 1, 1).astype(BF16)
            for h in range(heads):
                for item in range(ITEMS):
                    att_ref[item * heads + h] = items[
                        h * head_dim : (h + 1) * head_dim, item * PIECE : (item + 1) * PIECE
                    ]
            att_ref[pl.ds(ITEMS * heads, GROUP - ITEMS * heads)] = jnp.zeros(
                (GROUP - ITEMS * heads, head_dim, PIECE), BF16
            )
        else:
            att_ref[...] = att.reshape(heads, head_dim, span)

    own_rows = row_blocks(0, count, width, span)
    rows = row_blocks(first, count, width, span)
    line = pl.BlockSpec((1, width), lambda i: (0, 0))
    if is_long:
        att_spec = pl.BlockSpec((GROUP, head_dim, PIECE), lambda i: (0, 0, 0))
        att_shape = (GROUP, head_dim, PIECE)
    else:
        att_spec = pl.BlockSpec((heads, head_dim, span), lambda i: (0, 0, i))
        att_shape = (heads, head_dim, count * span)
    return pl.pallas_call(
        body,
        grid=(count,),
        in_specs=[
            rows, row_blocks(first, count, 1, span), rows, own_rows, own_rows, line,
            pl.BlockSpec((cols, width), lambda i: (0, 0)),
        ]
        + [ANYWHERE] * len(into),
        out_specs=[rows, rows, att_spec, line, line],
        out_shape=[
            jax.ShapeDtypeStruct((row_total, width), F32),
            jax.ShapeDtypeStruct((row_total, width), BF16),
            jax.ShapeDtypeStruct(att_shape, BF16),
            jax.ShapeDtypeStruct((1, width), F32),
            jax.ShapeDtypeStruct((1, width), F32),
        ],
        input_output_aliases={7 + at: at for at in range(len(into))},
        compiler_params=pltpu.CompilerParams(vmem_limit_bytes=VMEM_BYTES),
        cost_estimate=lasting(4 * count),
    )(unit, inverse, grad_sum, own, other, gain, out_weight, *into)


NORM_SLOT = 8


def gradient_terms(mine, act, grad_ffn, normed, grad_pre, mixed, grad_proj, norm_lines):
    row_total, width = grad_ffn.shape
    units, cols = act.shape[1], mixed.shape[0]
    span = ITEMS * PIECE
    counts = [units // 16, width // 16, width // 16, cols // 16, NORM_SLOT]
    steps = row_total // span

    def body(
        mine_ref, act_ref, ffn_ref, low_ref, pre_ref, mixed_ref, proj_ref, norm_ref, *rest
    ):
        outs, (outer, inner, out) = rest[:4], rest[4:]
        step = pl.program_id(0)

        @pl.when(step == 0)
        def _():
            outer[...] = jnp.zeros_like(outer)
            inner[...] = jnp.zeros_like(inner)
            out[...] = jnp.zeros_like(out)

        outer[...] += contract(act_ref[...], ffn_ref[...], 0, 0)
        inner[...] += contract(low_ref[...], pre_ref[...], 0, 0)
        out[...] += contract(mixed_ref[...], proj_ref[...], 1, 0)

        @pl.when(step == steps - 1)
        def _():
            slot = lax.broadcasted_iota(jnp.int32, (NORM_SLOT, width), 0) == 0
            for away, ref in enumerate(outs):
                first = lax.bitwise_xor(mine_ref[0], away)

                def rows(source, count, second):
                    at = pl.multiple_of((first * 4 + second) * count, count)
                    return source[pl.ds(at, count), :]

                for second in range(4):
                    at = 0
                    ref[second, pl.ds(at, counts[0]), :] = rows(outer, counts[0], second).astype(BF16)
                    at += counts[0]
                    both = rows(inner, counts[1], second).astype(BF16)
                    ref[second, pl.ds(at, counts[1]), :] = both[:, :width]
                    at += counts[1]
                    ref[second, pl.ds(at, counts[2]), :] = both[:, width:]
                    at += counts[2]
                    line = norm_ref[pl.ds(first, 1), :] if second == 0 else jnp.zeros((1, width), F32)
                    tail = jnp.concatenate(
                        [rows(out, counts[3], second), jnp.where(slot, line, 0.0)], axis=0
                    )
                    ref[second, pl.ds(at, counts[3] + NORM_SLOT), :] = tail.astype(BF16)

    def rows(array):
        return pl.BlockSpec((span, array.shape[1]), lambda i: (i, 0))

    shape = (4, sum(counts), width)
    return counts, pl.pallas_call(
        body,
        grid=(steps,),
        in_specs=[
            pl.BlockSpec(memory_space=pltpu.SMEM),
            rows(act),
            rows(grad_ffn),
            rows(normed),
            rows(grad_pre),
            pl.BlockSpec((cols, span), lambda i: (0, i)),
            rows(grad_proj),
            pl.BlockSpec((4, width), lambda i: (0, 0)),
        ],
        out_specs=[pl.BlockSpec(shape, lambda i: (0, 0, 0))] * 4,
        out_shape=[jax.ShapeDtypeStruct(shape, BF16)] * 4,
        scratch_shapes=[
            pltpu.VMEM((units, width), F32),
            pltpu.VMEM((width, units), F32),
            pltpu.VMEM((cols, width), F32),
        ],
        compiler_params=pltpu.CompilerParams(vmem_limit_bytes=VMEM_BYTES),
        cost_estimate=lasting(15),
    )(mine, act, grad_ffn, normed, grad_pre, mixed, grad_proj, norm_lines)


def gathered_sums(gathered, counts, peers):
    width = gathered.shape[2]
    groups = bit_groups(peers)

    def body(in_ref, outer_ref, inner_ref, out_ref, norm_ref):
        for at_place in range(peers):
            order = 0
            for bits in groups:
                size = 1 << len(bits)
                order = order * size + ((at_place >> bits[0]) & (size - 1))
            at = 0
            for index, count in enumerate(counts):
                rows = in_ref[at_place, pl.ds(at, count), :].astype(F32)
                to = pl.ds(order * count, count)
                if index == 0:
                    outer_ref[to, :] = rows
                elif index < 3:
                    inner_ref[to, pl.ds((index - 1) * width, width)] = rows
                elif index == 3:
                    out_ref[to, :] = rows
                elif order % (peers // 4) == 0:
                    norm_ref[pl.ds(order // (peers // 4), 1), :] = rows[:1]
                at += count

    def whole(shape):
        return pl.BlockSpec(shape, lambda: (0,) * len(shape))

    shapes = [
        (peers * counts[0], width),
        (peers * counts[1], 2 * width),
        (peers * counts[3], width),
        (4, width),
    ]
    return pl.pallas_call(
        body,
        in_specs=[whole(gathered.shape)],
        out_specs=[whole(shape) for shape in shapes],
        out_shape=[jax.ShapeDtypeStruct(shape, F32) for shape in shapes],
        compiler_params=pltpu.CompilerParams(vmem_limit_bytes=VMEM_BYTES),
        cost_estimate=lasting(6),
    )(gathered)


def unit_back(moved_pairs, moved_values, short_parts, unit, inverse):
    heads, head_dim = unit.shape[1:3]
    short_heads, _, short_rows = short_parts[0][0].shape
    count = len(short_parts)
    span = ITEMS * PIECE
    blocks = 1 + short_rows // span
    cols = heads * head_dim

    def body(*refs):
        pairs_ref, values_ref = refs[:2]
        short_refs = refs[2 : 2 + 3 * count]
        unit_ref, inv_ref, out_ref, items = refs[2 + 3 * count :]
        block = pl.program_id(0)

        def short_part(which):
            return jnp.concatenate([short_refs[3 * at + which][...] for at in range(count)], axis=0)

        def back(which, grad):
            unit = unit_ref[which]
            along = jnp.sum(unit * grad, axis=1, keepdims=True)
            return ((grad - unit * along) * inv_ref[which]).astype(BF16).reshape(cols, span)

        @pl.when(block == 0)
        def _():
            def long_part(ref, at):
                part = pl.ds(at, head_dim)
                heads_of = [
                    jnp.concatenate([ref[h, part, :], ref[heads + h, part, :]], axis=1)
                    for h in range(heads)
                ]
                return jnp.stack(heads_of, axis=0)

            for which in range(2):
                items[pl.ds(which * cols, cols), :] = back(
                    which, long_part(pairs_ref, which * head_dim).astype(F32)
                )
            items[pl.ds(2 * cols, cols), :] = long_part(values_ref, 0).reshape(cols, span)
            out_ref[...] = contract(items[...], place_of_item(span), 1, 0).astype(BF16)

        @pl.when(block > 0)
        def _():
            out_ref[pl.ds(0, cols), :] = back(0, short_part(0))
            out_ref[pl.ds(cols, cols), :] = back(1, short_part(1))
            out_ref[pl.ds(2 * cols, cols), :] = short_part(2).astype(BF16).reshape(
                cols, span
            )

    short = pl.BlockSpec(
        (short_heads, head_dim, span), lambda i: (0, 0, jnp.maximum(i - 1, 0))
    )
    return pl.pallas_call(
        body,
        grid=(blocks,),
        in_specs=[
            pl.BlockSpec((GROUP, moved_pairs.shape[1], PIECE), lambda i: (0, 0, 0)),
            pl.BlockSpec((GROUP, head_dim, PIECE), lambda i: (0, 0, 0)),
        ]
        + [short] * (3 * count)
        + [
            pl.BlockSpec((2, heads, head_dim, span), lambda i: (0, 0, 0, i)),
            pl.BlockSpec((2, heads, 1, span), lambda i: (0, 0, 0, i)),
        ],
        out_specs=pl.BlockSpec((3 * cols, span), lambda i: (0, i)),
        out_shape=jax.ShapeDtypeStruct((3 * cols, span * blocks), BF16),
        scratch_shapes=[pltpu.VMEM((3 * cols, span), BF16)],
        compiler_params=pltpu.CompilerParams(vmem_limit_bytes=VMEM_BYTES),
        cost_estimate=lasting(8),
    )(moved_pairs, moved_values, *sum(map(tuple, short_parts), ()), unit, inverse)


def other_half(part):
    return lax.ppermute(part, "tp", [(0, 1), (1, 0)])


def bit_groups(peers):
    bits = peers.bit_length() - 1
    return [list(range(low, min(low + 2, bits))) for low in range(0, bits, 2)]


def terms_for(part, bits):
    mine = (lax.axis_index("seq") >> bits[0]) & ((1 << len(bits)) - 1)
    return [
        lax.dynamic_index_in_dim(part, mine ^ away, 0, False) for away in range(1 << len(bits))
    ]


def in_order(gathered, peers):
    sizes = [1 << len(bits) for bits in reversed(bit_groups(peers))]
    count = len(sizes)
    array = gathered.reshape(sizes + list(gathered.shape[1:]))
    array = jnp.transpose(array, list(range(count))[::-1] + [count, count + 1])
    return array.reshape(-1, gathered.shape[-1])


def terms_sent(terms, bits, first=1):
    peers = lax.axis_size("seq")
    terms = terms if first > 1 else terms[1:]
    return [
        lax.ppermute(term, "seq", [(i, i ^ (away << bits[0])) for i in range(peers)])
        for away, term in enumerate(terms, first)
    ]


def terms_gathered(own, bits):
    mine = (lax.axis_index("seq") >> bits[0]) & ((1 << len(bits)) - 1)
    every = jnp.stack([own] + terms_sent([own] * (1 << len(bits)), bits), axis=0)
    return jnp.stack(
        [
            lax.dynamic_index_in_dim(every, mine ^ place, 0, False)
            for place in range(1 << len(bits))
        ],
        axis=0,
    )


def terms_summed(own, came):
    total = own.astype(F32)
    for term in came:
        total = total + term.astype(F32)
    return total.astype(BF16)


def after(first, second):
    return lax.optimization_barrier((first, second))


def shards(
    tokens,
    short_lengths,
    query_weight,
    key_weight,
    value_weight,
    conv_kernel,
    out_weight,
    gain_one,
    bias_one,
    inner_weight,
    outer_weight,
    gain_two,
    bias_two,
    cotangent,
):
    row_total, width = tokens.shape
    heads_dev = conv_kernel.shape[0]
    head_cols = query_weight.shape[1]
    head_dim = head_cols // heads_dev
    short_rows = row_total - ITEMS * PIECE
    units = ITEMS * heads_dev
    place = lax.axis_index("seq") % GROUP
    groups = [
        [first + i for i in range(GROUP)] for first in range(0, lax.axis_size("seq"), GROUP)
    ]

    def exchange(pieces):
        return lax.all_to_all(pieces, "seq", 0, 0, axis_index_groups=groups)

    def by_position(moved, count):
        return jnp.transpose(moved, (1, 0, 2)).reshape(count, head_dim, GROUP * PIECE)

    item_ends = jnp.cumsum(short_lengths[0])
    positions = jnp.arange(short_rows, dtype=jnp.int32)
    item_ids = jnp.sum((positions[:, None] >= item_ends[None, :]).astype(jnp.int32), axis=1)
    ids_row = jnp.pad(item_ids, (REACH, REACH), constant_values=-1)[None, :]
    ids_col = item_ids[:, None]
    item_starts = jnp.concatenate([jnp.zeros((1,), jnp.int32), item_ends[:-1]])
    block_first = jnp.arange(0, short_rows, PIECE, dtype=jnp.int32)
    block_last = block_first + (PIECE - 1)
    inside = (item_starts[None, :] <= block_last[:, None]) & (
        item_ends[None, :] > block_first[:, None]
    )
    lowest = jnp.min(jnp.where(inside, item_starts[None, :], short_rows), axis=1)
    highest = jnp.max(jnp.where(inside, item_ends[None, :], 0), axis=1)
    reach = jnp.stack([lowest // PIECE, (highest + PIECE - 1) // PIECE]).astype(jnp.int32)

    first_tap = REACH - HALF_WIDTH
    tap_pad = ((0, 0), (first_tap, PIECE + 2 * REACH - first_tap - CONV_WIDTH))
    lines = jnp.pad(conv_kernel, tap_pad)[:, None, :]
    lines_back = jnp.pad(conv_kernel[:, ::-1], tap_pad)[:, None, :]
    unit_head = place % heads_dev
    long_line = lax.dynamic_index_in_dim(lines, unit_head, 0, False)
    long_line_back = lax.dynamic_index_in_dim(lines_back, unit_head, 0, False)

    long_send, short_pack, unit, inverse = project_in(
        tokens, query_weight, key_weight, value_weight, heads_dev
    )
    lines_of = [line[None, :] for line in (gain_one, bias_one, gain_two, bias_two)]
    gain_one, bias_one, gain_two, bias_two = lines_of

    long_moved = exchange(long_send)
    short_att, short_w, short_s = short_forward(reach, ids_row, ids_col, short_pack, lines)
    mixed, short_proj = project_out_short(short_att, out_weight, row_total)
    long_moved, short_proj = after(long_moved, short_proj)
    long_pack = by_position(long_moved, 3)
    long_att, long_w, long_s = long_forward(long_pack[0], long_pack[1], long_pack[2], long_line)

    long_att, short_proj = after(long_att, short_proj)
    long_halves = jnp.split(long_att, 2, axis=1)
    low_half = exchange(long_halves[0])
    first_short = ITEMS
    *forward, short_ffn = feed_forward(
        first_short, tokens, short_proj, other_half(short_proj), gain_one, bias_one, inner_weight,
        outer_weight,
    )
    low_half, short_ffn, high_half = lax.optimization_barrier(
        (low_half, short_ffn, long_halves[1])
    )
    high_half = exchange(high_half)
    *backward, short_back, short_gain_two, short_bias_two = feed_back(
        first_short, forward[0], short_ffn, other_half(short_ffn), gain_one, bias_one, gain_two,
        bias_two, cotangent, forward[4], inner_weight, outer_weight,
    )
    high_half, short_back = after(high_half, short_back)
    short_back_other = other_half(short_back)

    mixed, long_proj = project_out_long(low_half, high_half, out_weight, mixed)
    *forward, long_ffn = feed_forward(
        0, tokens, long_proj, other_half(long_proj), gain_one, bias_one, inner_weight,
        outer_weight, forward,
    )
    norm_unit, norm_inverse, normed_low, act_low, act_slope = forward
    *backward, long_back, long_gain_two, long_bias_two = feed_back(
        0, norm_unit, long_ffn, other_half(long_ffn), gain_one, bias_one, gain_two, bias_two,
        cotangent, act_slope, inner_weight, outer_weight, backward,
    )
    output, grad_sum, grad_ffn_low, grad_pre_low = backward
    long_back_other = other_half(long_back)
    grad_hidden, grad_proj_low, short_grad, short_gain_one, short_bias_one = project_back(
        1, norm_unit, norm_inverse, grad_sum, short_back, short_back_other, gain_one, out_weight,
        heads_dev,
    )
    grad_hidden, grad_proj_low, long_grad, long_gain_one, long_bias_one = project_back(
        0, norm_unit, norm_inverse, grad_sum, long_back, long_back_other, gain_one, out_weight,
        heads_dev, (grad_hidden, grad_proj_low),
    )
    norm_lines = jnp.concatenate(
        [
            long_gain_one + short_gain_one,
            long_bias_one + short_bias_one,
            long_gain_two + short_gain_two,
            long_bias_two + short_bias_two,
        ],
        axis=0,
    )

    peers = lax.axis_size("seq")
    steps = bit_groups(peers)
    long_grad, norm_lines = after(long_grad, norm_lines)
    long_grad = exchange(long_grad)
    mine = (lax.axis_index("seq") & 3).astype(jnp.int32)[None]
    counts, terms = gradient_terms(
        mine, act_low, grad_ffn_low, normed_low, grad_pre_low, mixed, grad_proj_low, norm_lines
    )
    terms, long_grad = after(terms, long_grad)
    came = terms_sent(terms[:3], steps[0])
    long_grad = by_position(long_grad, 1)[0]
    long_dv, long_taps = long_back_values(long_pack[2], long_grad, long_line_back, long_w)
    came, last_term, long_dv, long_grad = lax.optimization_barrier(
        (came, terms[3], long_dv, long_grad)
    )
    came += terms_sent([last_term], steps[0], 3)
    long_dv = exchange(long_dv)
    long_dq, long_dk = long_back_pairs(
        long_pack[0], long_pack[1], long_pack[2], long_grad, long_s
    )
    own, long_dv, long_dq, long_dk, short_grad = lax.optimization_barrier(
        (terms[0], long_dv, long_dq, long_dk, short_grad)
    )
    part = terms_summed(own, came)
    long_back = jnp.concatenate([long_dq, long_dk], axis=1)
    terms, long_back, short_grad = lax.optimization_barrier(
        (terms_for(part, steps[1]), long_back, short_grad)
    )
    long_back = exchange(long_back)
    came = terms_sent(terms, steps[1])
    *short_parts, short_taps = short_backward(
        0, 1, reach, ids_row, ids_col, short_pack, short_grad, lines_back, short_w, short_s
    )
    long_back, short_parts, short_taps = lax.optimization_barrier(
        (long_back, short_parts, short_taps)
    )
    grads_low = unit_back(long_back, long_dv, [short_parts], unit, inverse)
    own, grads_low = after(terms[0], grads_low)
    part = terms_summed(own, came)
    for bits in steps[2:]:
        places, at, pieces = 1 << len(bits), 0, []
        for index, count in enumerate(counts):
            pieces.append(part[at : at + count].reshape(places, -1, width))
            at, counts[index] = at + count, count // places
        terms = terms_for(jnp.concatenate(pieces, axis=1), bits)
        part = terms_summed(terms[0], terms_sent(terms, bits))

    taps = slice(first_tap, first_tap + CONV_WIDTH)
    owner = (jnp.arange(heads_dev) == unit_head) & (place < units)
    kernel_part = short_taps[:, 0, taps] + jnp.where(owner[:, None], long_taps[:, taps], 0.0)
    taps_line = kernel_part.reshape(1, -1)
    taps_line = jnp.pad(taps_line, ((0, 0), (0, width - taps_line.shape[1]))).astype(BF16)
    early = lax.all_gather(jnp.concatenate([part, taps_line], axis=0), "seq", axis=0)

    weight_part = contract(tokens, grads_low, 0, 1).astype(BF16)
    terms = terms_for(weight_part.reshape(1 << len(steps[0]), -1, 3 * head_cols), steps[0])
    terms, grads_low = after(terms, grads_low)
    came = terms_sent(terms, steps[0])
    weight_all = jnp.concatenate([query_weight, key_weight, value_weight], axis=1)
    token_own = contract(grads_low, weight_all, 0, 1).astype(BF16)
    own, token_own = after(terms[0], token_own)
    weight_part = terms_summed(own, came)
    for bits in steps[1:]:
        terms = terms_for(weight_part.reshape(1 << len(bits), -1, 3 * head_cols), bits)
        weight_part = terms_summed(terms[0], terms_sent(terms, bits))
    for bits in reversed(steps):
        weight_part = terms_gathered(weight_part, bits).reshape(-1, 3 * head_cols)
    weight_sum = weight_part.astype(F32)
    outer_sum, inner_sum, out_sum, norm_sums = gathered_sums(early, counts, peers)
    kernel_sum = jnp.sum(early[:, -1, : heads_dev * CONV_WIDTH].astype(F32), axis=0).reshape(
        heads_dev, CONV_WIDTH
    )
    token_grad = grad_hidden + (token_own.astype(F32) + other_half(token_own).astype(F32))
    return (
        output,
        token_grad,
        weight_sum[:, :head_cols],
        weight_sum[:, head_cols : 2 * head_cols],
        weight_sum[:, 2 * head_cols :],
        kernel_sum,
        out_sum,
        norm_sums[0],
        norm_sums[1],
        inner_sum,
        outer_sum,
        norm_sums[2],
        norm_sums[3],
    )


def solution(mesh):
    rows = P("seq", None)
    columns = P(None, "tp")
    split_rows = P("tp", None)
    return jax.shard_map(
        shards,
        mesh=mesh,
        in_specs=(
            rows, rows, columns, columns, columns, split_rows, split_rows,
            P(), P(), columns, split_rows, P(), P(), rows,
        ),
        out_specs=(
            rows, rows, columns, columns, columns, split_rows, split_rows,
            P(), P(), columns, split_rows, P(), P(),
        ),
        check_vma=False,
    )
```

```python
import math

import jax
import jax.numpy as jnp
from jax import lax
from jax.experimental import pallas as pl
from jax.experimental.pallas import tpu as pltpu
from jax.sharding import PartitionSpec as P

TAU = 8
CONV_WIDTH = 33
HALF_WIDTH = 16
GROUP = 16
PIECE = 256
ITEMS = 2
REACH = 32
BAND_ROWS = PIECE + 2 * REACH
LINE = 640

COS_SCALE = 0.98
EPS_UNIT = 1e-06
EPS_NORM = 1e-05
NEAR_POLY = (1.158024787902832, -0.36302468180656433, 0.09245320409536362, -0.011449637822806835)
TAIL_POLY = tuple(
    0.5 * a for a in (0.254829592, -0.284496736, 1.421413741, -1.453152027, 1.061405429)
)
SLOPE_SCALE = TAU / math.pi
VMEM_BYTES = 60 * 2**20

F32 = jnp.float32
BF16 = jnp.bfloat16


def norm_terms(values):
    centered = values - jnp.mean(values, axis=-1, keepdims=True)
    inverse = lax.rsqrt(jnp.mean(centered * centered, axis=-1, keepdims=True) + EPS_NORM)
    return centered * inverse, inverse


def norm_back(scaled, unit, inverse):
    along = jnp.mean(scaled * unit, axis=-1, keepdims=True)
    return inverse * (scaled - jnp.mean(scaled, axis=-1, keepdims=True) - unit * along)


def gelu_terms(values):
    share = 1.0 / (1.0 + (0.3275911 * math.sqrt(0.5)) * jnp.abs(values))
    bell = jnp.exp(-0.5 * (values * values))
    poly = TAIL_POLY[4] * share + TAIL_POLY[3]
    for coefficient in TAIL_POLY[2::-1]:
        poly = poly * share + coefficient
    tail = poly * (share * bell)
    below = jnp.where(values < 0.0, tail, 1.0 - tail)
    return values * below, below + values * (bell * (1.0 / math.sqrt(2.0 * math.pi)))


def place_of_item(rows):
    item_at = lax.broadcasted_iota(jnp.int32, (rows, rows), 0)
    place_at = lax.broadcasted_iota(jnp.int32, (rows, rows), 1)
    hit = item_at == (place_at & 1) * PIECE + (place_at >> 1)
    return jnp.where(hit, 1.0, 0.0).astype(BF16)


def lasting(microseconds):
    return pl.CostEstimate(flops=microseconds * 1_150_000_000, bytes_accessed=0, transcendentals=0)


def contract(left, right, left_dim, right_dim):
    return lax.dot_general(
        left, right, (((left_dim,), (right_dim,)), ((), ())), preferred_element_type=F32
    )


def pair_terms(dots, same=None):
    upper = 1.0 / COS_SCALE + dots
    lower = 1.0 / COS_SCALE - dots
    upper_inv = lax.rsqrt(upper)
    lower_inv = lax.rsqrt(lower)
    wide = 1.0 / 0.7 + lower * lower_inv
    wide_inv = lax.rsqrt(wide)
    root = wide * wide_inv
    ratio = NEAR_POLY[3] * root + NEAR_POLY[2]
    ratio = ratio * root + NEAR_POLY[1]
    ratio = ratio * root + NEAR_POLY[0]
    near = ratio * ((upper * upper_inv) * wide_inv)
    if same is not None:
        near = jnp.where(same, near, 0.0)
    near_2 = near * near
    near_4 = near_2 * near_2
    weights = (near_4 * near_4).astype(BF16)
    slopes = ((near_4 * near_2) * (near * (upper_inv * lower_inv))).astype(BF16)
    return weights, slopes


def banded(line):
    wide = jnp.broadcast_to(line, (BAND_ROWS, line.shape[1]))
    return pltpu.roll(wide, 0, 1, stride=1, stride_axis=0)[:, :PIECE].astype(BF16)


def unbanded(products):
    rows_at = lax.broadcasted_iota(jnp.int32, (BAND_ROWS, BAND_ROWS), 0)
    rows_to = lax.broadcasted_iota(jnp.int32, (BAND_ROWS, BAND_ROWS), 1)
    flip = jnp.where(rows_at + rows_to == BAND_ROWS - 1, 1.0, 0.0)
    flipped = lax.dot_general(
        flip, products, (((1,), (0,)), ((), ())), precision=lax.Precision.HIGHEST,
        preferred_element_type=F32,
    )
    wide = jnp.concatenate([flipped, jnp.zeros((BAND_ROWS, LINE - PIECE), F32)], axis=1)
    return jnp.sum(pltpu.roll(wide, 0, 1, stride=1, stride_axis=0), axis=0, keepdims=True)


def padded_rows(dst, src, length):
    edge = jnp.zeros((REACH, dst.shape[1]), dst.dtype)
    dst[pl.ds(0, REACH), :] = edge
    dst[pl.ds(REACH + length, REACH), :] = edge
    for start in range(0, length, PIECE):
        dst[pl.ds(REACH + start, PIECE), :] = src[:, pl.ds(start, PIECE)].T


def rows_of(dst, src, length):
    for start in range(0, length, PIECE):
        dst[pl.ds(start, PIECE), :] = src[:, pl.ds(start, PIECE)].T


def long_forward(query, key, value, line):
    head_dim, length = query.shape
    blocks = length // PIECE
    step = 512

    def body(q_ref, k_ref, v_ref, line_ref, o_ref, w_ref, s_ref, key_rows, taps):
        block = pl.program_id(0)

        @pl.when(block == 0)
        def _():
            rows_of(key_rows, k_ref, length)
            taps[...] = jnp.zeros_like(taps)
            taps[pl.ds(length - REACH, BAND_ROWS), :] = banded(line_ref[...])

        q = q_ref[...]
        start = block * PIECE
        total = jnp.zeros((head_dim, PIECE), F32)
        for at in range(0, length, step):
            dots = contract(key_rows[pl.ds(at, step), :], q, 1, 0)
            weights, slopes = pair_terms(dots)
            near = pl.multiple_of(length + at - start, PIECE)
            weights = weights + taps[pl.ds(near, step), :]
            w_ref[pl.ds(at, step), :] = weights
            s_ref[pl.ds(at, step), :] = slopes
            total = total + contract(v_ref[:, pl.ds(at, step)], weights, 1, 0)
        o_ref[...] = total.astype(BF16)

    whole = pl.BlockSpec((head_dim, length), lambda i: (0, 0))
    large = pl.BlockSpec((None, length, PIECE), lambda i: (i, 0, 0))
    large_shape = jax.ShapeDtypeStruct((blocks, length, PIECE), BF16)
    return pl.pallas_call(
        body,
        grid=(blocks,),
        in_specs=[
            pl.BlockSpec((head_dim, PIECE), lambda i: (0, i)),
            whole,
            whole,
            pl.BlockSpec((1, LINE), lambda i: (0, 0)),
        ],
        out_specs=[pl.BlockSpec((None, head_dim, PIECE), lambda i: (i, 0, 0)), large, large],
        out_shape=[jax.ShapeDtypeStruct((blocks, head_dim, PIECE), BF16), large_shape, large_shape],
        scratch_shapes=[
            pltpu.VMEM((length, head_dim), BF16),
            pltpu.VMEM((2 * length, PIECE), BF16),
        ],
        compiler_params=pltpu.CompilerParams(vmem_limit_bytes=VMEM_BYTES),
        cost_estimate=lasting(70),
    )(query, key, value, line)


def long_back_values(value, grad, weights):
    head_dim, length = grad.shape
    blocks = length // PIECE
    step = 1024

    def body(v_ref, g_ref, w_ref, dv_ref, taps_ref, value_sum, value_rows, products):
        block = pl.program_id(0)

        @pl.when(block == 0)
        def _():
            padded_rows(value_rows, v_ref, length)
            value_sum[...] = jnp.zeros_like(value_sum)
            products[...] = jnp.zeros_like(products)

        g = g_ref[...]
        start = pl.multiple_of(block * PIECE, PIECE)
        products[...] += contract(value_rows[pl.ds(start, BAND_ROWS), :], g, 1, 0)
        for at in range(0, length, step):
            value_sum[:, pl.ds(at, step)] += contract(g, w_ref[pl.ds(at, step), :], 1, 1)

        @pl.when(block == blocks - 1)
        def _():
            for index in range(blocks):
                dv_ref[index] = value_sum[:, pl.ds(index * PIECE, PIECE)].astype(BF16)
            taps_ref[...] = unbanded(products[...])

    return pl.pallas_call(
        body,
        grid=(blocks,),
        in_specs=[
            pl.BlockSpec((head_dim, length), lambda i: (0, 0)),
            pl.BlockSpec((head_dim, PIECE), lambda i: (0, i)),
            pl.BlockSpec((None, length, PIECE), lambda i: (i, 0, 0)),
        ],
        out_specs=[
            pl.BlockSpec((blocks, head_dim, PIECE), lambda i: (0, 0, 0)),
            pl.BlockSpec((1, LINE), lambda i: (0, 0)),
        ],
        out_shape=[
            jax.ShapeDtypeStruct((blocks, head_dim, PIECE), BF16),
            jax.ShapeDtypeStruct((1, LINE), F32),
        ],
        scratch_shapes=[
            pltpu.VMEM((head_dim, length), F32),
            pltpu.VMEM((length + 2 * REACH, head_dim), BF16),
            pltpu.VMEM((BAND_ROWS, PIECE), F32),
        ],
        compiler_params=pltpu.CompilerParams(vmem_limit_bytes=VMEM_BYTES),
        cost_estimate=lasting(26),
    )(value, grad, weights)


def long_back_pairs(query, key, value, grad, slopes):
    head_dim, length = query.shape
    blocks = length // PIECE
    step = 1024

    def body(q_ref, k_ref, v_ref, g_ref, s_ref, dq_ref, dk_ref, value_rows, key_sum):
        block = pl.program_id(0)

        @pl.when(block == 0)
        def _():
            rows_of(value_rows, v_ref, length)
            key_sum[...] = jnp.zeros_like(key_sum)

        q = q_ref[...]
        g = g_ref[...]
        total = jnp.zeros((head_dim, PIECE), F32)
        for at in range(0, length, step):
            grad_weights = contract(value_rows[pl.ds(at, step), :], g, 1, 0)
            terms = grad_weights.astype(BF16) * s_ref[pl.ds(at, step), :]
            total = total + contract(k_ref[:, pl.ds(at, step)], terms, 1, 0)
            key_sum[:, pl.ds(at, step)] += contract(q, terms, 1, 1)
        dq_ref[...] = (total * SLOPE_SCALE).astype(BF16)

        @pl.when(block == blocks - 1)
        def _():
            for index in range(blocks):
                piece = key_sum[:, pl.ds(index * PIECE, PIECE)]
                dk_ref[index] = (piece * SLOPE_SCALE).astype(BF16)

    whole = pl.BlockSpec((head_dim, length), lambda i: (0, 0))
    piece = pl.BlockSpec((head_dim, PIECE), lambda i: (0, i))
    pieces_shape = jax.ShapeDtypeStruct((blocks, head_dim, PIECE), BF16)
    return pl.pallas_call(
        body,
        grid=(blocks,),
        in_specs=[
            piece,
            whole,
            whole,
            piece,
            pl.BlockSpec((None, length, PIECE), lambda i: (i, 0, 0)),
        ],
        out_specs=[
            pl.BlockSpec((None, head_dim, PIECE), lambda i: (i, 0, 0)),
            pl.BlockSpec((blocks, head_dim, PIECE), lambda i: (0, 0, 0)),
        ],
        out_shape=[pieces_shape] * 2,
        scratch_shapes=[
            pltpu.VMEM((length, head_dim), BF16),
            pltpu.VMEM((head_dim, length), F32),
        ],
        compiler_params=pltpu.CompilerParams(vmem_limit_bytes=VMEM_BYTES),
        cost_estimate=lasting(40),
    )(query, key, value, grad, slopes)


def short_forward(reach, ids_row, ids_col, pack, lines):
    _, heads, head_dim, length = pack.shape
    blocks = length // PIECE

    def body(
        reach_ref, row_ref, col_ref, q_ref, k_ref, v_ref, line_ref,
        o_ref, w_ref, s_ref, key_rows, total, taps,
    ):
        block = pl.program_id(0)

        @pl.when(block == 0)
        def _():
            taps[...] = jnp.zeros_like(taps)
            for h in range(heads):
                rows_of(key_rows.at[h], k_ref.at[h], length)
                taps[h, pl.ds(length - REACH, BAND_ROWS), :] = banded(line_ref[h])

        total[...] = jnp.zeros_like(total)
        own_ids = row_ref[...]

        def turn(step, carry):
            at = pl.multiple_of(step * PIECE, PIECE)
            same = col_ref[pl.ds(REACH + at, PIECE), :] == own_ids
            same_low = same.astype(F32).astype(BF16)
            near = pl.multiple_of(length + at - block * PIECE, PIECE)
            for h in range(heads):
                dots = contract(key_rows[h, pl.ds(at, PIECE), :], q_ref[h], 1, 0)
                weights, slopes = pair_terms(dots, same)
                weights = weights + taps[h, pl.ds(near, PIECE), :] * same_low
                w_ref[h, pl.ds(at, PIECE), :] = weights
                s_ref[h, pl.ds(at, PIECE), :] = slopes
                total[h] += contract(v_ref[h, :, pl.ds(at, PIECE)], weights, 1, 0)
            return carry

        lax.fori_loop(reach_ref[0, block], reach_ref[1, block], turn, 0)
        o_ref[...] = total[...].astype(BF16)

    def packed(which):
        return pl.BlockSpec((None, heads, head_dim, length), lambda i: (which, 0, 0, 0))

    block_spec = pl.BlockSpec((heads, head_dim, PIECE), lambda i: (0, 0, i))
    large = pl.BlockSpec((None, heads, length, PIECE), lambda i: (i, 0, 0, 0))
    large_shape = jax.ShapeDtypeStruct((blocks, heads, length, PIECE), BF16)
    return pl.pallas_call(
        body,
        grid=(blocks,),
        in_specs=[
            pl.BlockSpec(memory_space=pltpu.SMEM),
            pl.BlockSpec((1, PIECE), lambda i: (0, i)),
            pl.BlockSpec(ids_col.shape, lambda i: (0, 0)),
            pl.BlockSpec((None, heads, head_dim, PIECE), lambda i: (0, 0, 0, i)),
            packed(1),
            packed(2),
            pl.BlockSpec((heads, 1, LINE), lambda i: (0, 0, 0)),
        ],
        out_specs=[block_spec, large, large],
        out_shape=[jax.ShapeDtypeStruct((heads, head_dim, length), BF16), large_shape, large_shape],
        scratch_shapes=[
            pltpu.VMEM((heads, length, head_dim), BF16),
            pltpu.VMEM((heads, head_dim, PIECE), F32),
            pltpu.VMEM((heads, 2 * length, PIECE), BF16),
        ],
        compiler_params=pltpu.CompilerParams(vmem_limit_bytes=VMEM_BYTES),
        cost_estimate=lasting(28),
    )(reach, ids_row, ids_col, pack, pack, pack, lines)


def short_backward(reach, ids_row, ids_col, pack, grad, weights, slopes):
    _, heads, head_dim, length = pack.shape
    blocks = length // PIECE

    def body(
        reach_ref, row_ref, col_ref, q_ref, k_ref, v_ref, g_ref, w_ref, s_ref,
        dq_ref, dk_ref, dv_ref, taps_ref, value_rows, products,
    ):
        block = pl.program_id(0)

        @pl.when(block == 0)
        def _():
            for h in range(heads):
                padded_rows(value_rows.at[h], v_ref.at[h], length)
            dk_ref[...] = jnp.zeros_like(dk_ref)
            dv_ref[...] = jnp.zeros_like(dv_ref)
            products[...] = jnp.zeros_like(products)

        start = pl.multiple_of(block * PIECE, PIECE)
        near = (col_ref[pl.ds(start, BAND_ROWS), :] == row_ref[...]).astype(F32)
        for h in range(heads):
            products[h] += (
                contract(value_rows[h, pl.ds(start, BAND_ROWS), :], g_ref[h], 1, 0) * near
            )
        dq_ref[...] = jnp.zeros_like(dq_ref)

        def turn(step, carry):
            at = pl.multiple_of(step * PIECE, PIECE)
            for h in range(heads):
                own = g_ref[h]
                grad_weights = contract(value_rows[h, pl.ds(REACH + at, PIECE), :], own, 1, 0)
                terms = grad_weights.astype(BF16) * s_ref[h, pl.ds(at, PIECE), :]
                dq_ref[h] += contract(k_ref[h, :, pl.ds(at, PIECE)], terms, 1, 0) * SLOPE_SCALE
                dk_ref[h, :, pl.ds(at, PIECE)] += contract(q_ref[h], terms, 1, 1) * SLOPE_SCALE
                dv_ref[h, :, pl.ds(at, PIECE)] += contract(own, w_ref[h, pl.ds(at, PIECE), :], 1, 1)
            return carry

        lax.fori_loop(reach_ref[0, block], reach_ref[1, block], turn, 0)

        @pl.when(block == blocks - 1)
        def _():
            for h in range(heads):
                taps_ref[h] = unbanded(products[h])

    def packed(which):
        return pl.BlockSpec((None, heads, head_dim, length), lambda i: (which, 0, 0, 0))

    block_spec = pl.BlockSpec((heads, head_dim, PIECE), lambda i: (0, 0, i))
    whole = pl.BlockSpec((heads, head_dim, length), lambda i: (0, 0, 0))
    large = pl.BlockSpec((None, heads, length, PIECE), lambda i: (i, 0, 0, 0))
    whole_shape = jax.ShapeDtypeStruct((heads, head_dim, length), F32)
    return pl.pallas_call(
        body,
        grid=(blocks,),
        in_specs=[
            pl.BlockSpec(memory_space=pltpu.SMEM),
            pl.BlockSpec((1, PIECE), lambda i: (0, i)),
            pl.BlockSpec(ids_col.shape, lambda i: (0, 0)),
            pl.BlockSpec((None, heads, head_dim, PIECE), lambda i: (0, 0, 0, i)),
            packed(1),
            packed(2),
            block_spec,
            large,
            large,
        ],
        out_specs=[block_spec, whole, whole, pl.BlockSpec((heads, 1, LINE), lambda i: (0, 0, 0))],
        out_shape=[whole_shape] * 3 + [jax.ShapeDtypeStruct((heads, 1, LINE), F32)],
        scratch_shapes=[
            pltpu.VMEM((heads, length + 2 * REACH, head_dim), BF16),
            pltpu.VMEM((heads, BAND_ROWS, PIECE), F32),
        ],
        compiler_params=pltpu.CompilerParams(vmem_limit_bytes=VMEM_BYTES),
        cost_estimate=lasting(28),
    )(reach, ids_row, ids_col, pack, pack, pack, grad, weights, slopes)


def project_in(tokens, query_weight, key_weight, value_weight, heads):
    row_total, width = tokens.shape
    cols = query_weight.shape[1]
    head_dim = cols // heads
    blocks = row_total // PIECE
    long_rows = ITEMS * PIECE

    def body(t_ref, wq_ref, wk_ref, wv_ref, long_ref, short_ref, unit_ref, inv_ref, turned, rows):
        block = pl.program_id(0)

        @pl.when(block == 0)
        def _():
            for index, ref in enumerate((wq_ref, wk_ref, wv_ref)):
                turned[pl.ds(index * cols, cols), :] = ref[...].T
            long_ref[pl.ds(ITEMS * heads, GROUP - ITEMS * heads)] = jnp.zeros(
                (GROUP - ITEMS * heads, 3 * head_dim, PIECE), BF16
            )

        @pl.when(block < ITEMS)
        def _():
            item_at = lax.broadcasted_iota(jnp.int32, (PIECE, long_rows), 0)
            place_at = lax.broadcasted_iota(jnp.int32, (PIECE, long_rows), 1)
            pick = jnp.where(place_at == ITEMS * item_at + block, 1.0, 0.0).astype(BF16)
            rows[...] = contract(pick, t_ref[pl.ds(0, long_rows), :], 1, 0).astype(BF16)

        @pl.when(block >= ITEMS)
        def _():
            rows[...] = t_ref[pl.ds(pl.multiple_of(block * PIECE, PIECE), PIECE), :]

        parts = contract(turned[...], rows[...], 1, 1).reshape(3, heads, head_dim, PIECE)
        raw = parts[:2]
        inverse = lax.rsqrt(jnp.sum(raw * raw, axis=2, keepdims=True) + EPS_UNIT)
        unit = raw * inverse
        unit_ref[...] = unit
        inv_ref[...] = inverse
        low = unit.astype(BF16)
        short_ref[:2] = low
        short_ref[2] = parts[2].astype(BF16)

        @pl.when(block < ITEMS)
        def _():
            for h in range(heads):
                unit_at = block * heads + h
                long_ref[unit_at, pl.ds(0, head_dim), :] = low[0, h]
                long_ref[unit_at, pl.ds(head_dim, head_dim), :] = low[1, h]
                long_ref[unit_at, pl.ds(2 * head_dim, head_dim), :] = parts[2, h].astype(BF16)

    weight = pl.BlockSpec((width, cols), lambda i: (0, 0))
    return pl.pallas_call(
        body,
        grid=(blocks,),
        in_specs=[pl.BlockSpec((row_total, width), lambda i: (0, 0)), weight, weight, weight],
        out_specs=[
            pl.BlockSpec((GROUP, 3 * head_dim, PIECE), lambda i: (0, 0, 0)),
            pl.BlockSpec(
                (3, heads, head_dim, PIECE), lambda i: (0, 0, 0, jnp.maximum(i - ITEMS, 0))
            ),
            pl.BlockSpec((2, heads, head_dim, PIECE), lambda i: (0, 0, 0, i)),
            pl.BlockSpec((2, heads, 1, PIECE), lambda i: (0, 0, 0, i)),
        ],
        out_shape=[
            jax.ShapeDtypeStruct((GROUP, 3 * head_dim, PIECE), BF16),
            jax.ShapeDtypeStruct((3, heads, head_dim, row_total - long_rows), BF16),
            jax.ShapeDtypeStruct((2, heads, head_dim, row_total), F32),
            jax.ShapeDtypeStruct((2, heads, 1, row_total), F32),
        ],
        scratch_shapes=[pltpu.VMEM((3 * cols, width), BF16), pltpu.VMEM((PIECE, width), BF16)],
        compiler_params=pltpu.CompilerParams(vmem_limit_bytes=VMEM_BYTES),
        cost_estimate=lasting(10),
    )(tokens, query_weight, key_weight, value_weight)


def row_blocks(first, count, cols, span=PIECE):
    return pl.BlockSpec((span, cols), lambda i: (i + first, 0))


ANYWHERE = pl.BlockSpec(memory_space=pl.ANY)


def project_out_short(short_att, out_weight, row_total):
    heads, head_dim, short_rows = short_att.shape
    cols, width = out_weight.shape
    span = ITEMS * PIECE

    def body(a_ref, w_ref, mixed_ref, part_ref):
        mixed = a_ref[...].reshape(cols, span)
        mixed_ref[...] = mixed
        part_ref[...] = contract(mixed, w_ref[...], 0, 0).astype(BF16)

    return pl.pallas_call(
        body,
        grid=(short_rows // span,),
        in_specs=[
            pl.BlockSpec((heads, head_dim, span), lambda i: (0, 0, i)),
            pl.BlockSpec((cols, width), lambda i: (0, 0)),
        ],
        out_specs=[
            pl.BlockSpec((cols, span), lambda i: (0, i + 1)),
            pl.BlockSpec((span, width), lambda i: (i, 0)),
        ],
        out_shape=[
            jax.ShapeDtypeStruct((cols, row_total), BF16),
            jax.ShapeDtypeStruct((short_rows, width), BF16),
        ],
        compiler_params=pltpu.CompilerParams(vmem_limit_bytes=VMEM_BYTES),
        cost_estimate=lasting(4),
    )(short_att, out_weight)


def project_out_long(moved_low, moved_high, out_weight, mixed):
    cols, width = out_weight.shape
    half = moved_low.shape[1]
    head_dim = 2 * half
    heads = cols // head_dim
    span = ITEMS * PIECE

    def body(low_ref, high_ref, w_ref, old_ref, mixed_ref, part_ref, items):
        for h in range(heads):
            for item in range(ITEMS):
                for at, ref in ((0, low_ref), (half, high_ref)):
                    items[pl.ds(h * head_dim + at, half), pl.ds(item * PIECE, PIECE)] = ref[
                        item * heads + h
                    ]
        placed = contract(items[...], place_of_item(span), 1, 0).astype(BF16)
        mixed_ref[...] = placed
        part_ref[...] = contract(placed, w_ref[...], 0, 0).astype(BF16)

    return pl.pallas_call(
        body,
        grid=(1,),
        in_specs=[
            pl.BlockSpec((GROUP, half, PIECE), lambda i: (0, 0, 0)),
            pl.BlockSpec((GROUP, half, PIECE), lambda i: (0, 0, 0)),
            pl.BlockSpec((cols, width), lambda i: (0, 0)),
            ANYWHERE,
        ],
        out_specs=[
            pl.BlockSpec((cols, span), lambda i: (0, 0)),
            pl.BlockSpec((span, width), lambda i: (0, 0)),
        ],
        out_shape=[
            jax.ShapeDtypeStruct(mixed.shape, BF16),
            jax.ShapeDtypeStruct((span, width), BF16),
        ],
        scratch_shapes=[pltpu.VMEM((cols, span), BF16)],
        input_output_aliases={3: 0},
        compiler_params=pltpu.CompilerParams(vmem_limit_bytes=VMEM_BYTES),
        cost_estimate=lasting(3),
    )(moved_low, moved_high, out_weight, mixed)


def feed_forward(first, tokens, own, other, gain, bias, inner_weight, outer_weight, into=()):
    row_total, width = tokens.shape
    count = own.shape[0] // PIECE
    hidden_units = inner_weight.shape[1]

    def body(t_ref, own_ref, other_ref, gain_ref, bias_ref, inner_ref, outer_ref, *rest):
        unit_ref, inv_ref, low_ref, act_ref, slope_ref, part_ref = rest[len(into) :]
        hidden = t_ref[...].astype(F32) + (
            own_ref[...].astype(F32) + other_ref[...].astype(F32)
        )
        unit, inverse = norm_terms(hidden)
        unit_ref[...] = unit
        inv_ref[...] = inverse
        low = (unit * gain_ref[...] + bias_ref[...]).astype(BF16)
        low_ref[...] = low
        act, slope = gelu_terms(contract(low, inner_ref[...], 1, 0))
        act = act.astype(BF16)
        act_ref[...] = act
        slope_ref[...] = slope.astype(BF16)
        part_ref[...] = contract(act, outer_ref[...], 1, 0).astype(BF16)

    own_rows = row_blocks(0, count, width)
    rows = row_blocks(first, count, width)
    units = row_blocks(first, count, hidden_units)
    line = pl.BlockSpec((1, width), lambda i: (0, 0))
    return pl.pallas_call(
        body,
        grid=(count,),
        in_specs=[
            rows, own_rows, own_rows, line, line,
            pl.BlockSpec((width, hidden_units), lambda i: (0, 0)),
            pl.BlockSpec((hidden_units, width), lambda i: (0, 0)),
        ]
        + [ANYWHERE] * len(into),
        out_specs=[rows, row_blocks(first, count, 1), rows, units, units, own_rows],
        out_shape=[
            jax.ShapeDtypeStruct((row_total, width), F32),
            jax.ShapeDtypeStruct((row_total, 1), F32),
            jax.ShapeDtypeStruct((row_total, width), BF16),
            jax.ShapeDtypeStruct((row_total, hidden_units), BF16),
            jax.ShapeDtypeStruct((row_total, hidden_units), BF16),
            jax.ShapeDtypeStruct((count * PIECE, width), BF16),
        ],
        input_output_aliases={7 + at: at for at in range(len(into))},
        compiler_params=pltpu.CompilerParams(vmem_limit_bytes=VMEM_BYTES),
        cost_estimate=lasting(3 * count),
    )(tokens, own, other, gain, bias, inner_weight, outer_weight, *into)


def feed_back(
    first, unit_one, own, other, gain_one, bias_one, gain_two, bias_two, cotangent, slope,
    inner_weight, outer_weight, into=(),
):
    row_total, width = unit_one.shape
    count = own.shape[0] // PIECE
    hidden_units = inner_weight.shape[1]

    def body(
        unit_ref, own_ref, other_ref, gain_one_ref, bias_one_ref, gain_ref, bias_ref, g_ref,
        slope_ref, inner_ref, outer_ref, *rest,
    ):
        out_ref, sum_ref, low_ref, pre_ref, part_ref, gain_grad_ref, bias_grad_ref = rest[
            len(into) :
        ]

        @pl.when(pl.program_id(0) == 0)
        def _():
            gain_grad_ref[...] = jnp.zeros_like(gain_grad_ref)
            bias_grad_ref[...] = jnp.zeros_like(bias_grad_ref)

        normed = unit_ref[...] * gain_one_ref[...] + bias_one_ref[...]
        unit, inverse = norm_terms(
            normed + (own_ref[...].astype(F32) + other_ref[...].astype(F32))
        )
        out_ref[...] = (unit * gain_ref[...] + bias_ref[...]).astype(BF16)
        g = g_ref[...].astype(F32)
        gain_grad_ref[...] += jnp.sum(g * unit, axis=0, keepdims=True)
        bias_grad_ref[...] += jnp.sum(g, axis=0, keepdims=True)
        grad_sum = norm_back(g * gain_ref[...], unit, inverse)
        sum_ref[...] = grad_sum
        low = grad_sum.astype(BF16)
        low_ref[...] = low
        pre = contract(low, outer_ref[...], 1, 1) * slope_ref[...].astype(F32)
        pre = pre.astype(BF16)
        pre_ref[...] = pre
        part_ref[...] = contract(pre, inner_ref[...], 1, 1).astype(BF16)

    own_rows = row_blocks(0, count, width)
    rows = row_blocks(first, count, width)
    units = row_blocks(first, count, hidden_units)
    line = pl.BlockSpec((1, width), lambda i: (0, 0))
    return pl.pallas_call(
        body,
        grid=(count,),
        in_specs=[
            rows, own_rows, own_rows, line, line, line, line, rows, units,
            pl.BlockSpec((width, hidden_units), lambda i: (0, 0)),
            pl.BlockSpec((hidden_units, width), lambda i: (0, 0)),
        ]
        + [ANYWHERE] * len(into),
        out_specs=[rows, rows, rows, units, own_rows, line, line],
        out_shape=[
            jax.ShapeDtypeStruct((row_total, width), BF16),
            jax.ShapeDtypeStruct((row_total, width), F32),
            jax.ShapeDtypeStruct((row_total, width), BF16),
            jax.ShapeDtypeStruct((row_total, hidden_units), BF16),
            jax.ShapeDtypeStruct((count * PIECE, width), BF16),
            jax.ShapeDtypeStruct((1, width), F32),
            jax.ShapeDtypeStruct((1, width), F32),
        ],
        input_output_aliases={11 + at: at for at in range(len(into))},
        compiler_params=pltpu.CompilerParams(vmem_limit_bytes=VMEM_BYTES),
        cost_estimate=lasting(3 * count),
    )(
        unit_one, own, other, gain_one, bias_one, gain_two, bias_two, cotangent, slope,
        inner_weight, outer_weight, *into,
    )


def project_back(first, unit, inverse, grad_sum, own, other, gain, out_weight, heads, into=()):
    row_total, width = unit.shape
    cols = out_weight.shape[0]
    head_dim = cols // heads
    span = ITEMS * PIECE
    count = own.shape[0] // span
    is_long = first == 0

    def body(unit_ref, inv_ref, sum_ref, own_ref, other_ref, gain_ref, w_ref, *rest):
        hidden_ref, low_ref, att_ref, gain_grad_ref, bias_grad_ref = rest[len(into) :]

        @pl.when(pl.program_id(0) == 0)
        def _():
            gain_grad_ref[...] = jnp.zeros_like(gain_grad_ref)
            bias_grad_ref[...] = jnp.zeros_like(bias_grad_ref)

        unit = unit_ref[...]
        grad = sum_ref[...] + (own_ref[...].astype(F32) + other_ref[...].astype(F32))
        gain_grad_ref[...] += jnp.sum(grad * unit, axis=0, keepdims=True)
        bias_grad_ref[...] += jnp.sum(grad, axis=0, keepdims=True)
        hidden = norm_back(grad * gain_ref[...], unit, inv_ref[...])
        hidden_ref[...] = hidden
        low = hidden.astype(BF16)
        low_ref[...] = low
        att = contract(w_ref[...], low, 1, 1).astype(BF16)
        if is_long:
            items = contract(att, place_of_item(span), 1, 1).astype(BF16)
            for h in range(heads):
                for item in range(ITEMS):
                    att_ref[item * heads + h] = items[
                        h * head_dim : (h + 1) * head_dim, item * PIECE : (item + 1) * PIECE
                    ]
            att_ref[pl.ds(ITEMS * heads, GROUP - ITEMS * heads)] = jnp.zeros(
                (GROUP - ITEMS * heads, head_dim, PIECE), BF16
            )
        else:
            att_ref[...] = att.reshape(heads, head_dim, span)

    own_rows = row_blocks(0, count, width, span)
    rows = row_blocks(first, count, width, span)
    line = pl.BlockSpec((1, width), lambda i: (0, 0))
    if is_long:
        att_spec = pl.BlockSpec((GROUP, head_dim, PIECE), lambda i: (0, 0, 0))
        att_shape = (GROUP, head_dim, PIECE)
    else:
        att_spec = pl.BlockSpec((heads, head_dim, span), lambda i: (0, 0, i))
        att_shape = (heads, head_dim, count * span)
    return pl.pallas_call(
        body,
        grid=(count,),
        in_specs=[
            rows, row_blocks(first, count, 1, span), rows, own_rows, own_rows, line,
            pl.BlockSpec((cols, width), lambda i: (0, 0)),
        ]
        + [ANYWHERE] * len(into),
        out_specs=[rows, rows, att_spec, line, line],
        out_shape=[
            jax.ShapeDtypeStruct((row_total, width), F32),
            jax.ShapeDtypeStruct((row_total, width), BF16),
            jax.ShapeDtypeStruct(att_shape, BF16),
            jax.ShapeDtypeStruct((1, width), F32),
            jax.ShapeDtypeStruct((1, width), F32),
        ],
        input_output_aliases={7 + at: at for at in range(len(into))},
        compiler_params=pltpu.CompilerParams(vmem_limit_bytes=VMEM_BYTES),
        cost_estimate=lasting(4 * count),
    )(unit, inverse, grad_sum, own, other, gain, out_weight, *into)


NORM_SLOT = 16
OUT_SLOT = 8


def first_rows(source, mine_ref, away, second, count):
    first = lax.bitwise_xor(mine_ref[0], away)
    return source[pl.ds(pl.multiple_of((first * 4 + second) * count, count), count), :]


def terms_call(body, mine, rows, columns, lines, counts, width, scratch, microseconds):
    span = ITEMS * PIECE
    shape = (4, sum(counts), width)
    return counts, pl.pallas_call(
        body,
        grid=(rows[0].shape[0] // span,),
        in_specs=[pl.BlockSpec(memory_space=pltpu.SMEM)]
        + [pl.BlockSpec((span, array.shape[1]), lambda i: (i, 0)) for array in rows]
        + [pl.BlockSpec((array.shape[0], span), lambda i: (0, i)) for array in columns]
        + [pl.BlockSpec(array.shape, lambda i: (0, 0)) for array in lines],
        out_specs=[pl.BlockSpec(shape, lambda i: (0, 0, 0))] * 4,
        out_shape=[jax.ShapeDtypeStruct(shape, BF16)] * 4,
        scratch_shapes=[pltpu.VMEM(dims, F32) for dims in scratch],
        compiler_params=pltpu.CompilerParams(vmem_limit_bytes=VMEM_BYTES),
        cost_estimate=lasting(microseconds),
    )(mine, *rows, *columns, *lines)


def outer_terms(mine, act, grad_ffn, norm_lines):
    units, width = act.shape[1], grad_ffn.shape[1]
    counts = [units // 16, NORM_SLOT]

    def body(mine_ref, act_ref, ffn_ref, norm_ref, *rest):
        outs, (outer,) = rest[:4], rest[4:]

        @pl.when(pl.program_id(0) == 0)
        def _():
            outer[...] = jnp.zeros_like(outer)

        outer[...] += contract(act_ref[...], ffn_ref[...], 0, 0)

        @pl.when(pl.program_id(0) == pl.num_programs(0) - 1)
        def _():
            slot = lax.broadcasted_iota(jnp.int32, (NORM_SLOT, width), 0) == 0
            for away, ref in enumerate(outs):
                line = norm_ref[pl.ds(lax.bitwise_xor(mine_ref[0], away), 1), :]
                for second in range(4):
                    rows = first_rows(outer, mine_ref, away, second, counts[0])
                    ref[second, pl.ds(0, counts[0]), :] = rows.astype(BF16)
                    lines = jnp.where(slot, line if second == 0 else 0.0, 0.0)
                    ref[second, pl.ds(counts[0], NORM_SLOT), :] = lines.astype(BF16)

    return terms_call(
        body, mine, [act, grad_ffn], [], [norm_lines], counts, width, [(units, width)], 9
    )


def inner_terms(mine, normed, grad_pre, mixed, grad_proj):
    units, width, cols = grad_pre.shape[1], normed.shape[1], mixed.shape[0]
    counts = [width // 16, width // 16, cols // 16, OUT_SLOT]

    def body(mine_ref, low_ref, pre_ref, proj_ref, mixed_ref, *rest):
        outs, (inner, out) = rest[:4], rest[4:]

        @pl.when(pl.program_id(0) == 0)
        def _():
            inner[...] = jnp.zeros_like(inner)
            out[...] = jnp.zeros_like(out)

        inner[...] += contract(low_ref[...], pre_ref[...], 0, 0)
        out[...] += contract(mixed_ref[...], proj_ref[...], 1, 0)

        @pl.when(pl.program_id(0) == pl.num_programs(0) - 1)
        def _():
            for away, ref in enumerate(outs):
                for second in range(4):
                    both = first_rows(inner, mine_ref, away, second, counts[0]).astype(BF16)
                    ref[second, pl.ds(0, counts[0]), :] = both[:, :width]
                    ref[second, pl.ds(counts[0], counts[1]), :] = both[:, width:]
                    tail = jnp.concatenate(
                        [
                            first_rows(out, mine_ref, away, second, counts[2]),
                            jnp.zeros((OUT_SLOT, width), F32),
                        ],
                        axis=0,
                    )
                    ref[second, pl.ds(counts[0] + counts[1], counts[2] + OUT_SLOT), :] = (
                        tail.astype(BF16)
                    )

    return terms_call(
        body, mine, [normed, grad_pre, grad_proj], [mixed], [], counts, width,
        [(width, units), (cols, width)], 9,
    )


def next_terms(part, counts, bits):
    places, at, pieces = 1 << len(bits), 0, []
    for index, count in enumerate(counts):
        pieces.append(part[at : at + count].reshape(places, -1, part.shape[1]))
        at, counts[index] = at + count, count // places
    return terms_for(jnp.concatenate(pieces, axis=1), bits)


def gathered_sums(gathered, counts, targets, shapes):
    peers = gathered.shape[0]
    width = gathered.shape[2]
    groups = bit_groups(peers)

    def body(in_ref, *outs):
        for at_place in range(peers):
            order = 0
            for bits in groups:
                size = 1 << len(bits)
                order = order * size + ((at_place >> bits[0]) & (size - 1))
            at = 0
            for count, target in zip(counts, targets):
                if target is not None:
                    index, column = target
                    rows = in_ref[at_place, pl.ds(at, count), :].astype(F32)
                    if column is not None:
                        outs[index][pl.ds(order * count, count), pl.ds(column, width)] = rows
                    elif order % (peers // 4) == 0:
                        outs[index][pl.ds(order // (peers // 4), 1), :] = rows[:1]
                at += count

    def whole(shape):
        return pl.BlockSpec(shape, lambda: (0,) * len(shape))

    return pl.pallas_call(
        body,
        in_specs=[whole(gathered.shape)],
        out_specs=[whole(shape) for shape in shapes],
        out_shape=[jax.ShapeDtypeStruct(shape, F32) for shape in shapes],
        compiler_params=pltpu.CompilerParams(vmem_limit_bytes=VMEM_BYTES),
        cost_estimate=lasting(4),
    )(gathered)


def placed_sums(mine, arrays, counts, targets, shapes):
    width = arrays[0].shape[2]

    def body(mine_ref, *refs):
        ins, outs = refs[: len(arrays)], refs[len(arrays) :]
        for first_away, ref in enumerate(ins):
            first = lax.bitwise_xor(mine_ref[0], first_away)
            for second_away in range(ref.shape[0]):
                second = lax.bitwise_xor(mine_ref[1], second_away)
                order = first * ref.shape[0] + second
                at = 0
                for count, target in zip(counts, targets):
                    rows = pl.ds(at, count)
                    at += count
                    if target is None:
                        continue
                    out = outs[target[0]]
                    if target[1] is not None:
                        to = pl.ds(pl.multiple_of(order * count, count), count)
                        out[to, pl.ds(target[1], width)] = ref[second_away, rows, :].astype(F32)
                    elif out.shape[0] > 4:
                        out[pl.ds(order, 1), :] = ref[second_away, rows, :].astype(F32)[:1]
                    else:

                        @pl.when(second == 0)
                        def _():
                            out[pl.ds(first, 1), :] = ref[second_away, rows, :].astype(F32)[:1]

    def whole(shape):
        return pl.BlockSpec(shape, lambda: (0,) * len(shape))

    return pl.pallas_call(
        body,
        in_specs=[pl.BlockSpec(memory_space=pltpu.SMEM)] + [whole(array.shape) for array in arrays],
        out_specs=[whole(shape) for shape in shapes],
        out_shape=[jax.ShapeDtypeStruct(shape, F32) for shape in shapes],
        compiler_params=pltpu.CompilerParams(vmem_limit_bytes=VMEM_BYTES),
        cost_estimate=lasting(4),
    )(mine, *arrays)


def gathered_or_placed(part, steps, counts, targets, shapes):
    peers = lax.axis_size("seq")
    place = lax.axis_index("seq")
    if len(steps) != 2 or any(len(bits) != 2 for bits in steps):
        gathered = lax.all_gather(part, "seq", axis=0)
        taken = [target for target in targets if target is None or target[1] is not None or
                 shapes[target[0]][0] == 4]
        sums = gathered_sums(gathered, counts[: len(taken)], taken, [
            shape for shape in shapes if shape[0] != peers])
        return sums if len(sums) == len(shapes) else [
            *sums, gathered[:, sum(counts[:-1])].astype(F32)]
    arrays = [part[None]] + [came[None] for came in terms_sent([part] * 4, steps[1])]
    own = jnp.concatenate(arrays, axis=0)
    arrays = [own] + terms_sent([own] * 4, steps[0])
    mine = jnp.stack([place & 3, (place >> 2) & 3]).astype(jnp.int32)
    return placed_sums(mine, arrays, counts, targets, shapes)


def unit_back(moved_pairs, moved_values, short_parts, unit, inverse):
    heads, head_dim = unit.shape[1:3]
    short_heads, _, short_rows = short_parts[0][0].shape
    count = len(short_parts)
    span = ITEMS * PIECE
    blocks = 1 + short_rows // span
    cols = heads * head_dim

    def body(*refs):
        pairs_ref, values_ref = refs[:2]
        short_refs = refs[2 : 2 + 3 * count]
        unit_ref, inv_ref, out_ref, items = refs[2 + 3 * count :]
        block = pl.program_id(0)

        def short_part(which):
            return jnp.concatenate([short_refs[3 * at + which][...] for at in range(count)], axis=0)

        def back(which, grad):
            unit = unit_ref[which]
            along = jnp.sum(unit * grad, axis=1, keepdims=True)
            return ((grad - unit * along) * inv_ref[which]).astype(BF16).reshape(cols, span)

        @pl.when(block == 0)
        def _():
            def long_part(ref, at):
                part = pl.ds(at, head_dim)
                heads_of = [
                    jnp.concatenate([ref[h, part, :], ref[heads + h, part, :]], axis=1)
                    for h in range(heads)
                ]
                return jnp.stack(heads_of, axis=0)

            for which in range(2):
                items[pl.ds(which * cols, cols), :] = back(
                    which, long_part(pairs_ref, which * head_dim).astype(F32)
                )
            items[pl.ds(2 * cols, cols), :] = long_part(values_ref, 0).reshape(cols, span)
            out_ref[...] = contract(items[...], place_of_item(span), 1, 0).astype(BF16)

        @pl.when(block > 0)
        def _():
            out_ref[pl.ds(0, cols), :] = back(0, short_part(0))
            out_ref[pl.ds(cols, cols), :] = back(1, short_part(1))
            out_ref[pl.ds(2 * cols, cols), :] = short_part(2).astype(BF16).reshape(
                cols, span
            )

    short = pl.BlockSpec(
        (short_heads, head_dim, span), lambda i: (0, 0, jnp.maximum(i - 1, 0))
    )
    return pl.pallas_call(
        body,
        grid=(blocks,),
        in_specs=[
            pl.BlockSpec((GROUP, moved_pairs.shape[1], PIECE), lambda i: (0, 0, 0)),
            pl.BlockSpec((GROUP, head_dim, PIECE), lambda i: (0, 0, 0)),
        ]
        + [short] * (3 * count)
        + [
            pl.BlockSpec((2, heads, head_dim, span), lambda i: (0, 0, 0, i)),
            pl.BlockSpec((2, heads, 1, span), lambda i: (0, 0, 0, i)),
        ],
        out_specs=pl.BlockSpec((3 * cols, span), lambda i: (0, i)),
        out_shape=jax.ShapeDtypeStruct((3 * cols, span * blocks), BF16),
        scratch_shapes=[pltpu.VMEM((3 * cols, span), BF16)],
        compiler_params=pltpu.CompilerParams(vmem_limit_bytes=VMEM_BYTES),
        cost_estimate=lasting(8),
    )(moved_pairs, moved_values, *sum(map(tuple, short_parts), ()), unit, inverse)


def other_half(part):
    return lax.ppermute(part, "tp", [(0, 1), (1, 0)])


def bit_groups(peers):
    bits = peers.bit_length() - 1
    return [list(range(low, min(low + 2, bits))) for low in range(0, bits, 2)]


def terms_for(part, bits):
    mine = (lax.axis_index("seq") >> bits[0]) & ((1 << len(bits)) - 1)
    return [
        lax.dynamic_index_in_dim(part, mine ^ away, 0, False) for away in range(1 << len(bits))
    ]


def in_order(gathered, peers):
    sizes = [1 << len(bits) for bits in reversed(bit_groups(peers))]
    count = len(sizes)
    array = gathered.reshape(sizes + list(gathered.shape[1:]))
    array = jnp.transpose(array, list(range(count))[::-1] + [count, count + 1])
    return array.reshape(-1, gathered.shape[-1])


def terms_sent(terms, bits, first=1):
    peers = lax.axis_size("seq")
    terms = terms if first > 1 else terms[1:]
    return [
        lax.ppermute(term, "seq", [(i, i ^ (away << bits[0])) for i in range(peers)])
        for away, term in enumerate(terms, first)
    ]


def terms_gathered(own, bits):
    mine = (lax.axis_index("seq") >> bits[0]) & ((1 << len(bits)) - 1)
    every = jnp.stack([own] + terms_sent([own] * (1 << len(bits)), bits), axis=0)
    return jnp.stack(
        [
            lax.dynamic_index_in_dim(every, mine ^ place, 0, False)
            for place in range(1 << len(bits))
        ],
        axis=0,
    )


def terms_summed(own, came):
    total = own.astype(F32)
    for term in came:
        total = total + term.astype(F32)
    return total.astype(BF16)


def after(first, second):
    return lax.optimization_barrier((first, second))


def shards(
    tokens,
    short_lengths,
    query_weight,
    key_weight,
    value_weight,
    conv_kernel,
    out_weight,
    gain_one,
    bias_one,
    inner_weight,
    outer_weight,
    gain_two,
    bias_two,
    cotangent,
):
    row_total, width = tokens.shape
    heads_dev = conv_kernel.shape[0]
    head_cols = query_weight.shape[1]
    head_dim = head_cols // heads_dev
    short_rows = row_total - ITEMS * PIECE
    units = ITEMS * heads_dev
    place = lax.axis_index("seq") % GROUP
    groups = [
        [first + i for i in range(GROUP)] for first in range(0, lax.axis_size("seq"), GROUP)
    ]

    def exchange(pieces):
        return lax.all_to_all(pieces, "seq", 0, 0, axis_index_groups=groups)

    def by_position(moved, count):
        return jnp.transpose(moved, (1, 0, 2)).reshape(count, head_dim, GROUP * PIECE)

    item_ends = jnp.cumsum(short_lengths[0])
    positions = jnp.arange(short_rows, dtype=jnp.int32)
    item_ids = jnp.sum((positions[:, None] >= item_ends[None, :]).astype(jnp.int32), axis=1)
    ids_row = item_ids[None, :]
    ids_col = jnp.pad(item_ids, (REACH, REACH), constant_values=-1)[:, None]
    item_starts = jnp.concatenate([jnp.zeros((1,), jnp.int32), item_ends[:-1]])
    block_first = jnp.arange(0, short_rows, PIECE, dtype=jnp.int32)
    block_last = block_first + (PIECE - 1)
    inside = (item_starts[None, :] <= block_last[:, None]) & (
        item_ends[None, :] > block_first[:, None]
    )
    lowest = jnp.min(jnp.where(inside, item_starts[None, :], short_rows), axis=1)
    highest = jnp.max(jnp.where(inside, item_ends[None, :], 0), axis=1)
    reach = jnp.stack([lowest // PIECE, (highest + PIECE - 1) // PIECE]).astype(jnp.int32)

    last_tap = LINE - REACH - HALF_WIDTH
    lines = jnp.pad(
        conv_kernel[:, ::-1], ((0, 0), (last_tap, LINE - last_tap - CONV_WIDTH))
    )[:, None, :]
    unit_head = place % heads_dev
    long_line = lax.dynamic_index_in_dim(lines, unit_head, 0, False)

    long_send, short_pack, unit, inverse = project_in(
        tokens, query_weight, key_weight, value_weight, heads_dev
    )
    lines_of = [line[None, :] for line in (gain_one, bias_one, gain_two, bias_two)]
    gain_one, bias_one, gain_two, bias_two = lines_of

    long_moved = exchange(long_send)
    short_att, short_w, short_s = short_forward(reach, ids_row, ids_col, short_pack, lines)
    mixed, short_proj = project_out_short(short_att, out_weight, row_total)
    long_moved, short_proj = after(long_moved, short_proj)
    long_pack = by_position(long_moved, 3)
    long_att, long_w, long_s = long_forward(long_pack[0], long_pack[1], long_pack[2], long_line)

    long_att, short_proj = after(long_att, short_proj)
    long_halves = jnp.split(long_att, 2, axis=1)
    low_half = exchange(long_halves[0])
    first_short = ITEMS
    *forward, short_ffn = feed_forward(
        first_short, tokens, short_proj, other_half(short_proj), gain_one, bias_one, inner_weight,
        outer_weight,
    )
    low_half, short_ffn, high_half = lax.optimization_barrier(
        (low_half, short_ffn, long_halves[1])
    )
    high_half = exchange(high_half)
    *backward, short_back, short_gain_two, short_bias_two = feed_back(
        first_short, forward[0], short_ffn, other_half(short_ffn), gain_one, bias_one, gain_two,
        bias_two, cotangent, forward[4], inner_weight, outer_weight,
    )
    high_half, short_back = after(high_half, short_back)
    short_back_other = other_half(short_back)

    mixed, long_proj = project_out_long(low_half, high_half, out_weight, mixed)
    *forward, long_ffn = feed_forward(
        0, tokens, long_proj, other_half(long_proj), gain_one, bias_one, inner_weight,
        outer_weight, forward,
    )
    norm_unit, norm_inverse, normed_low, act_low, act_slope = forward
    *backward, long_back, long_gain_two, long_bias_two = feed_back(
        0, norm_unit, long_ffn, other_half(long_ffn), gain_one, bias_one, gain_two, bias_two,
        cotangent, act_slope, inner_weight, outer_weight, backward,
    )
    output, grad_sum, grad_ffn_low, grad_pre_low = backward
    long_back_other = other_half(long_back)
    grad_hidden, grad_proj_low, short_grad, short_gain_one, short_bias_one = project_back(
        1, norm_unit, norm_inverse, grad_sum, short_back, short_back_other, gain_one, out_weight,
        heads_dev,
    )
    grad_hidden, grad_proj_low, long_grad, long_gain_one, long_bias_one = project_back(
        0, norm_unit, norm_inverse, grad_sum, long_back, long_back_other, gain_one, out_weight,
        heads_dev, (grad_hidden, grad_proj_low),
    )
    norm_lines = jnp.concatenate(
        [
            long_gain_one + short_gain_one,
            long_bias_one + short_bias_one,
            long_gain_two + short_gain_two,
            long_bias_two + short_bias_two,
        ],
        axis=0,
    )

    peers = lax.axis_size("seq")
    steps = bit_groups(peers)
    long_grad, norm_lines = after(long_grad, norm_lines)
    long_grad = exchange(long_grad)
    mine = (lax.axis_index("seq") & 3).astype(jnp.int32)[None]
    outer_counts, outer_terms_now = outer_terms(mine, act_low, grad_ffn_low, norm_lines)
    outer_terms_now, grad_pre_low = after(outer_terms_now, grad_pre_low)
    outer_came = terms_sent(outer_terms_now, steps[0])
    inner_counts, inner_terms_now = inner_terms(
        mine, normed_low, grad_pre_low, mixed, grad_proj_low
    )
    inner_terms_now, long_grad = after(inner_terms_now, long_grad)
    long_grad = by_position(long_grad, 1)[0]
    long_dv, long_taps = long_back_values(long_pack[2], long_grad, long_w)
    outer_came, own, inner_terms_now, long_dv, long_grad = lax.optimization_barrier(
        (outer_came, outer_terms_now[0], inner_terms_now, long_dv, long_grad)
    )
    outer_part = terms_summed(own, outer_came)
    inner_came = terms_sent(inner_terms_now, steps[0])
    outer_terms_now, long_dv, long_grad = lax.optimization_barrier(
        (terms_for(outer_part, steps[1]), long_dv, long_grad)
    )
    outer_came = terms_sent(outer_terms_now, steps[1])
    long_dv = exchange(long_dv)
    long_dq, long_dk = long_back_pairs(
        long_pack[0], long_pack[1], long_pack[2], long_grad, long_s
    )
    outer_came, outer_own, inner_came, inner_own, long_dv, long_dq, long_dk, short_grad = (
        lax.optimization_barrier(
            (
                outer_came, outer_terms_now[0], inner_came, inner_terms_now[0], long_dv, long_dq,
                long_dk, short_grad,
            )
        )
    )
    outer_part = terms_summed(outer_own, outer_came)
    for bits in steps[2:]:
        terms = next_terms(outer_part, outer_counts, bits)
        outer_part = terms_summed(terms[0], terms_sent(terms, bits))
    inner_part = terms_summed(inner_own, inner_came)
    long_back = jnp.concatenate([long_dq, long_dk], axis=1)
    inner_terms_now, outer_part, long_back, short_grad = lax.optimization_barrier(
        (terms_for(inner_part, steps[1]), outer_part, long_back, short_grad)
    )
    outer_sum, norm_sums = gathered_or_placed(
        outer_part, steps, outer_counts, [(0, 0), (1, None)], [outer_weight.shape, (4, width)]
    )
    long_back = exchange(long_back)
    inner_came = terms_sent(inner_terms_now, steps[1])
    *short_parts, short_taps = short_backward(
        reach, ids_row, ids_col, short_pack, short_grad, short_w, short_s
    )
    long_back, short_parts, short_taps = lax.optimization_barrier(
        (long_back, short_parts, short_taps)
    )
    grads_low = unit_back(long_back, long_dv, [short_parts], unit, inverse)
    own, grads_low = after(inner_terms_now[0], grads_low)
    inner_part = terms_summed(own, inner_came)
    for bits in steps[2:]:
        terms = next_terms(inner_part, inner_counts, bits)
        inner_part = terms_summed(terms[0], terms_sent(terms, bits))

    first_tap = BAND_ROWS - 1 - REACH + HALF_WIDTH
    taps = slice(first_tap, first_tap - CONV_WIDTH, -1)
    owner = (jnp.arange(heads_dev) == unit_head) & (place < units)
    kernel_part = short_taps[:, 0, taps] + jnp.where(owner[:, None], long_taps[:, taps], 0.0)
    taps_line = kernel_part.reshape(1, -1)
    taps_line = jnp.pad(taps_line, ((0, 15), (0, width - taps_line.shape[1]))).astype(BF16)
    inner_sum, out_sum, tap_lines = gathered_or_placed(
        jnp.concatenate([inner_part, taps_line], axis=0), steps, inner_counts + [16],
        [(0, 0), (0, width), (1, 0), None, (2, None)],
        [inner_weight.shape, out_weight.shape, (peers, width)],
    )
    kernel_sum = jnp.sum(tap_lines[:, : heads_dev * CONV_WIDTH], axis=0).reshape(
        heads_dev, CONV_WIDTH
    )

    weight_part = contract(tokens, grads_low, 0, 1).astype(BF16)
    terms = terms_for(weight_part.reshape(1 << len(steps[0]), -1, 3 * head_cols), steps[0])
    terms, grads_low = after(terms, grads_low)
    came = terms_sent(terms, steps[0])
    weight_all = jnp.concatenate([query_weight, key_weight, value_weight], axis=1)
    token_own = contract(grads_low, weight_all, 0, 1).astype(BF16)
    own, token_own = after(terms[0], token_own)
    weight_part = terms_summed(own, came)
    for bits in steps[1:]:
        terms = terms_for(weight_part.reshape(1 << len(bits), -1, 3 * head_cols), bits)
        weight_part = terms_summed(terms[0], terms_sent(terms, bits))
    for bits in reversed(steps):
        weight_part = terms_gathered(weight_part, bits).reshape(-1, 3 * head_cols)
    weight_sum = weight_part.astype(F32)
    token_grad = grad_hidden + (token_own.astype(F32) + other_half(token_own).astype(F32))
    return (
        output,
        token_grad,
        weight_sum[:, :head_cols],
        weight_sum[:, head_cols : 2 * head_cols],
        weight_sum[:, 2 * head_cols :],
        kernel_sum,
        out_sum,
        norm_sums[0],
        norm_sums[1],
        inner_sum,
        outer_sum,
        norm_sums[2],
        norm_sums[3],
    )


def solution(mesh):
    rows = P("seq", None)
    columns = P(None, "tp")
    split_rows = P("tp", None)
    return jax.shard_map(
        shards,
        mesh=mesh,
        in_specs=(
            rows, rows, columns, columns, columns, split_rows, split_rows,
            P(), P(), columns, split_rows, P(), P(), rows,
        ),
        out_specs=(
            rows, rows, columns, columns, columns, split_rows, split_rows,
            P(), P(), columns, split_rows, P(), P(),
        ),
        check_vma=False,
    )
```

```python
import math

import jax
import jax.numpy as jnp
from jax import lax
from jax.experimental import pallas as pl
from jax.experimental.pallas import tpu as pltpu
from jax.sharding import PartitionSpec as P

TAU = 8
CONV_WIDTH = 33
HALF_WIDTH = 16
GROUP = 16
PIECE = 256
ITEMS = 2
REACH = 32
BAND_ROWS = PIECE + 2 * REACH
LINE = 640

COS_SCALE = 0.98
EPS_UNIT = 1e-06
EPS_NORM = 1e-05
NEAR_POLY = (1.158024787902832, -0.36302468180656433, 0.09245320409536362, -0.011449637822806835)
TAIL_POLY = tuple(
    0.5 * a for a in (0.254829592, -0.284496736, 1.421413741, -1.453152027, 1.061405429)
)
SLOPE_SCALE = TAU / math.pi
VMEM_BYTES = 60 * 2**20

F32 = jnp.float32
BF16 = jnp.bfloat16


def norm_terms(values):
    centered = values - jnp.mean(values, axis=-1, keepdims=True)
    inverse = lax.rsqrt(jnp.mean(centered * centered, axis=-1, keepdims=True) + EPS_NORM)
    return centered * inverse, inverse


def norm_back(scaled, unit, inverse):
    along = jnp.mean(scaled * unit, axis=-1, keepdims=True)
    return inverse * (scaled - jnp.mean(scaled, axis=-1, keepdims=True) - unit * along)


def gelu_terms(values):
    share = 1.0 / (1.0 + (0.3275911 * math.sqrt(0.5)) * jnp.abs(values))
    bell = jnp.exp(-0.5 * (values * values))
    poly = TAIL_POLY[4] * share + TAIL_POLY[3]
    for coefficient in TAIL_POLY[2::-1]:
        poly = poly * share + coefficient
    tail = poly * (share * bell)
    below = jnp.where(values < 0.0, tail, 1.0 - tail)
    return values * below, below + values * (bell * (1.0 / math.sqrt(2.0 * math.pi)))


def place_of_item(rows):
    item_at = lax.broadcasted_iota(jnp.int32, (rows, rows), 0)
    place_at = lax.broadcasted_iota(jnp.int32, (rows, rows), 1)
    hit = item_at == (place_at & 1) * PIECE + (place_at >> 1)
    return jnp.where(hit, 1.0, 0.0).astype(BF16)


def lasting(microseconds):
    return pl.CostEstimate(flops=microseconds * 1_150_000_000, bytes_accessed=0, transcendentals=0)


def contract(left, right, left_dim, right_dim):
    return lax.dot_general(
        left, right, (((left_dim,), (right_dim,)), ((), ())), preferred_element_type=F32
    )


def pair_terms(dots, same=None):
    upper = 1.0 / COS_SCALE + dots
    lower = 1.0 / COS_SCALE - dots
    upper_inv = lax.rsqrt(upper)
    lower_inv = lax.rsqrt(lower)
    wide = 1.0 / 0.7 + lower * lower_inv
    wide_inv = lax.rsqrt(wide)
    root = wide * wide_inv
    ratio = NEAR_POLY[3] * root + NEAR_POLY[2]
    ratio = ratio * root + NEAR_POLY[1]
    ratio = ratio * root + NEAR_POLY[0]
    near = ratio * ((upper * upper_inv) * wide_inv)
    if same is not None:
        near = jnp.where(same, near, 0.0)
    near_2 = near * near
    near_4 = near_2 * near_2
    weights = (near_4 * near_4).astype(BF16)
    slopes = ((near_4 * near_2) * (near * (upper_inv * lower_inv))).astype(BF16)
    return weights, slopes


def banded(line):
    wide = jnp.broadcast_to(line, (BAND_ROWS, line.shape[1]))
    return pltpu.roll(wide, 0, 1, stride=1, stride_axis=0)[:, :PIECE].astype(BF16)


def unbanded(products):
    rows_at = lax.broadcasted_iota(jnp.int32, (BAND_ROWS, BAND_ROWS), 0)
    rows_to = lax.broadcasted_iota(jnp.int32, (BAND_ROWS, BAND_ROWS), 1)
    flip = jnp.where(rows_at + rows_to == BAND_ROWS - 1, 1.0, 0.0)
    flipped = lax.dot_general(
        flip, products, (((1,), (0,)), ((), ())), precision=lax.Precision.HIGHEST,
        preferred_element_type=F32,
    )
    wide = jnp.concatenate([flipped, jnp.zeros((BAND_ROWS, LINE - PIECE), F32)], axis=1)
    return jnp.sum(pltpu.roll(wide, 0, 1, stride=1, stride_axis=0), axis=0, keepdims=True)


def padded_rows(dst, src, length):
    edge = jnp.zeros((REACH, dst.shape[1]), dst.dtype)
    dst[pl.ds(0, REACH), :] = edge
    dst[pl.ds(REACH + length, REACH), :] = edge
    for start in range(0, length, PIECE):
        dst[pl.ds(REACH + start, PIECE), :] = src[:, pl.ds(start, PIECE)].T


def rows_of(dst, src, length):
    for start in range(0, length, PIECE):
        dst[pl.ds(start, PIECE), :] = src[:, pl.ds(start, PIECE)].T


def long_forward(query, key, value, line):
    head_dim, length = query.shape
    blocks = length // PIECE
    step = 512

    def body(q_ref, k_ref, v_ref, line_ref, o_ref, w_ref, s_ref, key_rows, taps):
        block = pl.program_id(0)

        @pl.when(block == 0)
        def _():
            rows_of(key_rows, k_ref, length)
            taps[...] = jnp.zeros_like(taps)
            taps[pl.ds(length - REACH, BAND_ROWS), :] = banded(line_ref[...])

        q = q_ref[...]
        start = block * PIECE
        total = jnp.zeros((head_dim, PIECE), F32)
        for at in range(0, length, step):
            dots = contract(key_rows[pl.ds(at, step), :], q, 1, 0)
            weights, slopes = pair_terms(dots)
            near = pl.multiple_of(length + at - start, PIECE)
            weights = weights + taps[pl.ds(near, step), :]
            w_ref[pl.ds(at, step), :] = weights
            s_ref[pl.ds(at, step), :] = slopes
            total = total + contract(v_ref[:, pl.ds(at, step)], weights, 1, 0)
        o_ref[...] = total.astype(BF16)

    whole = pl.BlockSpec((head_dim, length), lambda i: (0, 0))
    large = pl.BlockSpec((None, length, PIECE), lambda i: (i, 0, 0))
    large_shape = jax.ShapeDtypeStruct((blocks, length, PIECE), BF16)
    return pl.pallas_call(
        body,
        grid=(blocks,),
        in_specs=[
            pl.BlockSpec((head_dim, PIECE), lambda i: (0, i)),
            whole,
            whole,
            pl.BlockSpec((1, LINE), lambda i: (0, 0)),
        ],
        out_specs=[pl.BlockSpec((None, head_dim, PIECE), lambda i: (i, 0, 0)), large, large],
        out_shape=[jax.ShapeDtypeStruct((blocks, head_dim, PIECE), BF16), large_shape, large_shape],
        scratch_shapes=[
            pltpu.VMEM((length, head_dim), BF16),
            pltpu.VMEM((2 * length, PIECE), BF16),
        ],
        compiler_params=pltpu.CompilerParams(vmem_limit_bytes=VMEM_BYTES),
        cost_estimate=lasting(70),
    )(query, key, value, line)


def long_back_values(value, grad, weights):
    head_dim, length = grad.shape
    blocks = length // PIECE
    step = 1024

    def body(v_ref, g_ref, w_ref, dv_ref, taps_ref, value_sum, value_rows, products):
        block = pl.program_id(0)

        @pl.when(block == 0)
        def _():
            padded_rows(value_rows, v_ref, length)
            value_sum[...] = jnp.zeros_like(value_sum)
            products[...] = jnp.zeros_like(products)

        g = g_ref[...]
        start = pl.multiple_of(block * PIECE, PIECE)
        products[...] += contract(value_rows[pl.ds(start, BAND_ROWS), :], g, 1, 0)
        for at in range(0, length, step):
            value_sum[:, pl.ds(at, step)] += contract(g, w_ref[pl.ds(at, step), :], 1, 1)

        @pl.when(block == blocks - 1)
        def _():
            for index in range(blocks):
                dv_ref[index] = value_sum[:, pl.ds(index * PIECE, PIECE)].astype(BF16)
            taps_ref[...] = unbanded(products[...])

    return pl.pallas_call(
        body,
        grid=(blocks,),
        in_specs=[
            pl.BlockSpec((head_dim, length), lambda i: (0, 0)),
            pl.BlockSpec((head_dim, PIECE), lambda i: (0, i)),
            pl.BlockSpec((None, length, PIECE), lambda i: (i, 0, 0)),
        ],
        out_specs=[
            pl.BlockSpec((blocks, head_dim, PIECE), lambda i: (0, 0, 0)),
            pl.BlockSpec((1, LINE), lambda i: (0, 0)),
        ],
        out_shape=[
            jax.ShapeDtypeStruct((blocks, head_dim, PIECE), BF16),
            jax.ShapeDtypeStruct((1, LINE), F32),
        ],
        scratch_shapes=[
            pltpu.VMEM((head_dim, length), F32),
            pltpu.VMEM((length + 2 * REACH, head_dim), BF16),
            pltpu.VMEM((BAND_ROWS, PIECE), F32),
        ],
        compiler_params=pltpu.CompilerParams(vmem_limit_bytes=VMEM_BYTES),
        cost_estimate=lasting(1),
    )(value, grad, weights)


def long_back_pairs(query, key, value, grad, slopes):
    head_dim, length = query.shape
    blocks = length // PIECE
    step = 1024

    def body(q_ref, k_ref, v_ref, g_ref, s_ref, dq_ref, dk_ref, value_rows, key_sum):
        block = pl.program_id(0)

        @pl.when(block == 0)
        def _():
            rows_of(value_rows, v_ref, length)
            key_sum[...] = jnp.zeros_like(key_sum)

        q = q_ref[...]
        g = g_ref[...]
        total = jnp.zeros((head_dim, PIECE), F32)
        for at in range(0, length, step):
            grad_weights = contract(value_rows[pl.ds(at, step), :], g, 1, 0)
            terms = grad_weights.astype(BF16) * s_ref[pl.ds(at, step), :]
            total = total + contract(k_ref[:, pl.ds(at, step)], terms, 1, 0)
            key_sum[:, pl.ds(at, step)] += contract(q, terms, 1, 1)
        dq_ref[...] = (total * SLOPE_SCALE).astype(BF16)

        @pl.when(block == blocks - 1)
        def _():
            for index in range(blocks):
                piece = key_sum[:, pl.ds(index * PIECE, PIECE)]
                dk_ref[index] = (piece * SLOPE_SCALE).astype(BF16)

    whole = pl.BlockSpec((head_dim, length), lambda i: (0, 0))
    piece = pl.BlockSpec((head_dim, PIECE), lambda i: (0, i))
    pieces_shape = jax.ShapeDtypeStruct((blocks, head_dim, PIECE), BF16)
    return pl.pallas_call(
        body,
        grid=(blocks,),
        in_specs=[
            piece,
            whole,
            whole,
            piece,
            pl.BlockSpec((None, length, PIECE), lambda i: (i, 0, 0)),
        ],
        out_specs=[
            pl.BlockSpec((None, head_dim, PIECE), lambda i: (i, 0, 0)),
            pl.BlockSpec((blocks, head_dim, PIECE), lambda i: (0, 0, 0)),
        ],
        out_shape=[pieces_shape] * 2,
        scratch_shapes=[
            pltpu.VMEM((length, head_dim), BF16),
            pltpu.VMEM((head_dim, length), F32),
        ],
        compiler_params=pltpu.CompilerParams(vmem_limit_bytes=VMEM_BYTES),
        cost_estimate=lasting(40),
    )(query, key, value, grad, slopes)


def short_forward(reach, ids_row, ids_col, pack, lines):
    _, heads, head_dim, length = pack.shape
    blocks = length // PIECE

    def body(
        reach_ref, row_ref, col_ref, q_ref, k_ref, v_ref, line_ref,
        o_ref, w_ref, s_ref, key_rows, total, taps,
    ):
        block = pl.program_id(0)

        @pl.when(block == 0)
        def _():
            taps[...] = jnp.zeros_like(taps)
            for h in range(heads):
                rows_of(key_rows.at[h], k_ref.at[h], length)
                taps[h, pl.ds(length - REACH, BAND_ROWS), :] = banded(line_ref[h])

        total[...] = jnp.zeros_like(total)
        own_ids = row_ref[...]

        def turn(step, carry):
            at = pl.multiple_of(step * PIECE, PIECE)
            same = col_ref[pl.ds(REACH + at, PIECE), :] == own_ids
            same_low = same.astype(F32).astype(BF16)
            near = pl.multiple_of(length + at - block * PIECE, PIECE)
            for h in range(heads):
                dots = contract(key_rows[h, pl.ds(at, PIECE), :], q_ref[h], 1, 0)
                weights, slopes = pair_terms(dots, same)
                weights = weights + taps[h, pl.ds(near, PIECE), :] * same_low
                w_ref[h, pl.ds(at, PIECE), :] = weights
                s_ref[h, pl.ds(at, PIECE), :] = slopes
                total[h] += contract(v_ref[h, :, pl.ds(at, PIECE)], weights, 1, 0)
            return carry

        lax.fori_loop(reach_ref[0, block], reach_ref[1, block], turn, 0)
        o_ref[...] = total[...].astype(BF16)

    def packed(which):
        return pl.BlockSpec((None, heads, head_dim, length), lambda i: (which, 0, 0, 0))

    block_spec = pl.BlockSpec((heads, head_dim, PIECE), lambda i: (0, 0, i))
    large = pl.BlockSpec((None, heads, length, PIECE), lambda i: (i, 0, 0, 0))
    large_shape = jax.ShapeDtypeStruct((blocks, heads, length, PIECE), BF16)
    return pl.pallas_call(
        body,
        grid=(blocks,),
        in_specs=[
            pl.BlockSpec(memory_space=pltpu.SMEM),
            pl.BlockSpec((1, PIECE), lambda i: (0, i)),
            pl.BlockSpec(ids_col.shape, lambda i: (0, 0)),
            pl.BlockSpec((None, heads, head_dim, PIECE), lambda i: (0, 0, 0, i)),
            packed(1),
            packed(2),
            pl.BlockSpec((heads, 1, LINE), lambda i: (0, 0, 0)),
        ],
        out_specs=[block_spec, large, large],
        out_shape=[jax.ShapeDtypeStruct((heads, head_dim, length), BF16), large_shape, large_shape],
        scratch_shapes=[
            pltpu.VMEM((heads, length, head_dim), BF16),
            pltpu.VMEM((heads, head_dim, PIECE), F32),
            pltpu.VMEM((heads, 2 * length, PIECE), BF16),
        ],
        compiler_params=pltpu.CompilerParams(vmem_limit_bytes=VMEM_BYTES),
        cost_estimate=lasting(28),
    )(reach, ids_row, ids_col, pack, pack, pack, lines)


def short_backward(reach, ids_row, ids_col, pack, grad, weights, slopes):
    _, heads, head_dim, length = pack.shape
    blocks = length // PIECE

    def body(
        reach_ref, row_ref, col_ref, q_ref, k_ref, v_ref, g_ref, w_ref, s_ref,
        dq_ref, dk_ref, dv_ref, taps_ref, value_rows, products,
    ):
        block = pl.program_id(0)

        @pl.when(block == 0)
        def _():
            for h in range(heads):
                padded_rows(value_rows.at[h], v_ref.at[h], length)
            dk_ref[...] = jnp.zeros_like(dk_ref)
            dv_ref[...] = jnp.zeros_like(dv_ref)
            products[...] = jnp.zeros_like(products)

        start = pl.multiple_of(block * PIECE, PIECE)
        near = (col_ref[pl.ds(start, BAND_ROWS), :] == row_ref[...]).astype(F32)
        for h in range(heads):
            products[h] += (
                contract(value_rows[h, pl.ds(start, BAND_ROWS), :], g_ref[h], 1, 0) * near
            )
        dq_ref[...] = jnp.zeros_like(dq_ref)

        def turn(step, carry):
            at = pl.multiple_of(step * PIECE, PIECE)
            for h in range(heads):
                own = g_ref[h]
                grad_weights = contract(value_rows[h, pl.ds(REACH + at, PIECE), :], own, 1, 0)
                terms = grad_weights.astype(BF16) * s_ref[h, pl.ds(at, PIECE), :]
                dq_ref[h] += contract(k_ref[h, :, pl.ds(at, PIECE)], terms, 1, 0) * SLOPE_SCALE
                dk_ref[h, :, pl.ds(at, PIECE)] += contract(q_ref[h], terms, 1, 1) * SLOPE_SCALE
                dv_ref[h, :, pl.ds(at, PIECE)] += contract(own, w_ref[h, pl.ds(at, PIECE), :], 1, 1)
            return carry

        lax.fori_loop(reach_ref[0, block], reach_ref[1, block], turn, 0)

        @pl.when(block == blocks - 1)
        def _():
            for h in range(heads):
                taps_ref[h] = unbanded(products[h])

    def packed(which):
        return pl.BlockSpec((None, heads, head_dim, length), lambda i: (which, 0, 0, 0))

    block_spec = pl.BlockSpec((heads, head_dim, PIECE), lambda i: (0, 0, i))
    whole = pl.BlockSpec((heads, head_dim, length), lambda i: (0, 0, 0))
    large = pl.BlockSpec((None, heads, length, PIECE), lambda i: (i, 0, 0, 0))
    whole_shape = jax.ShapeDtypeStruct((heads, head_dim, length), F32)
    return pl.pallas_call(
        body,
        grid=(blocks,),
        in_specs=[
            pl.BlockSpec(memory_space=pltpu.SMEM),
            pl.BlockSpec((1, PIECE), lambda i: (0, i)),
            pl.BlockSpec(ids_col.shape, lambda i: (0, 0)),
            pl.BlockSpec((None, heads, head_dim, PIECE), lambda i: (0, 0, 0, i)),
            packed(1),
            packed(2),
            block_spec,
            large,
            large,
        ],
        out_specs=[block_spec, whole, whole, pl.BlockSpec((heads, 1, LINE), lambda i: (0, 0, 0))],
        out_shape=[whole_shape] * 3 + [jax.ShapeDtypeStruct((heads, 1, LINE), F32)],
        scratch_shapes=[
            pltpu.VMEM((heads, length + 2 * REACH, head_dim), BF16),
            pltpu.VMEM((heads, BAND_ROWS, PIECE), F32),
        ],
        compiler_params=pltpu.CompilerParams(vmem_limit_bytes=VMEM_BYTES),
        cost_estimate=lasting(28),
    )(reach, ids_row, ids_col, pack, pack, pack, grad, weights, slopes)


def project_in(tokens, query_weight, key_weight, value_weight, heads):
    row_total, width = tokens.shape
    cols = query_weight.shape[1]
    head_dim = cols // heads
    blocks = row_total // PIECE
    long_rows = ITEMS * PIECE

    def body(t_ref, wq_ref, wk_ref, wv_ref, long_ref, short_ref, unit_ref, inv_ref, turned, rows):
        block = pl.program_id(0)

        @pl.when(block == 0)
        def _():
            for index, ref in enumerate((wq_ref, wk_ref, wv_ref)):
                turned[pl.ds(index * cols, cols), :] = ref[...].T
            long_ref[pl.ds(ITEMS * heads, GROUP - ITEMS * heads)] = jnp.zeros(
                (GROUP - ITEMS * heads, 3 * head_dim, PIECE), BF16
            )

        @pl.when(block < ITEMS)
        def _():
            item_at = lax.broadcasted_iota(jnp.int32, (PIECE, long_rows), 0)
            place_at = lax.broadcasted_iota(jnp.int32, (PIECE, long_rows), 1)
            pick = jnp.where(place_at == ITEMS * item_at + block, 1.0, 0.0).astype(BF16)
            rows[...] = contract(pick, t_ref[pl.ds(0, long_rows), :], 1, 0).astype(BF16)

        @pl.when(block >= ITEMS)
        def _():
            rows[...] = t_ref[pl.ds(pl.multiple_of(block * PIECE, PIECE), PIECE), :]

        parts = contract(turned[...], rows[...], 1, 1).reshape(3, heads, head_dim, PIECE)
        raw = parts[:2]
        inverse = lax.rsqrt(jnp.sum(raw * raw, axis=2, keepdims=True) + EPS_UNIT)
        unit = raw * inverse
        unit_ref[...] = unit
        inv_ref[...] = inverse
        low = unit.astype(BF16)
        short_ref[:2] = low
        short_ref[2] = parts[2].astype(BF16)

        @pl.when(block < ITEMS)
        def _():
            for h in range(heads):
                unit_at = block * heads + h
                long_ref[unit_at, pl.ds(0, head_dim), :] = low[0, h]
                long_ref[unit_at, pl.ds(head_dim, head_dim), :] = low[1, h]
                long_ref[unit_at, pl.ds(2 * head_dim, head_dim), :] = parts[2, h].astype(BF16)

    weight = pl.BlockSpec((width, cols), lambda i: (0, 0))
    return pl.pallas_call(
        body,
        grid=(blocks,),
        in_specs=[pl.BlockSpec((row_total, width), lambda i: (0, 0)), weight, weight, weight],
        out_specs=[
            pl.BlockSpec((GROUP, 3 * head_dim, PIECE), lambda i: (0, 0, 0)),
            pl.BlockSpec(
                (3, heads, head_dim, PIECE), lambda i: (0, 0, 0, jnp.maximum(i - ITEMS, 0))
            ),
            pl.BlockSpec((2, heads, head_dim, PIECE), lambda i: (0, 0, 0, i)),
            pl.BlockSpec((2, heads, 1, PIECE), lambda i: (0, 0, 0, i)),
        ],
        out_shape=[
            jax.ShapeDtypeStruct((GROUP, 3 * head_dim, PIECE), BF16),
            jax.ShapeDtypeStruct((3, heads, head_dim, row_total - long_rows), BF16),
            jax.ShapeDtypeStruct((2, heads, head_dim, row_total), F32),
            jax.ShapeDtypeStruct((2, heads, 1, row_total), F32),
        ],
        scratch_shapes=[pltpu.VMEM((3 * cols, width), BF16), pltpu.VMEM((PIECE, width), BF16)],
        compiler_params=pltpu.CompilerParams(vmem_limit_bytes=VMEM_BYTES),
        cost_estimate=lasting(10),
    )(tokens, query_weight, key_weight, value_weight)


def row_blocks(first, count, cols, span=PIECE):
    return pl.BlockSpec((span, cols), lambda i: (i + first, 0))


ANYWHERE = pl.BlockSpec(memory_space=pl.ANY)


def project_out_short(short_att, out_weight, row_total):
    heads, head_dim, short_rows = short_att.shape
    cols, width = out_weight.shape
    span = ITEMS * PIECE

    def body(a_ref, w_ref, mixed_ref, part_ref):
        mixed = a_ref[...].reshape(cols, span)
        mixed_ref[...] = mixed
        part_ref[...] = contract(mixed, w_ref[...], 0, 0).astype(BF16)

    return pl.pallas_call(
        body,
        grid=(short_rows // span,),
        in_specs=[
            pl.BlockSpec((heads, head_dim, span), lambda i: (0, 0, i)),
            pl.BlockSpec((cols, width), lambda i: (0, 0)),
        ],
        out_specs=[
            pl.BlockSpec((cols, span), lambda i: (0, i + 1)),
            pl.BlockSpec((span, width), lambda i: (i, 0)),
        ],
        out_shape=[
            jax.ShapeDtypeStruct((cols, row_total), BF16),
            jax.ShapeDtypeStruct((short_rows, width), BF16),
        ],
        compiler_params=pltpu.CompilerParams(vmem_limit_bytes=VMEM_BYTES),
        cost_estimate=lasting(4),
    )(short_att, out_weight)


def project_out_long(moved, out_weight, mixed):
    cols, width = out_weight.shape
    head_dim = moved.shape[1]
    heads = cols // head_dim
    span = ITEMS * PIECE

    def body(m_ref, w_ref, old_ref, mixed_ref, part_ref, items):
        for h in range(heads):
            for item in range(ITEMS):
                items[pl.ds(h * head_dim, head_dim), pl.ds(item * PIECE, PIECE)] = m_ref[
                    item * heads + h
                ]
        placed = contract(items[...], place_of_item(span), 1, 0).astype(BF16)
        mixed_ref[...] = placed
        part_ref[...] = contract(placed, w_ref[...], 0, 0).astype(BF16)

    return pl.pallas_call(
        body,
        grid=(1,),
        in_specs=[
            pl.BlockSpec((GROUP, head_dim, PIECE), lambda i: (0, 0, 0)),
            pl.BlockSpec((cols, width), lambda i: (0, 0)),
            ANYWHERE,
        ],
        out_specs=[
            pl.BlockSpec((cols, span), lambda i: (0, 0)),
            pl.BlockSpec((span, width), lambda i: (0, 0)),
        ],
        out_shape=[
            jax.ShapeDtypeStruct(mixed.shape, BF16),
            jax.ShapeDtypeStruct((span, width), BF16),
        ],
        scratch_shapes=[pltpu.VMEM((cols, span), BF16)],
        input_output_aliases={2: 0},
        compiler_params=pltpu.CompilerParams(vmem_limit_bytes=VMEM_BYTES),
        cost_estimate=lasting(3),
    )(moved, out_weight, mixed)


def feed_forward(first, tokens, own, other, gain, bias, inner_weight, outer_weight, into=()):
    row_total, width = tokens.shape
    count = own.shape[0] // PIECE
    hidden_units = inner_weight.shape[1]

    def body(t_ref, own_ref, other_ref, gain_ref, bias_ref, inner_ref, outer_ref, *rest):
        unit_ref, inv_ref, low_ref, act_ref, slope_ref, part_ref = rest[len(into) :]
        hidden = t_ref[...].astype(F32) + (
            own_ref[...].astype(F32) + other_ref[...].astype(F32)
        )
        unit, inverse = norm_terms(hidden)
        unit_ref[...] = unit
        inv_ref[...] = inverse
        low = (unit * gain_ref[...] + bias_ref[...]).astype(BF16)
        low_ref[...] = low
        act, slope = gelu_terms(contract(low, inner_ref[...], 1, 0))
        act = act.astype(BF16)
        act_ref[...] = act
        slope_ref[...] = slope.astype(BF16)
        part_ref[...] = contract(act, outer_ref[...], 1, 0).astype(BF16)

    own_rows = row_blocks(0, count, width)
    rows = row_blocks(first, count, width)
    units = row_blocks(first, count, hidden_units)
    line = pl.BlockSpec((1, width), lambda i: (0, 0))
    return pl.pallas_call(
        body,
        grid=(count,),
        in_specs=[
            rows, own_rows, own_rows, line, line,
            pl.BlockSpec((width, hidden_units), lambda i: (0, 0)),
            pl.BlockSpec((hidden_units, width), lambda i: (0, 0)),
        ]
        + [ANYWHERE] * len(into),
        out_specs=[rows, row_blocks(first, count, 1), rows, units, units, own_rows],
        out_shape=[
            jax.ShapeDtypeStruct((row_total, width), F32),
            jax.ShapeDtypeStruct((row_total, 1), F32),
            jax.ShapeDtypeStruct((row_total, width), BF16),
            jax.ShapeDtypeStruct((row_total, hidden_units), BF16),
            jax.ShapeDtypeStruct((row_total, hidden_units), BF16),
            jax.ShapeDtypeStruct((count * PIECE, width), BF16),
        ],
        input_output_aliases={7 + at: at for at in range(len(into))},
        compiler_params=pltpu.CompilerParams(vmem_limit_bytes=VMEM_BYTES),
        cost_estimate=lasting(3 * count),
    )(tokens, own, other, gain, bias, inner_weight, outer_weight, *into)


def feed_back(
    first, unit_one, own, other, gain_one, bias_one, gain_two, bias_two, cotangent, slope,
    inner_weight, outer_weight, into=(),
):
    row_total, width = unit_one.shape
    count = own.shape[0] // PIECE
    hidden_units = inner_weight.shape[1]

    def body(
        unit_ref, own_ref, other_ref, gain_one_ref, bias_one_ref, gain_ref, bias_ref, g_ref,
        slope_ref, inner_ref, outer_ref, *rest,
    ):
        out_ref, sum_ref, low_ref, pre_ref, part_ref, gain_grad_ref, bias_grad_ref = rest[
            len(into) :
        ]

        @pl.when(pl.program_id(0) == 0)
        def _():
            gain_grad_ref[...] = jnp.zeros_like(gain_grad_ref)
            bias_grad_ref[...] = jnp.zeros_like(bias_grad_ref)

        normed = unit_ref[...] * gain_one_ref[...] + bias_one_ref[...]
        unit, inverse = norm_terms(
            normed + (own_ref[...].astype(F32) + other_ref[...].astype(F32))
        )
        out_ref[...] = (unit * gain_ref[...] + bias_ref[...]).astype(BF16)
        g = g_ref[...].astype(F32)
        gain_grad_ref[...] += jnp.sum(g * unit, axis=0, keepdims=True)
        bias_grad_ref[...] += jnp.sum(g, axis=0, keepdims=True)
        grad_sum = norm_back(g * gain_ref[...], unit, inverse)
        sum_ref[...] = grad_sum
        low = grad_sum.astype(BF16)
        low_ref[...] = low
        pre = contract(low, outer_ref[...], 1, 1) * slope_ref[...].astype(F32)
        pre = pre.astype(BF16)
        pre_ref[...] = pre
        part_ref[...] = contract(pre, inner_ref[...], 1, 1).astype(BF16)

    own_rows = row_blocks(0, count, width)
    rows = row_blocks(first, count, width)
    units = row_blocks(first, count, hidden_units)
    line = pl.BlockSpec((1, width), lambda i: (0, 0))
    return pl.pallas_call(
        body,
        grid=(count,),
        in_specs=[
            rows, own_rows, own_rows, line, line, line, line, rows, units,
            pl.BlockSpec((width, hidden_units), lambda i: (0, 0)),
            pl.BlockSpec((hidden_units, width), lambda i: (0, 0)),
        ]
        + [ANYWHERE] * len(into),
        out_specs=[rows, rows, rows, units, own_rows, line, line],
        out_shape=[
            jax.ShapeDtypeStruct((row_total, width), BF16),
            jax.ShapeDtypeStruct((row_total, width), F32),
            jax.ShapeDtypeStruct((row_total, width), BF16),
            jax.ShapeDtypeStruct((row_total, hidden_units), BF16),
            jax.ShapeDtypeStruct((count * PIECE, width), BF16),
            jax.ShapeDtypeStruct((1, width), F32),
            jax.ShapeDtypeStruct((1, width), F32),
        ],
        input_output_aliases={11 + at: at for at in range(len(into))},
        compiler_params=pltpu.CompilerParams(vmem_limit_bytes=VMEM_BYTES),
        cost_estimate=lasting(3 * count),
    )(
        unit_one, own, other, gain_one, bias_one, gain_two, bias_two, cotangent, slope,
        inner_weight, outer_weight, *into,
    )


def project_back(first, unit, inverse, grad_sum, own, other, gain, out_weight, heads, into=()):
    row_total, width = unit.shape
    cols = out_weight.shape[0]
    head_dim = cols // heads
    span = ITEMS * PIECE
    count = own.shape[0] // span
    is_long = first == 0

    def body(unit_ref, inv_ref, sum_ref, own_ref, other_ref, gain_ref, w_ref, *rest):
        hidden_ref, low_ref, att_ref, gain_grad_ref, bias_grad_ref = rest[len(into) :]

        @pl.when(pl.program_id(0) == 0)
        def _():
            gain_grad_ref[...] = jnp.zeros_like(gain_grad_ref)
            bias_grad_ref[...] = jnp.zeros_like(bias_grad_ref)

        unit = unit_ref[...]
        grad = sum_ref[...] + (own_ref[...].astype(F32) + other_ref[...].astype(F32))
        gain_grad_ref[...] += jnp.sum(grad * unit, axis=0, keepdims=True)
        bias_grad_ref[...] += jnp.sum(grad, axis=0, keepdims=True)
        hidden = norm_back(grad * gain_ref[...], unit, inv_ref[...])
        hidden_ref[...] = hidden
        low = hidden.astype(BF16)
        low_ref[...] = low
        att = contract(w_ref[...], low, 1, 1).astype(BF16)
        if is_long:
            items = contract(att, place_of_item(span), 1, 1).astype(BF16)
            for h in range(heads):
                for item in range(ITEMS):
                    att_ref[item * heads + h] = items[
                        h * head_dim : (h + 1) * head_dim, item * PIECE : (item + 1) * PIECE
                    ]
            att_ref[pl.ds(ITEMS * heads, GROUP - ITEMS * heads)] = jnp.zeros(
                (GROUP - ITEMS * heads, head_dim, PIECE), BF16
            )
        else:
            att_ref[...] = att.reshape(heads, head_dim, span)

    own_rows = row_blocks(0, count, width, span)
    rows = row_blocks(first, count, width, span)
    line = pl.BlockSpec((1, width), lambda i: (0, 0))
    if is_long:
        att_spec = pl.BlockSpec((GROUP, head_dim, PIECE), lambda i: (0, 0, 0))
        att_shape = (GROUP, head_dim, PIECE)
    else:
        att_spec = pl.BlockSpec((heads, head_dim, span), lambda i: (0, 0, i))
        att_shape = (heads, head_dim, count * span)
    return pl.pallas_call(
        body,
        grid=(count,),
        in_specs=[
            rows, row_blocks(first, count, 1, span), rows, own_rows, own_rows, line,
            pl.BlockSpec((cols, width), lambda i: (0, 0)),
        ]
        + [ANYWHERE] * len(into),
        out_specs=[rows, rows, att_spec, line, line],
        out_shape=[
            jax.ShapeDtypeStruct((row_total, width), F32),
            jax.ShapeDtypeStruct((row_total, width), BF16),
            jax.ShapeDtypeStruct(att_shape, BF16),
            jax.ShapeDtypeStruct((1, width), F32),
            jax.ShapeDtypeStruct((1, width), F32),
        ],
        input_output_aliases={7 + at: at for at in range(len(into))},
        compiler_params=pltpu.CompilerParams(vmem_limit_bytes=VMEM_BYTES),
        cost_estimate=lasting(4 * count),
    )(unit, inverse, grad_sum, own, other, gain, out_weight, *into)


NORM_SLOT = 16
OUT_SLOT = 8


def first_rows(source, mine_ref, away, second, count):
    first = lax.bitwise_xor(mine_ref[0], away)
    return source[pl.ds(pl.multiple_of((first * 4 + second) * count, count), count), :]


def terms_call(body, mine, rows, columns, lines, counts, width, scratch, microseconds):
    span = ITEMS * PIECE
    shape = (4, sum(counts), width)
    return counts, pl.pallas_call(
        body,
        grid=(rows[0].shape[0] // span,),
        in_specs=[pl.BlockSpec(memory_space=pltpu.SMEM)]
        + [pl.BlockSpec((span, array.shape[1]), lambda i: (i, 0)) for array in rows]
        + [pl.BlockSpec((array.shape[0], span), lambda i: (0, i)) for array in columns]
        + [pl.BlockSpec(array.shape, lambda i: (0, 0)) for array in lines],
        out_specs=[pl.BlockSpec(shape, lambda i: (0, 0, 0))] * 4,
        out_shape=[jax.ShapeDtypeStruct(shape, BF16)] * 4,
        scratch_shapes=[pltpu.VMEM(dims, F32) for dims in scratch],
        compiler_params=pltpu.CompilerParams(vmem_limit_bytes=VMEM_BYTES),
        cost_estimate=lasting(microseconds),
    )(mine, *rows, *columns, *lines)


def outer_terms(mine, act, grad_ffn, norm_lines):
    units, width = act.shape[1], grad_ffn.shape[1]
    counts = [units // 16, NORM_SLOT]

    def body(mine_ref, act_ref, ffn_ref, norm_ref, *rest):
        outs, (outer,) = rest[:4], rest[4:]

        @pl.when(pl.program_id(0) == 0)
        def _():
            outer[...] = jnp.zeros_like(outer)

        outer[...] += contract(act_ref[...], ffn_ref[...], 0, 0)

        @pl.when(pl.program_id(0) == pl.num_programs(0) - 1)
        def _():
            slot = lax.broadcasted_iota(jnp.int32, (NORM_SLOT, width), 0) == 0
            for away, ref in enumerate(outs):
                line = norm_ref[pl.ds(lax.bitwise_xor(mine_ref[0], away), 1), :]
                for second in range(4):
                    rows = first_rows(outer, mine_ref, away, second, counts[0])
                    ref[second, pl.ds(0, counts[0]), :] = rows.astype(BF16)
                    lines = jnp.where(slot, line if second == 0 else 0.0, 0.0)
                    ref[second, pl.ds(counts[0], NORM_SLOT), :] = lines.astype(BF16)

    return terms_call(
        body, mine, [act, grad_ffn], [], [norm_lines], counts, width, [(units, width)], 9
    )


def inner_terms(mine, normed, grad_pre, mixed, grad_proj):
    units, width, cols = grad_pre.shape[1], normed.shape[1], mixed.shape[0]
    counts = [width // 16, width // 16, cols // 16, OUT_SLOT]

    def body(mine_ref, low_ref, pre_ref, proj_ref, mixed_ref, *rest):
        outs, (inner, out) = rest[:4], rest[4:]

        @pl.when(pl.program_id(0) == 0)
        def _():
            inner[...] = jnp.zeros_like(inner)
            out[...] = jnp.zeros_like(out)

        inner[...] += contract(low_ref[...], pre_ref[...], 0, 0)
        out[...] += contract(mixed_ref[...], proj_ref[...], 1, 0)

        @pl.when(pl.program_id(0) == pl.num_programs(0) - 1)
        def _():
            for away, ref in enumerate(outs):
                for second in range(4):
                    both = first_rows(inner, mine_ref, away, second, counts[0]).astype(BF16)
                    ref[second, pl.ds(0, counts[0]), :] = both[:, :width]
                    ref[second, pl.ds(counts[0], counts[1]), :] = both[:, width:]
                    tail = jnp.concatenate(
                        [
                            first_rows(out, mine_ref, away, second, counts[2]),
                            jnp.zeros((OUT_SLOT, width), F32),
                        ],
                        axis=0,
                    )
                    ref[second, pl.ds(counts[0] + counts[1], counts[2] + OUT_SLOT), :] = (
                        tail.astype(BF16)
                    )

    return terms_call(
        body, mine, [normed, grad_pre, grad_proj], [mixed], [], counts, width,
        [(width, units), (cols, width)], 9,
    )


def next_terms(part, counts, bits):
    places, at, pieces = 1 << len(bits), 0, []
    for index, count in enumerate(counts):
        pieces.append(part[at : at + count].reshape(places, -1, part.shape[1]))
        at, counts[index] = at + count, count // places
    return terms_for(jnp.concatenate(pieces, axis=1), bits)


def gathered_sums(gathered, counts, targets, shapes):
    peers = gathered.shape[0]
    width = gathered.shape[2]
    groups = bit_groups(peers)

    def body(in_ref, *outs):
        for at_place in range(peers):
            order = 0
            for bits in groups:
                size = 1 << len(bits)
                order = order * size + ((at_place >> bits[0]) & (size - 1))
            at = 0
            for count, target in zip(counts, targets):
                if target is not None:
                    index, column = target
                    rows = in_ref[at_place, pl.ds(at, count), :].astype(F32)
                    if column is not None:
                        outs[index][pl.ds(order * count, count), pl.ds(column, width)] = rows
                    elif order % (peers // 4) == 0:
                        outs[index][pl.ds(order // (peers // 4), 1), :] = rows[:1]
                at += count

    def whole(shape):
        return pl.BlockSpec(shape, lambda: (0,) * len(shape))

    return pl.pallas_call(
        body,
        in_specs=[whole(gathered.shape)],
        out_specs=[whole(shape) for shape in shapes],
        out_shape=[jax.ShapeDtypeStruct(shape, F32) for shape in shapes],
        compiler_params=pltpu.CompilerParams(vmem_limit_bytes=VMEM_BYTES),
        cost_estimate=lasting(4),
    )(gathered)


def placed_sums(mine, arrays, aways, counts, targets, shapes):
    width = arrays[0].shape[2]

    def body(mine_ref, *refs):
        ins, outs = refs[: len(arrays)], refs[len(arrays) :]
        pieces = [(ref, at, *away) for ref, pairs in zip(ins, aways) for at, away in enumerate(pairs)]
        for ref, piece, first_away, second_away in pieces:
            first = lax.bitwise_xor(mine_ref[0], first_away)
            second = lax.bitwise_xor(mine_ref[1], second_away)
            order = first * 4 + second
            at = 0
            for count, target in zip(counts, targets):
                rows = pl.ds(at, count)
                at += count
                if target is None:
                    continue
                out = outs[target[0]]
                if target[1] is not None:
                    to = pl.ds(pl.multiple_of(order * count, count), count)
                    out[to, pl.ds(target[1], width)] = ref[piece, rows, :].astype(F32)
                elif out.shape[0] > 4:
                    out[pl.ds(order, 1), :] = ref[piece, rows, :].astype(F32)[:1]
                else:

                    @pl.when(second == 0)
                    def _():
                        out[pl.ds(first, 1), :] = ref[piece, rows, :].astype(F32)[:1]

    def whole(shape):
        return pl.BlockSpec(shape, lambda: (0,) * len(shape))

    return pl.pallas_call(
        body,
        in_specs=[pl.BlockSpec(memory_space=pltpu.SMEM)] + [whole(array.shape) for array in arrays],
        out_specs=[whole(shape) for shape in shapes],
        out_shape=[jax.ShapeDtypeStruct(shape, F32) for shape in shapes],
        compiler_params=pltpu.CompilerParams(vmem_limit_bytes=VMEM_BYTES),
        cost_estimate=lasting(4),
    )(mine, *arrays)


def by_twos(steps):
    return len(steps) == 2 and all(len(bits) == 2 for bits in steps)


def across(array, mask):
    peers = lax.axis_size("seq")
    return lax.ppermute(array, "seq", [(i, i ^ mask) for i in range(peers)])


def gather_second(part, steps):
    if not by_twos(steps):
        return part
    came = [came[None] for came in terms_sent([part] * 4, steps[1])]
    return jnp.concatenate([part[None]] + came, axis=0)


def gather_near(own, steps):
    return (across(own[:2], 1), across(own[2:], 2)) if by_twos(steps) else ()


def gather_far(own, near, steps):
    if not near:
        return ()
    return (
        across(jnp.concatenate([own[:2], near[0]], axis=0), 2),
        across(jnp.concatenate([own[2:], near[1]], axis=0), 1),
    )


def placed(own, near, far, counts, targets, shapes):
    peers = lax.axis_size("seq")
    place = lax.axis_index("seq")
    if not near:
        gathered = lax.all_gather(own, "seq", axis=0)
        single = [target for target in targets if target is not None and target[1] is None]
        if not single or shapes[single[0][0]][0] == 4:
            return gathered_sums(gathered, counts, targets, shapes)
        sums = gathered_sums(gathered, counts[:-1], targets[:-1], shapes[:-1])
        return [*sums, gathered[:, sum(counts[:-1])].astype(F32)]
    mine = jnp.stack([place & 3, (place >> 2) & 3]).astype(jnp.int32)
    aways = [
        [(0, 0), (0, 1), (0, 2), (0, 3)],
        [(1, 0), (1, 1)],
        [(2, 2), (2, 3)],
        [(2, 0), (2, 1), (3, 0), (3, 1)],
        [(1, 2), (1, 3), (3, 2), (3, 3)],
    ]
    return placed_sums(mine, [own, *near, *far], aways, counts, targets, shapes)


def unit_back(moved_pairs, moved_values, short_parts, unit, inverse):
    heads, head_dim = unit.shape[1:3]
    short_heads, _, short_rows = short_parts[0][0].shape
    count = len(short_parts)
    span = ITEMS * PIECE
    blocks = 1 + short_rows // span
    cols = heads * head_dim

    def body(*refs):
        pairs_ref, values_ref = refs[:2]
        short_refs = refs[2 : 2 + 3 * count]
        unit_ref, inv_ref, out_ref, items = refs[2 + 3 * count :]
        block = pl.program_id(0)

        def short_part(which):
            return jnp.concatenate([short_refs[3 * at + which][...] for at in range(count)], axis=0)

        def back(which, grad):
            unit = unit_ref[which]
            along = jnp.sum(unit * grad, axis=1, keepdims=True)
            return ((grad - unit * along) * inv_ref[which]).astype(BF16).reshape(cols, span)

        @pl.when(block == 0)
        def _():
            def long_part(ref, at):
                part = pl.ds(at, head_dim)
                heads_of = [
                    jnp.concatenate([ref[h, part, :], ref[heads + h, part, :]], axis=1)
                    for h in range(heads)
                ]
                return jnp.stack(heads_of, axis=0)

            for which in range(2):
                items[pl.ds(which * cols, cols), :] = back(
                    which, long_part(pairs_ref, which * head_dim).astype(F32)
                )
            items[pl.ds(2 * cols, cols), :] = long_part(values_ref, 0).reshape(cols, span)
            out_ref[...] = contract(items[...], place_of_item(span), 1, 0).astype(BF16)

        @pl.when(block > 0)
        def _():
            out_ref[pl.ds(0, cols), :] = back(0, short_part(0))
            out_ref[pl.ds(cols, cols), :] = back(1, short_part(1))
            out_ref[pl.ds(2 * cols, cols), :] = short_part(2).astype(BF16).reshape(
                cols, span
            )

    short = pl.BlockSpec(
        (short_heads, head_dim, span), lambda i: (0, 0, jnp.maximum(i - 1, 0))
    )
    return pl.pallas_call(
        body,
        grid=(blocks,),
        in_specs=[
            pl.BlockSpec((GROUP, moved_pairs.shape[1], PIECE), lambda i: (0, 0, 0)),
            pl.BlockSpec((GROUP, head_dim, PIECE), lambda i: (0, 0, 0)),
        ]
        + [short] * (3 * count)
        + [
            pl.BlockSpec((2, heads, head_dim, span), lambda i: (0, 0, 0, i)),
            pl.BlockSpec((2, heads, 1, span), lambda i: (0, 0, 0, i)),
        ],
        out_specs=pl.BlockSpec((3 * cols, span), lambda i: (0, i)),
        out_shape=jax.ShapeDtypeStruct((3 * cols, span * blocks), BF16),
        scratch_shapes=[pltpu.VMEM((3 * cols, span), BF16)],
        compiler_params=pltpu.CompilerParams(vmem_limit_bytes=VMEM_BYTES),
        cost_estimate=lasting(8),
    )(moved_pairs, moved_values, *sum(map(tuple, short_parts), ()), unit, inverse)


def other_half(part):
    return lax.ppermute(part, "tp", [(0, 1), (1, 0)])


def bit_groups(peers):
    bits = peers.bit_length() - 1
    return [list(range(low, min(low + 2, bits))) for low in range(0, bits, 2)]


def terms_for(part, bits):
    mine = (lax.axis_index("seq") >> bits[0]) & ((1 << len(bits)) - 1)
    return [
        lax.dynamic_index_in_dim(part, mine ^ away, 0, False) for away in range(1 << len(bits))
    ]


def in_order(gathered, peers):
    sizes = [1 << len(bits) for bits in reversed(bit_groups(peers))]
    count = len(sizes)
    array = gathered.reshape(sizes + list(gathered.shape[1:]))
    array = jnp.transpose(array, list(range(count))[::-1] + [count, count + 1])
    return array.reshape(-1, gathered.shape[-1])


def terms_sent(terms, bits, first=1):
    peers = lax.axis_size("seq")
    terms = terms if first > 1 else terms[1:]
    return [
        lax.ppermute(term, "seq", [(i, i ^ (away << bits[0])) for i in range(peers)])
        for away, term in enumerate(terms, first)
    ]


def terms_gathered(own, bits):
    mine = (lax.axis_index("seq") >> bits[0]) & ((1 << len(bits)) - 1)
    every = jnp.stack([own] + terms_sent([own] * (1 << len(bits)), bits), axis=0)
    return jnp.stack(
        [
            lax.dynamic_index_in_dim(every, mine ^ place, 0, False)
            for place in range(1 << len(bits))
        ],
        axis=0,
    )


def terms_summed(own, came):
    total = own.astype(F32)
    for term in came:
        total = total + term.astype(F32)
    return total.astype(BF16)


def after(first, second):
    return lax.optimization_barrier((first, second))


def shards(
    tokens,
    short_lengths,
    query_weight,
    key_weight,
    value_weight,
    conv_kernel,
    out_weight,
    gain_one,
    bias_one,
    inner_weight,
    outer_weight,
    gain_two,
    bias_two,
    cotangent,
):
    row_total, width = tokens.shape
    heads_dev = conv_kernel.shape[0]
    head_cols = query_weight.shape[1]
    head_dim = head_cols // heads_dev
    short_rows = row_total - ITEMS * PIECE
    units = ITEMS * heads_dev
    place = lax.axis_index("seq") % GROUP
    groups = [
        [first + i for i in range(GROUP)] for first in range(0, lax.axis_size("seq"), GROUP)
    ]

    def exchange(pieces):
        return lax.all_to_all(pieces, "seq", 0, 0, axis_index_groups=groups)

    def by_position(moved, count):
        return jnp.transpose(moved, (1, 0, 2)).reshape(count, head_dim, GROUP * PIECE)

    item_ends = jnp.cumsum(short_lengths[0])
    positions = jnp.arange(short_rows, dtype=jnp.int32)
    item_ids = jnp.sum((positions[:, None] >= item_ends[None, :]).astype(jnp.int32), axis=1)
    ids_row = item_ids[None, :]
    ids_col = jnp.pad(item_ids, (REACH, REACH), constant_values=-1)[:, None]
    item_starts = jnp.concatenate([jnp.zeros((1,), jnp.int32), item_ends[:-1]])
    block_first = jnp.arange(0, short_rows, PIECE, dtype=jnp.int32)
    block_last = block_first + (PIECE - 1)
    inside = (item_starts[None, :] <= block_last[:, None]) & (
        item_ends[None, :] > block_first[:, None]
    )
    lowest = jnp.min(jnp.where(inside, item_starts[None, :], short_rows), axis=1)
    highest = jnp.max(jnp.where(inside, item_ends[None, :], 0), axis=1)
    reach = jnp.stack([lowest // PIECE, (highest + PIECE - 1) // PIECE]).astype(jnp.int32)

    last_tap = LINE - REACH - HALF_WIDTH
    lines = jnp.pad(
        conv_kernel[:, ::-1], ((0, 0), (last_tap, LINE - last_tap - CONV_WIDTH))
    )[:, None, :]
    unit_head = place % heads_dev
    long_line = lax.dynamic_index_in_dim(lines, unit_head, 0, False)

    long_send, short_pack, unit, inverse = project_in(
        tokens, query_weight, key_weight, value_weight, heads_dev
    )
    lines_of = [line[None, :] for line in (gain_one, bias_one, gain_two, bias_two)]
    gain_one, bias_one, gain_two, bias_two = lines_of

    long_moved = exchange(long_send)
    short_att, short_w, short_s = short_forward(reach, ids_row, ids_col, short_pack, lines)
    mixed, short_proj = project_out_short(short_att, out_weight, row_total)
    long_moved, short_proj = after(long_moved, short_proj)
    long_pack = by_position(long_moved, 3)
    long_att, long_w, long_s = long_forward(long_pack[0], long_pack[1], long_pack[2], long_line)

    long_att, short_proj = after(long_att, short_proj)
    long_att = exchange(long_att)
    *forward, short_ffn = feed_forward(
        ITEMS, tokens, short_proj, other_half(short_proj), gain_one, bias_one, inner_weight,
        outer_weight,
    )
    long_att, short_ffn = after(long_att, short_ffn)
    short_ffn_other = other_half(short_ffn)

    mixed, long_proj = project_out_long(long_att, out_weight, mixed)
    *forward, long_ffn = feed_forward(
        0, tokens, long_proj, other_half(long_proj), gain_one, bias_one, inner_weight,
        outer_weight, forward,
    )
    norm_unit, norm_inverse, normed_low, act_low, act_slope = forward
    *backward, long_back, long_gain_two, long_bias_two = feed_back(
        0, norm_unit, long_ffn, other_half(long_ffn), gain_one, bias_one, gain_two, bias_two,
        cotangent, act_slope, inner_weight, outer_weight,
    )
    grad_hidden, grad_proj_low, long_grad, long_gain_one, long_bias_one = project_back(
        0, norm_unit, norm_inverse, backward[1], long_back, other_half(long_back), gain_one,
        out_weight, heads_dev,
    )
    long_grad, backward, short_ffn, short_ffn_other = lax.optimization_barrier(
        (long_grad, backward, short_ffn, short_ffn_other)
    )
    long_grad = exchange(long_grad)
    *backward, short_back, short_gain_two, short_bias_two = feed_back(
        ITEMS, norm_unit, short_ffn, short_ffn_other, gain_one, bias_one, gain_two, bias_two,
        cotangent, act_slope, inner_weight, outer_weight, backward,
    )
    output, grad_sum, grad_ffn_low, grad_pre_low = backward
    grad_hidden, grad_proj_low, short_grad, short_gain_one, short_bias_one = project_back(
        1, norm_unit, norm_inverse, grad_sum, short_back, other_half(short_back), gain_one,
        out_weight, heads_dev, (grad_hidden, grad_proj_low),
    )
    norm_lines = jnp.concatenate(
        [
            long_gain_one + short_gain_one,
            long_bias_one + short_bias_one,
            long_gain_two + short_gain_two,
            long_bias_two + short_bias_two,
        ],
        axis=0,
    )

    peers = lax.axis_size("seq")
    steps = bit_groups(peers)
    mine = (lax.axis_index("seq") & 3).astype(jnp.int32)[None]
    outer_counts, outer_terms_now = outer_terms(mine, act_low, grad_ffn_low, norm_lines)
    outer_terms_now, grad_pre_low = after(outer_terms_now, grad_pre_low)
    outer_came = terms_sent(outer_terms_now, steps[0])
    inner_counts, inner_terms_now = inner_terms(
        mine, normed_low, grad_pre_low, mixed, grad_proj_low
    )
    inner_terms_now, long_grad = after(inner_terms_now, long_grad)
    long_grad = by_position(long_grad, 1)[0]
    long_dv, long_taps = long_back_values(long_pack[2], long_grad, long_w)
    outer_came, own, inner_terms_now, long_dv, long_grad = lax.optimization_barrier(
        (outer_came, outer_terms_now[0], inner_terms_now, long_dv, long_grad)
    )
    outer_part = terms_summed(own, outer_came)
    inner_came = terms_sent(inner_terms_now, steps[0])
    outer_terms_now, long_dv, long_grad = lax.optimization_barrier(
        (terms_for(outer_part, steps[1]), long_dv, long_grad)
    )
    outer_came = terms_sent(outer_terms_now, steps[1])
    long_dv = exchange(long_dv)
    long_dq, long_dk = long_back_pairs(
        long_pack[0], long_pack[1], long_pack[2], long_grad, long_s
    )
    outer_came, outer_own, inner_came, inner_own, long_dv, long_dq, long_dk, short_grad = (
        lax.optimization_barrier(
            (
                outer_came, outer_terms_now[0], inner_came, inner_terms_now[0], long_dv, long_dq,
                long_dk, short_grad,
            )
        )
    )
    outer_part = terms_summed(outer_own, outer_came)
    for bits in steps[2:]:
        terms = next_terms(outer_part, outer_counts, bits)
        outer_part = terms_summed(terms[0], terms_sent(terms, bits))
    inner_part = terms_summed(inner_own, inner_came)
    long_back = jnp.concatenate([long_dq, long_dk], axis=1)
    inner_terms_now, outer_part, long_back, short_grad = lax.optimization_barrier(
        (terms_for(inner_part, steps[1]), outer_part, long_back, short_grad)
    )
    outer_own = gather_second(outer_part, steps)
    long_back = exchange(long_back)
    inner_came = terms_sent(inner_terms_now, steps[1])
    outer_own, short_grad = after(outer_own, short_grad)
    outer_near = gather_near(outer_own, steps)
    *short_parts, short_taps = short_backward(
        reach, ids_row, ids_col, short_pack, short_grad, short_w, short_s
    )
    long_back, short_parts, short_taps, outer_own, outer_near = lax.optimization_barrier(
        (long_back, short_parts, short_taps, outer_own, outer_near)
    )
    outer_far = gather_far(outer_own, outer_near, steps)
    grads_low = unit_back(long_back, long_dv, [short_parts], unit, inverse)
    own, grads_low, outer_far = lax.optimization_barrier(
        (inner_terms_now[0], grads_low, outer_far)
    )
    inner_part = terms_summed(own, inner_came)
    for bits in steps[2:]:
        terms = next_terms(inner_part, inner_counts, bits)
        inner_part = terms_summed(terms[0], terms_sent(terms, bits))

    first_tap = BAND_ROWS - 1 - REACH + HALF_WIDTH
    taps = slice(first_tap, first_tap - CONV_WIDTH, -1)
    owner = (jnp.arange(heads_dev) == unit_head) & (place < units)
    kernel_part = short_taps[:, 0, taps] + jnp.where(owner[:, None], long_taps[:, taps], 0.0)
    taps_line = kernel_part.reshape(1, -1)
    taps_line = jnp.pad(taps_line, ((0, 15), (0, width - taps_line.shape[1]))).astype(BF16)
    outer_sum, norm_sums = placed(
        outer_own, outer_near, outer_far, outer_counts, [(0, 0), (1, None)],
        [outer_weight.shape, (4, width)],
    )
    inner_own = gather_second(jnp.concatenate([inner_part, taps_line], axis=0), steps)
    inner_near = gather_near(inner_own, steps)
    inner_far = gather_far(inner_own, inner_near, steps)

    weight_part = contract(tokens, grads_low, 0, 1).astype(BF16)
    terms = terms_for(weight_part.reshape(1 << len(steps[0]), -1, 3 * head_cols), steps[0])
    terms, grads_low = after(terms, grads_low)
    came = terms_sent(terms, steps[0])
    weight_all = jnp.concatenate([query_weight, key_weight, value_weight], axis=1)
    token_own = contract(grads_low, weight_all, 0, 1).astype(BF16)
    own, token_own = after(terms[0], token_own)
    weight_part = terms_summed(own, came)
    for bits in steps[1:]:
        terms = terms_for(weight_part.reshape(1 << len(bits), -1, 3 * head_cols), bits)
        weight_part = terms_summed(terms[0], terms_sent(terms, bits))
    for bits in reversed(steps):
        weight_part = terms_gathered(weight_part, bits).reshape(-1, 3 * head_cols)
    weight_sum = weight_part.astype(F32)
    token_grad = grad_hidden + (token_own.astype(F32) + other_half(token_own).astype(F32))
    inner_sum, out_sum, tap_lines = placed(
        inner_own, inner_near, inner_far, inner_counts + [16],
        [(0, 0), (0, width), (1, 0), None, (2, None)],
        [inner_weight.shape, out_weight.shape, (peers, width)],
    )
    kernel_sum = jnp.sum(tap_lines[:, : heads_dev * CONV_WIDTH], axis=0).reshape(
        heads_dev, CONV_WIDTH
    )
    return (
        output,
        token_grad,
        weight_sum[:, :head_cols],
        weight_sum[:, head_cols : 2 * head_cols],
        weight_sum[:, 2 * head_cols :],
        kernel_sum,
        out_sum,
        norm_sums[0],
        norm_sums[1],
        inner_sum,
        outer_sum,
        norm_sums[2],
        norm_sums[3],
    )


def solution(mesh):
    rows = P("seq", None)
    columns = P(None, "tp")
    split_rows = P("tp", None)
    return jax.shard_map(
        shards,
        mesh=mesh,
        in_specs=(
            rows, rows, columns, columns, columns, split_rows, split_rows,
            P(), P(), columns, split_rows, P(), P(), rows,
        ),
        out_specs=(
            rows, rows, columns, columns, columns, split_rows, split_rows,
            P(), P(), columns, split_rows, P(), P(),
        ),
        check_vma=False,
    )
```

```python
import math

import jax
import jax.numpy as jnp
from jax import lax
from jax.experimental import pallas as pl
from jax.experimental.pallas import tpu as pltpu
from jax.sharding import PartitionSpec as P

TAU = 8
CONV_WIDTH = 33
HALF_WIDTH = 16
GROUP = 16
PIECE = 256
ITEMS = 2
REACH = 32
BAND_ROWS = PIECE + 2 * REACH
LINE = 640

COS_SCALE = 0.98
EPS_UNIT = 1e-06
EPS_NORM = 1e-05
NEAR_POLY = (1.158024787902832, -0.36302468180656433, 0.09245320409536362, -0.011449637822806835)
TAIL_POLY = tuple(
    0.5 * a for a in (0.254829592, -0.284496736, 1.421413741, -1.453152027, 1.061405429)
)
SLOPE_SCALE = TAU / math.pi
VMEM_BYTES = 60 * 2**20

F32 = jnp.float32
BF16 = jnp.bfloat16


def norm_terms(values):
    centered = values - jnp.mean(values, axis=-1, keepdims=True)
    inverse = lax.rsqrt(jnp.mean(centered * centered, axis=-1, keepdims=True) + EPS_NORM)
    return centered * inverse, inverse


def norm_back(scaled, unit, inverse):
    along = jnp.mean(scaled * unit, axis=-1, keepdims=True)
    return inverse * (scaled - jnp.mean(scaled, axis=-1, keepdims=True) - unit * along)


def gelu_terms(values):
    share = 1.0 / (1.0 + (0.3275911 * math.sqrt(0.5)) * jnp.abs(values))
    bell = jnp.exp(-0.5 * (values * values))
    poly = TAIL_POLY[4] * share + TAIL_POLY[3]
    for coefficient in TAIL_POLY[2::-1]:
        poly = poly * share + coefficient
    tail = poly * (share * bell)
    below = jnp.where(values < 0.0, tail, 1.0 - tail)
    return values * below, below + values * (bell * (1.0 / math.sqrt(2.0 * math.pi)))


def place_of_item(rows):
    item_at = lax.broadcasted_iota(jnp.int32, (rows, rows), 0)
    place_at = lax.broadcasted_iota(jnp.int32, (rows, rows), 1)
    hit = item_at == (place_at & 1) * PIECE + (place_at >> 1)
    return jnp.where(hit, 1.0, 0.0).astype(BF16)


def lasting(microseconds):
    return pl.CostEstimate(flops=microseconds * 1_150_000_000, bytes_accessed=0, transcendentals=0)


def contract(left, right, left_dim, right_dim):
    return lax.dot_general(
        left, right, (((left_dim,), (right_dim,)), ((), ())), preferred_element_type=F32
    )


def pair_terms(dots, same=None):
    upper = 1.0 / COS_SCALE + dots
    lower = 1.0 / COS_SCALE - dots
    upper_inv = lax.rsqrt(upper)
    lower_inv = lax.rsqrt(lower)
    wide = 1.0 / 0.7 + lower * lower_inv
    wide_inv = lax.rsqrt(wide)
    root = wide * wide_inv
    ratio = NEAR_POLY[3] * root + NEAR_POLY[2]
    ratio = ratio * root + NEAR_POLY[1]
    ratio = ratio * root + NEAR_POLY[0]
    near = ratio * ((upper * upper_inv) * wide_inv)
    if same is not None:
        near = jnp.where(same, near, 0.0)
    near_2 = near * near
    near_4 = near_2 * near_2
    weights = (near_4 * near_4).astype(BF16)
    slopes = ((near_4 * near_2) * (near * (upper_inv * lower_inv))).astype(BF16)
    return weights, slopes


def banded(line):
    wide = jnp.broadcast_to(line, (BAND_ROWS, line.shape[1]))
    return pltpu.roll(wide, 0, 1, stride=1, stride_axis=0)[:, :PIECE].astype(BF16)


def unbanded(products):
    rows_at = lax.broadcasted_iota(jnp.int32, (BAND_ROWS, BAND_ROWS), 0)
    rows_to = lax.broadcasted_iota(jnp.int32, (BAND_ROWS, BAND_ROWS), 1)
    flip = jnp.where(rows_at + rows_to == BAND_ROWS - 1, 1.0, 0.0)
    flipped = lax.dot_general(
        flip, products, (((1,), (0,)), ((), ())), precision=lax.Precision.HIGHEST,
        preferred_element_type=F32,
    )
    wide = jnp.concatenate([flipped, jnp.zeros((BAND_ROWS, LINE - PIECE), F32)], axis=1)
    return jnp.sum(pltpu.roll(wide, 0, 1, stride=1, stride_axis=0), axis=0, keepdims=True)


def padded_rows(dst, src, length):
    edge = jnp.zeros((REACH, dst.shape[1]), dst.dtype)
    dst[pl.ds(0, REACH), :] = edge
    dst[pl.ds(REACH + length, REACH), :] = edge
    for start in range(0, length, PIECE):
        dst[pl.ds(REACH + start, PIECE), :] = src[:, pl.ds(start, PIECE)].T


def rows_of(dst, src, length):
    for start in range(0, length, PIECE):
        dst[pl.ds(start, PIECE), :] = src[:, pl.ds(start, PIECE)].T


def long_forward(query, key, value, line):
    head_dim, length = query.shape
    blocks = length // PIECE
    step = 512

    def body(q_ref, k_ref, v_ref, line_ref, o_ref, w_ref, s_ref, key_rows, taps):
        block = pl.program_id(0)

        @pl.when(block == 0)
        def _():
            rows_of(key_rows, k_ref, length)
            taps[...] = jnp.zeros_like(taps)
            taps[pl.ds(length - REACH, BAND_ROWS), :] = banded(line_ref[...])

        q = q_ref[...]
        start = block * PIECE
        total = jnp.zeros((head_dim, PIECE), F32)
        for at in range(0, length, step):
            dots = contract(key_rows[pl.ds(at, step), :], q, 1, 0)
            weights, slopes = pair_terms(dots)
            near = pl.multiple_of(length + at - start, PIECE)
            weights = weights + taps[pl.ds(near, step), :]
            w_ref[pl.ds(at, step), :] = weights
            s_ref[pl.ds(at, step), :] = slopes
            total = total + contract(v_ref[:, pl.ds(at, step)], weights, 1, 0)
        o_ref[...] = total.astype(BF16)

    whole = pl.BlockSpec((head_dim, length), lambda i: (0, 0))
    large = pl.BlockSpec((None, length, PIECE), lambda i: (i, 0, 0))
    large_shape = jax.ShapeDtypeStruct((blocks, length, PIECE), BF16)
    return pl.pallas_call(
        body,
        grid=(blocks,),
        in_specs=[
            pl.BlockSpec((head_dim, PIECE), lambda i: (0, i)),
            whole,
            whole,
            pl.BlockSpec((1, LINE), lambda i: (0, 0)),
        ],
        out_specs=[pl.BlockSpec((None, head_dim, PIECE), lambda i: (i, 0, 0)), large, large],
        out_shape=[jax.ShapeDtypeStruct((blocks, head_dim, PIECE), BF16), large_shape, large_shape],
        scratch_shapes=[
            pltpu.VMEM((length, head_dim), BF16),
            pltpu.VMEM((2 * length, PIECE), BF16),
        ],
        compiler_params=pltpu.CompilerParams(vmem_limit_bytes=VMEM_BYTES),
        cost_estimate=lasting(70),
    )(query, key, value, line)


def long_back_values(value, grad, weights):
    head_dim, length = grad.shape
    blocks = length // PIECE
    step = 1024

    def body(v_ref, g_ref, w_ref, dv_ref, taps_ref, value_sum, value_rows, products):
        block = pl.program_id(0)

        @pl.when(block == 0)
        def _():
            padded_rows(value_rows, v_ref, length)
            value_sum[...] = jnp.zeros_like(value_sum)
            products[...] = jnp.zeros_like(products)

        g = g_ref[...]
        start = pl.multiple_of(block * PIECE, PIECE)
        products[...] += contract(value_rows[pl.ds(start, BAND_ROWS), :], g, 1, 0)
        for at in range(0, length, step):
            value_sum[:, pl.ds(at, step)] += contract(g, w_ref[pl.ds(at, step), :], 1, 1)

        @pl.when(block == blocks - 1)
        def _():
            for index in range(blocks):
                dv_ref[index] = value_sum[:, pl.ds(index * PIECE, PIECE)].astype(BF16)
            taps_ref[...] = unbanded(products[...])

    return pl.pallas_call(
        body,
        grid=(blocks,),
        in_specs=[
            pl.BlockSpec((head_dim, length), lambda i: (0, 0)),
            pl.BlockSpec((head_dim, PIECE), lambda i: (0, i)),
            pl.BlockSpec((None, length, PIECE), lambda i: (i, 0, 0)),
        ],
        out_specs=[
            pl.BlockSpec((blocks, head_dim, PIECE), lambda i: (0, 0, 0)),
            pl.BlockSpec((1, LINE), lambda i: (0, 0)),
        ],
        out_shape=[
            jax.ShapeDtypeStruct((blocks, head_dim, PIECE), BF16),
            jax.ShapeDtypeStruct((1, LINE), F32),
        ],
        scratch_shapes=[
            pltpu.VMEM((head_dim, length), F32),
            pltpu.VMEM((length + 2 * REACH, head_dim), BF16),
            pltpu.VMEM((BAND_ROWS, PIECE), F32),
        ],
        compiler_params=pltpu.CompilerParams(vmem_limit_bytes=VMEM_BYTES),
        cost_estimate=lasting(1),
    )(value, grad, weights)


def long_back_pairs(query, key, value, grad, slopes):
    head_dim, length = query.shape
    blocks = length // PIECE
    step = 1024

    def body(q_ref, k_ref, v_ref, g_ref, s_ref, dq_ref, dk_ref, value_rows, key_sum):
        block = pl.program_id(0)

        @pl.when(block == 0)
        def _():
            rows_of(value_rows, v_ref, length)
            key_sum[...] = jnp.zeros_like(key_sum)

        q = q_ref[...]
        g = g_ref[...]
        total = jnp.zeros((head_dim, PIECE), F32)
        for at in range(0, length, step):
            grad_weights = contract(value_rows[pl.ds(at, step), :], g, 1, 0)
            terms = grad_weights.astype(BF16) * s_ref[pl.ds(at, step), :]
            total = total + contract(k_ref[:, pl.ds(at, step)], terms, 1, 0)
            key_sum[:, pl.ds(at, step)] += contract(q, terms, 1, 1)
        dq_ref[...] = (total * SLOPE_SCALE).astype(BF16)

        @pl.when(block == blocks - 1)
        def _():
            for index in range(blocks):
                piece = key_sum[:, pl.ds(index * PIECE, PIECE)]
                dk_ref[index] = (piece * SLOPE_SCALE).astype(BF16)

    whole = pl.BlockSpec((head_dim, length), lambda i: (0, 0))
    piece = pl.BlockSpec((head_dim, PIECE), lambda i: (0, i))
    pieces_shape = jax.ShapeDtypeStruct((blocks, head_dim, PIECE), BF16)
    return pl.pallas_call(
        body,
        grid=(blocks,),
        in_specs=[
            piece,
            whole,
            whole,
            piece,
            pl.BlockSpec((None, length, PIECE), lambda i: (i, 0, 0)),
        ],
        out_specs=[
            pl.BlockSpec((None, head_dim, PIECE), lambda i: (i, 0, 0)),
            pl.BlockSpec((blocks, head_dim, PIECE), lambda i: (0, 0, 0)),
        ],
        out_shape=[pieces_shape] * 2,
        scratch_shapes=[
            pltpu.VMEM((length, head_dim), BF16),
            pltpu.VMEM((head_dim, length), F32),
        ],
        compiler_params=pltpu.CompilerParams(vmem_limit_bytes=VMEM_BYTES),
        cost_estimate=lasting(40),
    )(query, key, value, grad, slopes)


def short_forward(reach, ids_row, ids_col, pack, lines):
    _, heads, head_dim, length = pack.shape
    blocks = length // PIECE

    def body(
        reach_ref, row_ref, col_ref, q_ref, k_ref, v_ref, line_ref,
        o_ref, w_ref, s_ref, key_rows, total, taps,
    ):
        block = pl.program_id(0)

        @pl.when(block == 0)
        def _():
            taps[...] = jnp.zeros_like(taps)
            for h in range(heads):
                rows_of(key_rows.at[h], k_ref.at[h], length)
                taps[h, pl.ds(length - REACH, BAND_ROWS), :] = banded(line_ref[h])

        total[...] = jnp.zeros_like(total)
        own_ids = row_ref[...]

        def turn(step, carry):
            at = pl.multiple_of(step * PIECE, PIECE)
            same = col_ref[pl.ds(REACH + at, PIECE), :] == own_ids
            same_low = same.astype(F32).astype(BF16)
            near = pl.multiple_of(length + at - block * PIECE, PIECE)
            for h in range(heads):
                dots = contract(key_rows[h, pl.ds(at, PIECE), :], q_ref[h], 1, 0)
                weights, slopes = pair_terms(dots, same)
                weights = weights + taps[h, pl.ds(near, PIECE), :] * same_low
                w_ref[h, pl.ds(at, PIECE), :] = weights
                s_ref[h, pl.ds(at, PIECE), :] = slopes
                total[h] += contract(v_ref[h, :, pl.ds(at, PIECE)], weights, 1, 0)
            return carry

        lax.fori_loop(reach_ref[0, block], reach_ref[1, block], turn, 0)
        o_ref[...] = total[...].astype(BF16)

    def packed(which):
        return pl.BlockSpec((None, heads, head_dim, length), lambda i: (which, 0, 0, 0))

    block_spec = pl.BlockSpec((heads, head_dim, PIECE), lambda i: (0, 0, i))
    large = pl.BlockSpec((None, heads, length, PIECE), lambda i: (i, 0, 0, 0))
    large_shape = jax.ShapeDtypeStruct((blocks, heads, length, PIECE), BF16)
    return pl.pallas_call(
        body,
        grid=(blocks,),
        in_specs=[
            pl.BlockSpec(memory_space=pltpu.SMEM),
            pl.BlockSpec((1, PIECE), lambda i: (0, i)),
            pl.BlockSpec(ids_col.shape, lambda i: (0, 0)),
            pl.BlockSpec((None, heads, head_dim, PIECE), lambda i: (0, 0, 0, i)),
            packed(1),
            packed(2),
            pl.BlockSpec((heads, 1, LINE), lambda i: (0, 0, 0)),
        ],
        out_specs=[block_spec, large, large],
        out_shape=[jax.ShapeDtypeStruct((heads, head_dim, length), BF16), large_shape, large_shape],
        scratch_shapes=[
            pltpu.VMEM((heads, length, head_dim), BF16),
            pltpu.VMEM((heads, head_dim, PIECE), F32),
            pltpu.VMEM((heads, 2 * length, PIECE), BF16),
        ],
        compiler_params=pltpu.CompilerParams(vmem_limit_bytes=VMEM_BYTES),
        cost_estimate=lasting(28),
    )(reach, ids_row, ids_col, pack, pack, pack, lines)


def short_backward(reach, ids_row, ids_col, pack, grad, weights, slopes):
    _, heads, head_dim, length = pack.shape
    blocks = length // PIECE

    def body(
        reach_ref, row_ref, col_ref, q_ref, k_ref, v_ref, g_ref, w_ref, s_ref,
        dq_ref, dk_ref, dv_ref, taps_ref, value_rows, products,
    ):
        block = pl.program_id(0)

        @pl.when(block == 0)
        def _():
            for h in range(heads):
                padded_rows(value_rows.at[h], v_ref.at[h], length)
            dk_ref[...] = jnp.zeros_like(dk_ref)
            dv_ref[...] = jnp.zeros_like(dv_ref)
            products[...] = jnp.zeros_like(products)

        start = pl.multiple_of(block * PIECE, PIECE)
        near = (col_ref[pl.ds(start, BAND_ROWS), :] == row_ref[...]).astype(F32)
        for h in range(heads):
            products[h] += (
                contract(value_rows[h, pl.ds(start, BAND_ROWS), :], g_ref[h], 1, 0) * near
            )
        dq_ref[...] = jnp.zeros_like(dq_ref)

        def turn(step, carry):
            at = pl.multiple_of(step * PIECE, PIECE)
            for h in range(heads):
                own = g_ref[h]
                grad_weights = contract(value_rows[h, pl.ds(REACH + at, PIECE), :], own, 1, 0)
                terms = grad_weights.astype(BF16) * s_ref[h, pl.ds(at, PIECE), :]
                dq_ref[h] += contract(k_ref[h, :, pl.ds(at, PIECE)], terms, 1, 0) * SLOPE_SCALE
                dk_ref[h, :, pl.ds(at, PIECE)] += contract(q_ref[h], terms, 1, 1) * SLOPE_SCALE
                dv_ref[h, :, pl.ds(at, PIECE)] += contract(own, w_ref[h, pl.ds(at, PIECE), :], 1, 1)
            return carry

        lax.fori_loop(reach_ref[0, block], reach_ref[1, block], turn, 0)

        @pl.when(block == blocks - 1)
        def _():
            for h in range(heads):
                taps_ref[h] = unbanded(products[h])

    def packed(which):
        return pl.BlockSpec((None, heads, head_dim, length), lambda i: (which, 0, 0, 0))

    block_spec = pl.BlockSpec((heads, head_dim, PIECE), lambda i: (0, 0, i))
    whole = pl.BlockSpec((heads, head_dim, length), lambda i: (0, 0, 0))
    large = pl.BlockSpec((None, heads, length, PIECE), lambda i: (i, 0, 0, 0))
    whole_shape = jax.ShapeDtypeStruct((heads, head_dim, length), F32)
    return pl.pallas_call(
        body,
        grid=(blocks,),
        in_specs=[
            pl.BlockSpec(memory_space=pltpu.SMEM),
            pl.BlockSpec((1, PIECE), lambda i: (0, i)),
            pl.BlockSpec(ids_col.shape, lambda i: (0, 0)),
            pl.BlockSpec((None, heads, head_dim, PIECE), lambda i: (0, 0, 0, i)),
            packed(1),
            packed(2),
            block_spec,
            large,
            large,
        ],
        out_specs=[block_spec, whole, whole, pl.BlockSpec((heads, 1, LINE), lambda i: (0, 0, 0))],
        out_shape=[whole_shape] * 3 + [jax.ShapeDtypeStruct((heads, 1, LINE), F32)],
        scratch_shapes=[
            pltpu.VMEM((heads, length + 2 * REACH, head_dim), BF16),
            pltpu.VMEM((heads, BAND_ROWS, PIECE), F32),
        ],
        compiler_params=pltpu.CompilerParams(vmem_limit_bytes=VMEM_BYTES),
        cost_estimate=lasting(28),
    )(reach, ids_row, ids_col, pack, pack, pack, grad, weights, slopes)


def project_in(tokens, query_weight, key_weight, value_weight, heads):
    row_total, width = tokens.shape
    cols = query_weight.shape[1]
    head_dim = cols // heads
    blocks = row_total // PIECE
    long_rows = ITEMS * PIECE

    def body(t_ref, wq_ref, wk_ref, wv_ref, long_ref, short_ref, unit_ref, inv_ref, turned, rows):
        block = pl.program_id(0)

        @pl.when(block == 0)
        def _():
            for index, ref in enumerate((wq_ref, wk_ref, wv_ref)):
                turned[pl.ds(index * cols, cols), :] = ref[...].T
            long_ref[pl.ds(ITEMS * heads, GROUP - ITEMS * heads)] = jnp.zeros(
                (GROUP - ITEMS * heads, 3 * head_dim, PIECE), BF16
            )

        @pl.when(block < ITEMS)
        def _():
            item_at = lax.broadcasted_iota(jnp.int32, (PIECE, long_rows), 0)
            place_at = lax.broadcasted_iota(jnp.int32, (PIECE, long_rows), 1)
            pick = jnp.where(place_at == ITEMS * item_at + block, 1.0, 0.0).astype(BF16)
            rows[...] = contract(pick, t_ref[pl.ds(0, long_rows), :], 1, 0).astype(BF16)

        @pl.when(block >= ITEMS)
        def _():
            rows[...] = t_ref[pl.ds(pl.multiple_of(block * PIECE, PIECE), PIECE), :]

        parts = contract(turned[...], rows[...], 1, 1).reshape(3, heads, head_dim, PIECE)
        raw = parts[:2]
        inverse = lax.rsqrt(jnp.sum(raw * raw, axis=2, keepdims=True) + EPS_UNIT)
        unit = raw * inverse
        unit_ref[...] = unit
        inv_ref[...] = inverse
        low = unit.astype(BF16)
        short_ref[:2] = low
        short_ref[2] = parts[2].astype(BF16)

        @pl.when(block < ITEMS)
        def _():
            for h in range(heads):
                unit_at = block * heads + h
                long_ref[unit_at, pl.ds(0, head_dim), :] = low[0, h]
                long_ref[unit_at, pl.ds(head_dim, head_dim), :] = low[1, h]
                long_ref[unit_at, pl.ds(2 * head_dim, head_dim), :] = parts[2, h].astype(BF16)

    weight = pl.BlockSpec((width, cols), lambda i: (0, 0))
    return pl.pallas_call(
        body,
        grid=(blocks,),
        in_specs=[pl.BlockSpec((row_total, width), lambda i: (0, 0)), weight, weight, weight],
        out_specs=[
            pl.BlockSpec((GROUP, 3 * head_dim, PIECE), lambda i: (0, 0, 0)),
            pl.BlockSpec(
                (3, heads, head_dim, PIECE), lambda i: (0, 0, 0, jnp.maximum(i - ITEMS, 0))
            ),
            pl.BlockSpec((2, heads, head_dim, PIECE), lambda i: (0, 0, 0, i)),
            pl.BlockSpec((2, heads, 1, PIECE), lambda i: (0, 0, 0, i)),
        ],
        out_shape=[
            jax.ShapeDtypeStruct((GROUP, 3 * head_dim, PIECE), BF16),
            jax.ShapeDtypeStruct((3, heads, head_dim, row_total - long_rows), BF16),
            jax.ShapeDtypeStruct((2, heads, head_dim, row_total), F32),
            jax.ShapeDtypeStruct((2, heads, 1, row_total), F32),
        ],
        scratch_shapes=[pltpu.VMEM((3 * cols, width), BF16), pltpu.VMEM((PIECE, width), BF16)],
        compiler_params=pltpu.CompilerParams(vmem_limit_bytes=VMEM_BYTES),
        cost_estimate=lasting(10),
    )(tokens, query_weight, key_weight, value_weight)


def row_blocks(first, count, cols, span=PIECE):
    return pl.BlockSpec((span, cols), lambda i: (i + first, 0))


ANYWHERE = pl.BlockSpec(memory_space=pl.ANY)


def project_out_short(short_att, out_weight, row_total):
    heads, head_dim, short_rows = short_att.shape
    cols, width = out_weight.shape
    span = ITEMS * PIECE

    def body(a_ref, w_ref, mixed_ref, part_ref):
        mixed = a_ref[...].reshape(cols, span)
        mixed_ref[...] = mixed
        part_ref[...] = contract(mixed, w_ref[...], 0, 0).astype(BF16)

    return pl.pallas_call(
        body,
        grid=(short_rows // span,),
        in_specs=[
            pl.BlockSpec((heads, head_dim, span), lambda i: (0, 0, i)),
            pl.BlockSpec((cols, width), lambda i: (0, 0)),
        ],
        out_specs=[
            pl.BlockSpec((cols, span), lambda i: (0, i + 1)),
            pl.BlockSpec((span, width), lambda i: (i, 0)),
        ],
        out_shape=[
            jax.ShapeDtypeStruct((cols, row_total), BF16),
            jax.ShapeDtypeStruct((short_rows, width), BF16),
        ],
        compiler_params=pltpu.CompilerParams(vmem_limit_bytes=VMEM_BYTES),
        cost_estimate=lasting(4),
    )(short_att, out_weight)


def project_out_long(moved, out_weight, mixed):
    cols, width = out_weight.shape
    head_dim = moved.shape[1]
    heads = cols // head_dim
    span = ITEMS * PIECE

    def body(m_ref, w_ref, old_ref, mixed_ref, part_ref, items):
        for h in range(heads):
            for item in range(ITEMS):
                items[pl.ds(h * head_dim, head_dim), pl.ds(item * PIECE, PIECE)] = m_ref[
                    item * heads + h
                ]
        placed = contract(items[...], place_of_item(span), 1, 0).astype(BF16)
        mixed_ref[...] = placed
        part_ref[...] = contract(placed, w_ref[...], 0, 0).astype(BF16)

    return pl.pallas_call(
        body,
        grid=(1,),
        in_specs=[
            pl.BlockSpec((GROUP, head_dim, PIECE), lambda i: (0, 0, 0)),
            pl.BlockSpec((cols, width), lambda i: (0, 0)),
            ANYWHERE,
        ],
        out_specs=[
            pl.BlockSpec((cols, span), lambda i: (0, 0)),
            pl.BlockSpec((span, width), lambda i: (0, 0)),
        ],
        out_shape=[
            jax.ShapeDtypeStruct(mixed.shape, BF16),
            jax.ShapeDtypeStruct((span, width), BF16),
        ],
        scratch_shapes=[pltpu.VMEM((cols, span), BF16)],
        input_output_aliases={2: 0},
        compiler_params=pltpu.CompilerParams(vmem_limit_bytes=VMEM_BYTES),
        cost_estimate=lasting(3),
    )(moved, out_weight, mixed)


def feed_forward(first, tokens, own, other, gain, bias, inner_weight, outer_weight, into=()):
    row_total, width = tokens.shape
    count = own.shape[0] // PIECE
    hidden_units = inner_weight.shape[1]

    def body(t_ref, own_ref, other_ref, gain_ref, bias_ref, inner_ref, outer_ref, *rest):
        unit_ref, inv_ref, low_ref, act_ref, slope_ref, part_ref = rest[len(into) :]
        hidden = t_ref[...].astype(F32) + (
            own_ref[...].astype(F32) + other_ref[...].astype(F32)
        )
        unit, inverse = norm_terms(hidden)
        unit_ref[...] = unit
        inv_ref[...] = inverse
        low = (unit * gain_ref[...] + bias_ref[...]).astype(BF16)
        low_ref[...] = low
        act, slope = gelu_terms(contract(low, inner_ref[...], 1, 0))
        act = act.astype(BF16)
        act_ref[...] = act
        slope_ref[...] = slope.astype(BF16)
        part_ref[...] = contract(act, outer_ref[...], 1, 0).astype(BF16)

    own_rows = row_blocks(0, count, width)
    rows = row_blocks(first, count, width)
    units = row_blocks(first, count, hidden_units)
    line = pl.BlockSpec((1, width), lambda i: (0, 0))
    return pl.pallas_call(
        body,
        grid=(count,),
        in_specs=[
            rows, own_rows, own_rows, line, line,
            pl.BlockSpec((width, hidden_units), lambda i: (0, 0)),
            pl.BlockSpec((hidden_units, width), lambda i: (0, 0)),
        ]
        + [ANYWHERE] * len(into),
        out_specs=[rows, row_blocks(first, count, 1), rows, units, units, own_rows],
        out_shape=[
            jax.ShapeDtypeStruct((row_total, width), F32),
            jax.ShapeDtypeStruct((row_total, 1), F32),
            jax.ShapeDtypeStruct((row_total, width), BF16),
            jax.ShapeDtypeStruct((row_total, hidden_units), BF16),
            jax.ShapeDtypeStruct((row_total, hidden_units), BF16),
            jax.ShapeDtypeStruct((count * PIECE, width), BF16),
        ],
        input_output_aliases={7 + at: at for at in range(len(into))},
        compiler_params=pltpu.CompilerParams(vmem_limit_bytes=VMEM_BYTES),
        cost_estimate=lasting(3 * count),
    )(tokens, own, other, gain, bias, inner_weight, outer_weight, *into)


def feed_back(
    first, unit_one, own, other, gain_one, bias_one, gain_two, bias_two, cotangent, slope,
    inner_weight, outer_weight, into=(),
):
    row_total, width = unit_one.shape
    count = own.shape[0] // PIECE
    hidden_units = inner_weight.shape[1]

    def body(
        unit_ref, own_ref, other_ref, gain_one_ref, bias_one_ref, gain_ref, bias_ref, g_ref,
        slope_ref, inner_ref, outer_ref, *rest,
    ):
        out_ref, sum_ref, low_ref, pre_ref, part_ref, gain_grad_ref, bias_grad_ref = rest[
            len(into) :
        ]

        @pl.when(pl.program_id(0) == 0)
        def _():
            gain_grad_ref[...] = jnp.zeros_like(gain_grad_ref)
            bias_grad_ref[...] = jnp.zeros_like(bias_grad_ref)

        normed = unit_ref[...] * gain_one_ref[...] + bias_one_ref[...]
        unit, inverse = norm_terms(
            normed + (own_ref[...].astype(F32) + other_ref[...].astype(F32))
        )
        out_ref[...] = (unit * gain_ref[...] + bias_ref[...]).astype(BF16)
        g = g_ref[...].astype(F32)
        gain_grad_ref[...] += jnp.sum(g * unit, axis=0, keepdims=True)
        bias_grad_ref[...] += jnp.sum(g, axis=0, keepdims=True)
        grad_sum = norm_back(g * gain_ref[...], unit, inverse)
        sum_ref[...] = grad_sum
        low = grad_sum.astype(BF16)
        low_ref[...] = low
        pre = contract(low, outer_ref[...], 1, 1) * slope_ref[...].astype(F32)
        pre = pre.astype(BF16)
        pre_ref[...] = pre
        part_ref[...] = contract(pre, inner_ref[...], 1, 1).astype(BF16)

    own_rows = row_blocks(0, count, width)
    rows = row_blocks(first, count, width)
    units = row_blocks(first, count, hidden_units)
    line = pl.BlockSpec((1, width), lambda i: (0, 0))
    return pl.pallas_call(
        body,
        grid=(count,),
        in_specs=[
            rows, own_rows, own_rows, line, line, line, line, rows, units,
            pl.BlockSpec((width, hidden_units), lambda i: (0, 0)),
            pl.BlockSpec((hidden_units, width), lambda i: (0, 0)),
        ]
        + [ANYWHERE] * len(into),
        out_specs=[rows, rows, rows, units, own_rows, line, line],
        out_shape=[
            jax.ShapeDtypeStruct((row_total, width), BF16),
            jax.ShapeDtypeStruct((row_total, width), F32),
            jax.ShapeDtypeStruct((row_total, width), BF16),
            jax.ShapeDtypeStruct((row_total, hidden_units), BF16),
            jax.ShapeDtypeStruct((count * PIECE, width), BF16),
            jax.ShapeDtypeStruct((1, width), F32),
            jax.ShapeDtypeStruct((1, width), F32),
        ],
        input_output_aliases={11 + at: at for at in range(len(into))},
        compiler_params=pltpu.CompilerParams(vmem_limit_bytes=VMEM_BYTES),
        cost_estimate=lasting(3 * count),
    )(
        unit_one, own, other, gain_one, bias_one, gain_two, bias_two, cotangent, slope,
        inner_weight, outer_weight, *into,
    )


def project_back(first, unit, inverse, grad_sum, own, other, gain, out_weight, heads, into=()):
    row_total, width = unit.shape
    cols = out_weight.shape[0]
    head_dim = cols // heads
    span = ITEMS * PIECE
    count = own.shape[0] // span
    is_long = first == 0

    def body(unit_ref, inv_ref, sum_ref, own_ref, other_ref, gain_ref, w_ref, *rest):
        hidden_ref, low_ref, att_ref, gain_grad_ref, bias_grad_ref = rest[len(into) :]

        @pl.when(pl.program_id(0) == 0)
        def _():
            gain_grad_ref[...] = jnp.zeros_like(gain_grad_ref)
            bias_grad_ref[...] = jnp.zeros_like(bias_grad_ref)

        unit = unit_ref[...]
        grad = sum_ref[...] + (own_ref[...].astype(F32) + other_ref[...].astype(F32))
        gain_grad_ref[...] += jnp.sum(grad * unit, axis=0, keepdims=True)
        bias_grad_ref[...] += jnp.sum(grad, axis=0, keepdims=True)
        hidden = norm_back(grad * gain_ref[...], unit, inv_ref[...])
        hidden_ref[...] = hidden
        low = hidden.astype(BF16)
        low_ref[...] = low
        att = contract(w_ref[...], low, 1, 1).astype(BF16)
        if is_long:
            items = contract(att, place_of_item(span), 1, 1).astype(BF16)
            for h in range(heads):
                for item in range(ITEMS):
                    att_ref[item * heads + h] = items[
                        h * head_dim : (h + 1) * head_dim, item * PIECE : (item + 1) * PIECE
                    ]
            att_ref[pl.ds(ITEMS * heads, GROUP - ITEMS * heads)] = jnp.zeros(
                (GROUP - ITEMS * heads, head_dim, PIECE), BF16
            )
        else:
            att_ref[...] = att.reshape(heads, head_dim, span)

    own_rows = row_blocks(0, count, width, span)
    rows = row_blocks(first, count, width, span)
    line = pl.BlockSpec((1, width), lambda i: (0, 0))
    if is_long:
        att_spec = pl.BlockSpec((GROUP, head_dim, PIECE), lambda i: (0, 0, 0))
        att_shape = (GROUP, head_dim, PIECE)
    else:
        att_spec = pl.BlockSpec((heads, head_dim, span), lambda i: (0, 0, i))
        att_shape = (heads, head_dim, count * span)
    return pl.pallas_call(
        body,
        grid=(count,),
        in_specs=[
            rows, row_blocks(first, count, 1, span), rows, own_rows, own_rows, line,
            pl.BlockSpec((cols, width), lambda i: (0, 0)),
        ]
        + [ANYWHERE] * len(into),
        out_specs=[rows, rows, att_spec, line, line],
        out_shape=[
            jax.ShapeDtypeStruct((row_total, width), F32),
            jax.ShapeDtypeStruct((row_total, width), BF16),
            jax.ShapeDtypeStruct(att_shape, BF16),
            jax.ShapeDtypeStruct((1, width), F32),
            jax.ShapeDtypeStruct((1, width), F32),
        ],
        input_output_aliases={7 + at: at for at in range(len(into))},
        compiler_params=pltpu.CompilerParams(vmem_limit_bytes=VMEM_BYTES),
        cost_estimate=lasting(4 * count),
    )(unit, inverse, grad_sum, own, other, gain, out_weight, *into)


SLOT = 8


def first_rows(source, mine_ref, away, second, count):
    first = lax.bitwise_xor(mine_ref[0], away)
    return source[pl.ds(pl.multiple_of((first * 4 + second) * count, count), count), :]


def terms_call(body, mine, rows, columns, lines, counts, width, scratch, microseconds):
    span = ITEMS * PIECE
    shape = (4, sum(counts), width)
    return counts, pl.pallas_call(
        body,
        grid=(rows[0].shape[0] // span,),
        in_specs=[pl.BlockSpec(memory_space=pltpu.SMEM)]
        + [pl.BlockSpec((span, array.shape[1]), lambda i: (i, 0)) for array in rows]
        + [pl.BlockSpec((array.shape[0], span), lambda i: (0, i)) for array in columns]
        + [pl.BlockSpec(array.shape, lambda i: (0, 0)) for array in lines],
        out_specs=[pl.BlockSpec(shape, lambda i: (0, 0, 0))] * 4,
        out_shape=[jax.ShapeDtypeStruct(shape, BF16)] * 4,
        scratch_shapes=[pltpu.VMEM(dims, F32) for dims in scratch],
        compiler_params=pltpu.CompilerParams(vmem_limit_bytes=VMEM_BYTES),
        cost_estimate=lasting(microseconds),
    )(mine, *rows, *columns, *lines)


def outer_terms(mine, act, grad_ffn):
    units, width = act.shape[1], grad_ffn.shape[1]
    counts = [units // 16]

    def body(mine_ref, act_ref, ffn_ref, *rest):
        outs, (outer,) = rest[:4], rest[4:]

        @pl.when(pl.program_id(0) == 0)
        def _():
            outer[...] = jnp.zeros_like(outer)

        outer[...] += contract(act_ref[...], ffn_ref[...], 0, 0)

        @pl.when(pl.program_id(0) == pl.num_programs(0) - 1)
        def _():
            for away, ref in enumerate(outs):
                for second in range(4):
                    rows = first_rows(outer, mine_ref, away, second, counts[0])
                    ref[second] = rows.astype(BF16)

    return terms_call(body, mine, [act, grad_ffn], [], [], counts, width, [(units, width)], 9)


def inner_terms(mine, normed, grad_pre, mixed, grad_proj, norm_lines):
    units, width, cols = grad_pre.shape[1], normed.shape[1], mixed.shape[0]
    counts = [width // 16, width // 16, cols // 16, SLOT]

    def body(mine_ref, low_ref, pre_ref, proj_ref, mixed_ref, norm_ref, *rest):
        outs, (inner, out) = rest[:4], rest[4:]

        @pl.when(pl.program_id(0) == 0)
        def _():
            inner[...] = jnp.zeros_like(inner)
            out[...] = jnp.zeros_like(out)

        inner[...] += contract(low_ref[...], pre_ref[...], 0, 0)
        out[...] += contract(mixed_ref[...], proj_ref[...], 1, 0)

        @pl.when(pl.program_id(0) == pl.num_programs(0) - 1)
        def _():
            slot = lax.broadcasted_iota(jnp.int32, (SLOT, width), 0) == 0
            for away, ref in enumerate(outs):
                line = norm_ref[pl.ds(lax.bitwise_xor(mine_ref[0], away), 1), :]
                for second in range(4):
                    both = first_rows(inner, mine_ref, away, second, counts[0]).astype(BF16)
                    ref[second, pl.ds(0, counts[0]), :] = both[:, :width]
                    ref[second, pl.ds(counts[0], counts[1]), :] = both[:, width:]
                    tail = jnp.concatenate(
                        [
                            first_rows(out, mine_ref, away, second, counts[2]),
                            jnp.where(slot, line if second == 0 else 0.0, 0.0),
                        ],
                        axis=0,
                    )
                    ref[second, pl.ds(counts[0] + counts[1], counts[2] + SLOT), :] = (
                        tail.astype(BF16)
                    )

    return terms_call(
        body, mine, [normed, grad_pre, grad_proj], [mixed], [norm_lines], counts, width,
        [(width, units), (cols, width)], 9,
    )


def next_terms(part, counts, bits):
    places, at, pieces = 1 << len(bits), 0, []
    for index, count in enumerate(counts):
        pieces.append(part[at : at + count].reshape(places, -1, part.shape[1]))
        at, counts[index] = at + count, count // places
    return terms_for(jnp.concatenate(pieces, axis=1), bits)


def lay_out(piece, counts, order, first, is_line, outs):
    width = piece.shape[1]
    rows = piece[...].astype(F32)

    def at(count):
        return pl.ds(order * count if isinstance(order, int) else pl.multiple_of(order * count, count), count)

    if len(counts) == 1:
        outs[0][at(counts[0]), :] = rows
        return
    inner, out, norm, taps = outs
    marks = [sum(counts[:index]) for index in range(len(counts))]
    inner[at(counts[0]), pl.ds(0, width)] = rows[: marks[1]]
    inner[at(counts[1]), pl.ds(width, width)] = rows[marks[1] : marks[2]]
    out[at(counts[2]), :] = rows[marks[2] : marks[3]]
    taps[pl.ds(order, 1), :] = rows[marks[3] + 1 : marks[3] + 2]

    @pl.when(is_line)
    def _():
        norm[pl.ds(first, 1), :] = rows[marks[3] : marks[3] + 1]


def gathered_sums(gathered, counts, shapes):
    peers = gathered.shape[0]
    groups = bit_groups(peers)

    def body(in_ref, *outs):
        for at_place in range(peers):
            order = 0
            for bits in groups:
                size = 1 << len(bits)
                order = order * size + ((at_place >> bits[0]) & (size - 1))
            share = peers // 4
            lay_out(in_ref.at[at_place], counts, order, order // share, order % share == 0, outs)

    return sums_call(body, [], [gathered], shapes)


def placed_sums(mine, arrays, aways, counts, shapes):
    def body(mine_ref, *refs):
        ins, outs = refs[: len(arrays)], refs[len(arrays) :]
        for ref, pairs in zip(ins, aways):
            for piece, (first_away, second_away) in enumerate(pairs):
                first = lax.bitwise_xor(mine_ref[0], first_away)
                second = lax.bitwise_xor(mine_ref[1], second_away)
                lay_out(ref.at[piece], counts, first * 4 + second, first, second == 0, outs)

    return sums_call(body, [mine], arrays, shapes)


def sums_call(body, scalars, arrays, shapes):
    def whole(shape):
        return pl.BlockSpec(shape, lambda: (0,) * len(shape))

    return pl.pallas_call(
        body,
        in_specs=[pl.BlockSpec(memory_space=pltpu.SMEM)] * len(scalars)
        + [whole(array.shape) for array in arrays],
        out_specs=[whole(shape) for shape in shapes],
        out_shape=[jax.ShapeDtypeStruct(shape, F32) for shape in shapes],
        compiler_params=pltpu.CompilerParams(vmem_limit_bytes=VMEM_BYTES),
        cost_estimate=lasting(4),
    )(*scalars, *arrays)


def by_twos(steps):
    return len(steps) == 2 and all(len(bits) == 2 for bits in steps)


def across(array, mask):
    peers = lax.axis_size("seq")
    return lax.ppermute(array, "seq", [(i, i ^ mask) for i in range(peers)])


def gather_second(part, steps):
    if not by_twos(steps):
        return part
    came = [came[None] for came in terms_sent([part] * 4, steps[1])]
    return jnp.concatenate([part[None]] + came, axis=0)


def gather_near(own, steps):
    return (across(own[:2], 1), across(own[2:], 2)) if by_twos(steps) else ()


def gather_far(own, near, steps):
    if not near:
        return ()
    return (
        across(jnp.concatenate([own[:2], near[0]], axis=0), 2),
        across(jnp.concatenate([own[2:], near[1]], axis=0), 1),
    )


def placed(own, near, far, counts, shapes):
    place = lax.axis_index("seq")
    if not near:
        return gathered_sums(lax.all_gather(own, "seq", axis=0), counts, shapes)
    mine = jnp.stack([place & 3, (place >> 2) & 3]).astype(jnp.int32)
    aways = [
        [(0, 0), (0, 1), (0, 2), (0, 3)],
        [(1, 0), (1, 1)],
        [(2, 2), (2, 3)],
        [(2, 0), (2, 1), (3, 0), (3, 1)],
        [(1, 2), (1, 3), (3, 2), (3, 3)],
    ]
    return placed_sums(mine, [own, *near, *far], aways, counts, shapes)


def unit_back(moved_pairs, moved_values, short_parts, unit, inverse):
    heads, head_dim = unit.shape[1:3]
    short_heads, _, short_rows = short_parts[0][0].shape
    count = len(short_parts)
    span = ITEMS * PIECE
    blocks = 1 + short_rows // span
    cols = heads * head_dim

    def body(*refs):
        pairs_ref, values_ref = refs[:2]
        short_refs = refs[2 : 2 + 3 * count]
        unit_ref, inv_ref, out_ref, items = refs[2 + 3 * count :]
        block = pl.program_id(0)

        def short_part(which):
            return jnp.concatenate([short_refs[3 * at + which][...] for at in range(count)], axis=0)

        def back(which, grad):
            unit = unit_ref[which]
            along = jnp.sum(unit * grad, axis=1, keepdims=True)
            return ((grad - unit * along) * inv_ref[which]).astype(BF16).reshape(cols, span)

        @pl.when(block == 0)
        def _():
            def long_part(ref, at):
                part = pl.ds(at, head_dim)
                heads_of = [
                    jnp.concatenate([ref[h, part, :], ref[heads + h, part, :]], axis=1)
                    for h in range(heads)
                ]
                return jnp.stack(heads_of, axis=0)

            for which in range(2):
                items[pl.ds(which * cols, cols), :] = back(
                    which, long_part(pairs_ref, which * head_dim).astype(F32)
                )
            items[pl.ds(2 * cols, cols), :] = long_part(values_ref, 0).reshape(cols, span)
            out_ref[...] = contract(items[...], place_of_item(span), 1, 0).astype(BF16)

        @pl.when(block > 0)
        def _():
            out_ref[pl.ds(0, cols), :] = back(0, short_part(0))
            out_ref[pl.ds(cols, cols), :] = back(1, short_part(1))
            out_ref[pl.ds(2 * cols, cols), :] = short_part(2).astype(BF16).reshape(
                cols, span
            )

    short = pl.BlockSpec(
        (short_heads, head_dim, span), lambda i: (0, 0, jnp.maximum(i - 1, 0))
    )
    return pl.pallas_call(
        body,
        grid=(blocks,),
        in_specs=[
            pl.BlockSpec((GROUP, moved_pairs.shape[1], PIECE), lambda i: (0, 0, 0)),
            pl.BlockSpec((GROUP, head_dim, PIECE), lambda i: (0, 0, 0)),
        ]
        + [short] * (3 * count)
        + [
            pl.BlockSpec((2, heads, head_dim, span), lambda i: (0, 0, 0, i)),
            pl.BlockSpec((2, heads, 1, span), lambda i: (0, 0, 0, i)),
        ],
        out_specs=pl.BlockSpec((3 * cols, span), lambda i: (0, i)),
        out_shape=jax.ShapeDtypeStruct((3 * cols, span * blocks), BF16),
        scratch_shapes=[pltpu.VMEM((3 * cols, span), BF16)],
        compiler_params=pltpu.CompilerParams(vmem_limit_bytes=VMEM_BYTES),
        cost_estimate=lasting(8),
    )(moved_pairs, moved_values, *sum(map(tuple, short_parts), ()), unit, inverse)


def other_half(part):
    return lax.ppermute(part, "tp", [(0, 1), (1, 0)])


def bit_groups(peers):
    bits = peers.bit_length() - 1
    return [list(range(low, min(low + 2, bits))) for low in range(0, bits, 2)]


def terms_for(part, bits):
    mine = (lax.axis_index("seq") >> bits[0]) & ((1 << len(bits)) - 1)
    return [
        lax.dynamic_index_in_dim(part, mine ^ away, 0, False) for away in range(1 << len(bits))
    ]


def in_order(gathered, peers):
    sizes = [1 << len(bits) for bits in reversed(bit_groups(peers))]
    count = len(sizes)
    array = gathered.reshape(sizes + list(gathered.shape[1:]))
    array = jnp.transpose(array, list(range(count))[::-1] + [count, count + 1])
    return array.reshape(-1, gathered.shape[-1])


def terms_sent(terms, bits, first=1):
    peers = lax.axis_size("seq")
    terms = terms if first > 1 else terms[1:]
    return [
        lax.ppermute(term, "seq", [(i, i ^ (away << bits[0])) for i in range(peers)])
        for away, term in enumerate(terms, first)
    ]


def terms_gathered(own, bits):
    mine = (lax.axis_index("seq") >> bits[0]) & ((1 << len(bits)) - 1)
    every = jnp.stack([own] + terms_sent([own] * (1 << len(bits)), bits), axis=0)
    return jnp.stack(
        [
            lax.dynamic_index_in_dim(every, mine ^ place, 0, False)
            for place in range(1 << len(bits))
        ],
        axis=0,
    )


def terms_summed(own, came):
    total = own.astype(F32)
    for term in came:
        total = total + term.astype(F32)
    return total.astype(BF16)


def after(first, second):
    return lax.optimization_barrier((first, second))


def shards(
    tokens,
    short_lengths,
    query_weight,
    key_weight,
    value_weight,
    conv_kernel,
    out_weight,
    gain_one,
    bias_one,
    inner_weight,
    outer_weight,
    gain_two,
    bias_two,
    cotangent,
):
    row_total, width = tokens.shape
    heads_dev = conv_kernel.shape[0]
    head_cols = query_weight.shape[1]
    head_dim = head_cols // heads_dev
    short_rows = row_total - ITEMS * PIECE
    units = ITEMS * heads_dev
    place = lax.axis_index("seq") % GROUP
    groups = [
        [first + i for i in range(GROUP)] for first in range(0, lax.axis_size("seq"), GROUP)
    ]

    def exchange(pieces):
        return lax.all_to_all(pieces, "seq", 0, 0, axis_index_groups=groups)

    def by_position(moved, count):
        return jnp.transpose(moved, (1, 0, 2)).reshape(count, head_dim, GROUP * PIECE)

    item_ends = jnp.cumsum(short_lengths[0])
    positions = jnp.arange(short_rows, dtype=jnp.int32)
    item_ids = jnp.sum((positions[:, None] >= item_ends[None, :]).astype(jnp.int32), axis=1)
    ids_row = item_ids[None, :]
    ids_col = jnp.pad(item_ids, (REACH, REACH), constant_values=-1)[:, None]
    item_starts = jnp.concatenate([jnp.zeros((1,), jnp.int32), item_ends[:-1]])
    block_first = jnp.arange(0, short_rows, PIECE, dtype=jnp.int32)
    block_last = block_first + (PIECE - 1)
    inside = (item_starts[None, :] <= block_last[:, None]) & (
        item_ends[None, :] > block_first[:, None]
    )
    lowest = jnp.min(jnp.where(inside, item_starts[None, :], short_rows), axis=1)
    highest = jnp.max(jnp.where(inside, item_ends[None, :], 0), axis=1)
    reach = jnp.stack([lowest // PIECE, (highest + PIECE - 1) // PIECE]).astype(jnp.int32)

    last_tap = LINE - REACH - HALF_WIDTH
    lines = jnp.pad(
        conv_kernel[:, ::-1], ((0, 0), (last_tap, LINE - last_tap - CONV_WIDTH))
    )[:, None, :]
    unit_head = place % heads_dev
    long_line = lax.dynamic_index_in_dim(lines, unit_head, 0, False)

    long_send, short_pack, unit, inverse = project_in(
        tokens, query_weight, key_weight, value_weight, heads_dev
    )
    lines_of = [line[None, :] for line in (gain_one, bias_one, gain_two, bias_two)]
    gain_one, bias_one, gain_two, bias_two = lines_of

    long_moved = exchange(long_send)
    short_att, short_w, short_s = short_forward(reach, ids_row, ids_col, short_pack, lines)
    mixed, short_proj = project_out_short(short_att, out_weight, row_total)
    long_moved, short_proj = after(long_moved, short_proj)
    long_pack = by_position(long_moved, 3)
    long_att, long_w, long_s = long_forward(long_pack[0], long_pack[1], long_pack[2], long_line)

    long_att, short_proj = after(long_att, short_proj)
    long_att = exchange(long_att)
    *forward, short_ffn = feed_forward(
        ITEMS, tokens, short_proj, other_half(short_proj), gain_one, bias_one, inner_weight,
        outer_weight,
    )
    long_att, short_ffn = after(long_att, short_ffn)
    short_ffn_other = other_half(short_ffn)

    mixed, long_proj = project_out_long(long_att, out_weight, mixed)
    *forward, long_ffn = feed_forward(
        0, tokens, long_proj, other_half(long_proj), gain_one, bias_one, inner_weight,
        outer_weight, forward,
    )
    norm_unit, norm_inverse, normed_low, act_low, act_slope = forward
    *backward, long_back, long_gain_two, long_bias_two = feed_back(
        0, norm_unit, long_ffn, other_half(long_ffn), gain_one, bias_one, gain_two, bias_two,
        cotangent, act_slope, inner_weight, outer_weight,
    )
    grad_hidden, grad_proj_low, long_grad, long_gain_one, long_bias_one = project_back(
        0, norm_unit, norm_inverse, backward[1], long_back, other_half(long_back), gain_one,
        out_weight, heads_dev,
    )
    long_grad, backward, short_ffn, short_ffn_other = lax.optimization_barrier(
        (long_grad, backward, short_ffn, short_ffn_other)
    )
    long_grad = exchange(long_grad)
    *backward, short_back, short_gain_two, short_bias_two = feed_back(
        ITEMS, norm_unit, short_ffn, short_ffn_other, gain_one, bias_one, gain_two, bias_two,
        cotangent, act_slope, inner_weight, outer_weight, backward,
    )
    output, grad_sum, grad_ffn_low, grad_pre_low = backward
    grad_hidden, grad_proj_low, short_grad, short_gain_one, short_bias_one = project_back(
        1, norm_unit, norm_inverse, grad_sum, short_back, other_half(short_back), gain_one,
        out_weight, heads_dev, (grad_hidden, grad_proj_low),
    )
    norm_lines = jnp.concatenate(
        [
            long_gain_one + short_gain_one,
            long_bias_one + short_bias_one,
            long_gain_two + short_gain_two,
            long_bias_two + short_bias_two,
        ],
        axis=0,
    )

    peers = lax.axis_size("seq")
    steps = bit_groups(peers)
    mine = (lax.axis_index("seq") & 3).astype(jnp.int32)[None]
    outer_counts, outer_terms_now = outer_terms(mine, act_low, grad_ffn_low)
    outer_terms_now, grad_pre_low = after(outer_terms_now, grad_pre_low)
    outer_came = terms_sent(outer_terms_now, steps[0])
    inner_counts, inner_terms_now = inner_terms(
        mine, normed_low, grad_pre_low, mixed, grad_proj_low, norm_lines
    )
    inner_terms_now, long_grad = after(inner_terms_now, long_grad)
    long_grad = by_position(long_grad, 1)[0]
    long_dv, long_taps = long_back_values(long_pack[2], long_grad, long_w)
    outer_came, own, inner_terms_now, long_dv, long_grad = lax.optimization_barrier(
        (outer_came, outer_terms_now[0], inner_terms_now, long_dv, long_grad)
    )
    outer_part = terms_summed(own, outer_came)
    inner_came = terms_sent(inner_terms_now, steps[0])
    outer_terms_now, long_dv, long_grad = lax.optimization_barrier(
        (terms_for(outer_part, steps[1]), long_dv, long_grad)
    )
    outer_came = terms_sent(outer_terms_now, steps[1])
    long_dv = exchange(long_dv)
    long_dq, long_dk = long_back_pairs(
        long_pack[0], long_pack[1], long_pack[2], long_grad, long_s
    )
    outer_came, outer_own, inner_came, inner_own, long_dv, long_dq, long_dk, short_grad = (
        lax.optimization_barrier(
            (
                outer_came, outer_terms_now[0], inner_came, inner_terms_now[0], long_dv, long_dq,
                long_dk, short_grad,
            )
        )
    )
    outer_part = terms_summed(outer_own, outer_came)
    for bits in steps[2:]:
        terms = next_terms(outer_part, outer_counts, bits)
        outer_part = terms_summed(terms[0], terms_sent(terms, bits))
    inner_part = terms_summed(inner_own, inner_came)
    long_back = jnp.concatenate([long_dq, long_dk], axis=1)
    inner_terms_now, outer_part, long_back, short_grad = lax.optimization_barrier(
        (terms_for(inner_part, steps[1]), outer_part, long_back, short_grad)
    )
    outer_own = gather_second(outer_part, steps)
    long_back = exchange(long_back)
    inner_came = terms_sent(inner_terms_now, steps[1])
    outer_own, short_grad = after(outer_own, short_grad)
    outer_near = gather_near(outer_own, steps)
    *short_parts, short_taps = short_backward(
        reach, ids_row, ids_col, short_pack, short_grad, short_w, short_s
    )
    long_back, short_parts, short_taps, outer_own, outer_near = lax.optimization_barrier(
        (long_back, short_parts, short_taps, outer_own, outer_near)
    )
    outer_far = gather_far(outer_own, outer_near, steps)
    grads_low = unit_back(long_back, long_dv, [short_parts], unit, inverse)
    own, grads_low, outer_far = lax.optimization_barrier(
        (inner_terms_now[0], grads_low, outer_far)
    )
    inner_part = terms_summed(own, inner_came)
    for bits in steps[2:]:
        terms = next_terms(inner_part, inner_counts, bits)
        inner_part = terms_summed(terms[0], terms_sent(terms, bits))

    first_tap = BAND_ROWS - 1 - REACH + HALF_WIDTH
    taps = slice(first_tap, first_tap - CONV_WIDTH, -1)
    owner = (jnp.arange(heads_dev) == unit_head) & (place < units)
    kernel_part = short_taps[:, 0, taps] + jnp.where(owner[:, None], long_taps[:, taps], 0.0)
    taps_line = kernel_part.reshape(1, -1)
    taps_line = jnp.pad(taps_line, ((0, 0), (0, width - taps_line.shape[1]))).astype(BF16)
    (outer_sum,) = placed(
        outer_own, outer_near, outer_far, outer_counts, [outer_weight.shape]
    )
    taps_at = sum(inner_counts[:-1]) + 1
    inner_part = jnp.concatenate(
        [inner_part[:taps_at], taps_line, inner_part[taps_at + 1 :]], axis=0
    )
    inner_own = gather_second(inner_part, steps)
    inner_near = gather_near(inner_own, steps)
    inner_far = gather_far(inner_own, inner_near, steps)

    weight_part = contract(tokens, grads_low, 0, 1).astype(BF16)
    terms = terms_for(weight_part.reshape(1 << len(steps[0]), -1, 3 * head_cols), steps[0])
    terms, grads_low = after(terms, grads_low)
    came = terms_sent(terms, steps[0])
    weight_all = jnp.concatenate([query_weight, key_weight, value_weight], axis=1)
    token_own = contract(grads_low, weight_all, 0, 1).astype(BF16)
    own, token_own = after(terms[0], token_own)
    weight_part = terms_summed(own, came)
    for bits in steps[1:]:
        terms = terms_for(weight_part.reshape(1 << len(bits), -1, 3 * head_cols), bits)
        weight_part = terms_summed(terms[0], terms_sent(terms, bits))
    for bits in reversed(steps):
        weight_part = terms_gathered(weight_part, bits).reshape(-1, 3 * head_cols)
    weight_sum = weight_part.astype(F32)
    token_grad = grad_hidden + (token_own.astype(F32) + other_half(token_own).astype(F32))
    inner_sum, out_sum, norm_sums, tap_lines = placed(
        inner_own, inner_near, inner_far, inner_counts,
        [inner_weight.shape, out_weight.shape, (4, width), (peers, width)],
    )
    kernel_sum = jnp.sum(tap_lines[:, : heads_dev * CONV_WIDTH], axis=0).reshape(
        heads_dev, CONV_WIDTH
    )
    return (
        output,
        token_grad,
        weight_sum[:, :head_cols],
        weight_sum[:, head_cols : 2 * head_cols],
        weight_sum[:, 2 * head_cols :],
        kernel_sum,
        out_sum,
        norm_sums[0],
        norm_sums[1],
        inner_sum,
        outer_sum,
        norm_sums[2],
        norm_sums[3],
    )


def solution(mesh):
    rows = P("seq", None)
    columns = P(None, "tp")
    split_rows = P("tp", None)
    return jax.shard_map(
        shards,
        mesh=mesh,
        in_specs=(
            rows, rows, columns, columns, columns, split_rows, split_rows,
            P(), P(), columns, split_rows, P(), P(), rows,
        ),
        out_specs=(
            rows, rows, columns, columns, columns, split_rows, split_rows,
            P(), P(), columns, split_rows, P(), P(),
        ),
        check_vma=False,
    )
```

```python
import math

import jax
import jax.numpy as jnp
from jax import lax
from jax.experimental import pallas as pl
from jax.experimental.pallas import tpu as pltpu
from jax.sharding import PartitionSpec as P

TAU = 8
CONV_WIDTH = 33
HALF_WIDTH = 16
GROUP = 16
PIECE = 256
ITEMS = 2
REACH = 32
BAND_ROWS = PIECE + 2 * REACH
LINE = 640

COS_SCALE = 0.98
EPS_UNIT = 1e-06
EPS_NORM = 1e-05
NEAR_POLY = (1.158024787902832, -0.36302468180656433, 0.09245320409536362, -0.011449637822806835)
TAIL_POLY = tuple(
    0.5 * a for a in (0.254829592, -0.284496736, 1.421413741, -1.453152027, 1.061405429)
)
SLOPE_SCALE = TAU / math.pi
VMEM_BYTES = 60 * 2**20

F32 = jnp.float32
BF16 = jnp.bfloat16


def norm_terms(values):
    centered = values - jnp.mean(values, axis=-1, keepdims=True)
    inverse = lax.rsqrt(jnp.mean(centered * centered, axis=-1, keepdims=True) + EPS_NORM)
    return centered * inverse, inverse


def norm_back(scaled, unit, inverse):
    along = jnp.mean(scaled * unit, axis=-1, keepdims=True)
    return inverse * (scaled - jnp.mean(scaled, axis=-1, keepdims=True) - unit * along)


def gelu_terms(values):
    share = 1.0 / (1.0 + (0.3275911 * math.sqrt(0.5)) * jnp.abs(values))
    bell = jnp.exp(-0.5 * (values * values))
    poly = TAIL_POLY[4] * share + TAIL_POLY[3]
    for coefficient in TAIL_POLY[2::-1]:
        poly = poly * share + coefficient
    tail = poly * (share * bell)
    below = jnp.where(values < 0.0, tail, 1.0 - tail)
    return values * below, below + values * (bell * (1.0 / math.sqrt(2.0 * math.pi)))


def place_of_item(rows):
    item_at = lax.broadcasted_iota(jnp.int32, (rows, rows), 0)
    place_at = lax.broadcasted_iota(jnp.int32, (rows, rows), 1)
    hit = item_at == (place_at & 1) * PIECE + (place_at >> 1)
    return jnp.where(hit, 1.0, 0.0).astype(BF16)


def lasting(microseconds):
    return pl.CostEstimate(flops=microseconds * 1_150_000_000, bytes_accessed=0, transcendentals=0)


def contract(left, right, left_dim, right_dim):
    return lax.dot_general(
        left, right, (((left_dim,), (right_dim,)), ((), ())), preferred_element_type=F32
    )


def pair_terms(dots, same=None):
    upper = 1.0 / COS_SCALE + dots
    lower = 1.0 / COS_SCALE - dots
    upper_inv = lax.rsqrt(upper)
    lower_inv = lax.rsqrt(lower)
    wide = 1.0 / 0.7 + lower * lower_inv
    wide_inv = lax.rsqrt(wide)
    root = wide * wide_inv
    ratio = NEAR_POLY[3] * root + NEAR_POLY[2]
    ratio = ratio * root + NEAR_POLY[1]
    ratio = ratio * root + NEAR_POLY[0]
    near = ratio * ((upper * upper_inv) * wide_inv)
    if same is not None:
        near = jnp.where(same, near, 0.0)
    near_2 = near * near
    near_4 = near_2 * near_2
    weights = (near_4 * near_4).astype(BF16)
    slopes = ((near_4 * near_2) * (near * (upper_inv * lower_inv))).astype(BF16)
    return weights, slopes


def banded(line):
    wide = jnp.broadcast_to(line, (BAND_ROWS, line.shape[1]))
    return pltpu.roll(wide, 0, 1, stride=1, stride_axis=0)[:, :PIECE].astype(BF16)


def unbanded(products):
    rows_at = lax.broadcasted_iota(jnp.int32, (BAND_ROWS, BAND_ROWS), 0)
    rows_to = lax.broadcasted_iota(jnp.int32, (BAND_ROWS, BAND_ROWS), 1)
    flip = jnp.where(rows_at + rows_to == BAND_ROWS - 1, 1.0, 0.0)
    flipped = lax.dot_general(
        flip, products, (((1,), (0,)), ((), ())), precision=lax.Precision.HIGHEST,
        preferred_element_type=F32,
    )
    wide = jnp.concatenate([flipped, jnp.zeros((BAND_ROWS, LINE - PIECE), F32)], axis=1)
    return jnp.sum(pltpu.roll(wide, 0, 1, stride=1, stride_axis=0), axis=0, keepdims=True)


def padded_rows(dst, src, length):
    edge = jnp.zeros((REACH, dst.shape[1]), dst.dtype)
    dst[pl.ds(0, REACH), :] = edge
    dst[pl.ds(REACH + length, REACH), :] = edge
    for start in range(0, length, PIECE):
        dst[pl.ds(REACH + start, PIECE), :] = src[:, pl.ds(start, PIECE)].T


def rows_of(dst, src, length):
    for start in range(0, length, PIECE):
        dst[pl.ds(start, PIECE), :] = src[:, pl.ds(start, PIECE)].T


def long_forward(query, key, value, line):
    head_dim, length = query.shape
    blocks = length // PIECE
    step = 512

    def body(q_ref, k_ref, v_ref, line_ref, o_ref, w_ref, s_ref, key_rows, taps):
        block = pl.program_id(0)

        @pl.when(block == 0)
        def _():
            rows_of(key_rows, k_ref, length)
            taps[...] = jnp.zeros_like(taps)
            taps[pl.ds(length - REACH, BAND_ROWS), :] = banded(line_ref[...])

        q = q_ref[...]
        start = block * PIECE
        total = jnp.zeros((head_dim, PIECE), F32)
        for at in range(0, length, step):
            dots = contract(key_rows[pl.ds(at, step), :], q, 1, 0)
            weights, slopes = pair_terms(dots)
            near = pl.multiple_of(length + at - start, PIECE)
            weights = weights + taps[pl.ds(near, step), :]
            w_ref[pl.ds(at, step), :] = weights
            s_ref[pl.ds(at, step), :] = slopes
            total = total + contract(v_ref[:, pl.ds(at, step)], weights, 1, 0)
        o_ref[...] = total.astype(BF16)

    whole = pl.BlockSpec((head_dim, length), lambda i: (0, 0))
    large = pl.BlockSpec((None, length, PIECE), lambda i: (i, 0, 0))
    large_shape = jax.ShapeDtypeStruct((blocks, length, PIECE), BF16)
    return pl.pallas_call(
        body,
        grid=(blocks,),
        in_specs=[
            pl.BlockSpec((head_dim, PIECE), lambda i: (0, i)),
            whole,
            whole,
            pl.BlockSpec((1, LINE), lambda i: (0, 0)),
        ],
        out_specs=[pl.BlockSpec((None, head_dim, PIECE), lambda i: (i, 0, 0)), large, large],
        out_shape=[jax.ShapeDtypeStruct((blocks, head_dim, PIECE), BF16), large_shape, large_shape],
        scratch_shapes=[
            pltpu.VMEM((length, head_dim), BF16),
            pltpu.VMEM((2 * length, PIECE), BF16),
        ],
        compiler_params=pltpu.CompilerParams(vmem_limit_bytes=VMEM_BYTES),
        cost_estimate=lasting(70),
    )(query, key, value, line)


def long_back_values(value, grad, weights):
    head_dim, length = grad.shape
    blocks = length // PIECE
    step = 1024

    def body(v_ref, g_ref, w_ref, dv_ref, taps_ref, value_sum, value_rows, products):
        block = pl.program_id(0)

        @pl.when(block == 0)
        def _():
            padded_rows(value_rows, v_ref, length)
            value_sum[...] = jnp.zeros_like(value_sum)
            products[...] = jnp.zeros_like(products)

        g = g_ref[...]
        start = pl.multiple_of(block * PIECE, PIECE)
        products[...] += contract(value_rows[pl.ds(start, BAND_ROWS), :], g, 1, 0)
        for at in range(0, length, step):
            value_sum[:, pl.ds(at, step)] += contract(g, w_ref[pl.ds(at, step), :], 1, 1)

        @pl.when(block == blocks - 1)
        def _():
            for index in range(blocks):
                dv_ref[index] = value_sum[:, pl.ds(index * PIECE, PIECE)].astype(BF16)
            taps_ref[...] = unbanded(products[...])

    return pl.pallas_call(
        body,
        grid=(blocks,),
        in_specs=[
            pl.BlockSpec((head_dim, length), lambda i: (0, 0)),
            pl.BlockSpec((head_dim, PIECE), lambda i: (0, i)),
            pl.BlockSpec((None, length, PIECE), lambda i: (i, 0, 0)),
        ],
        out_specs=[
            pl.BlockSpec((blocks, head_dim, PIECE), lambda i: (0, 0, 0)),
            pl.BlockSpec((1, LINE), lambda i: (0, 0)),
        ],
        out_shape=[
            jax.ShapeDtypeStruct((blocks, head_dim, PIECE), BF16),
            jax.ShapeDtypeStruct((1, LINE), F32),
        ],
        scratch_shapes=[
            pltpu.VMEM((head_dim, length), F32),
            pltpu.VMEM((length + 2 * REACH, head_dim), BF16),
            pltpu.VMEM((BAND_ROWS, PIECE), F32),
        ],
        compiler_params=pltpu.CompilerParams(vmem_limit_bytes=VMEM_BYTES),
        cost_estimate=lasting(1),
    )(value, grad, weights)


def long_back_pairs(query, key, value, grad, slopes):
    head_dim, length = query.shape
    blocks = length // PIECE
    step = 1024

    def body(q_ref, k_ref, v_ref, g_ref, s_ref, dq_ref, dk_ref, value_rows, key_sum):
        block = pl.program_id(0)

        @pl.when(block == 0)
        def _():
            rows_of(value_rows, v_ref, length)
            key_sum[...] = jnp.zeros_like(key_sum)

        q = q_ref[...]
        g = g_ref[...]
        total = jnp.zeros((head_dim, PIECE), F32)
        for at in range(0, length, step):
            grad_weights = contract(value_rows[pl.ds(at, step), :], g, 1, 0)
            terms = grad_weights.astype(BF16) * s_ref[pl.ds(at, step), :]
            total = total + contract(k_ref[:, pl.ds(at, step)], terms, 1, 0)
            key_sum[:, pl.ds(at, step)] += contract(q, terms, 1, 1)
        dq_ref[...] = (total * SLOPE_SCALE).astype(BF16)

        @pl.when(block == blocks - 1)
        def _():
            for index in range(blocks):
                piece = key_sum[:, pl.ds(index * PIECE, PIECE)]
                dk_ref[index] = (piece * SLOPE_SCALE).astype(BF16)

    whole = pl.BlockSpec((head_dim, length), lambda i: (0, 0))
    piece = pl.BlockSpec((head_dim, PIECE), lambda i: (0, i))
    pieces_shape = jax.ShapeDtypeStruct((blocks, head_dim, PIECE), BF16)
    return pl.pallas_call(
        body,
        grid=(blocks,),
        in_specs=[
            piece,
            whole,
            whole,
            piece,
            pl.BlockSpec((None, length, PIECE), lambda i: (i, 0, 0)),
        ],
        out_specs=[
            pl.BlockSpec((None, head_dim, PIECE), lambda i: (i, 0, 0)),
            pl.BlockSpec((blocks, head_dim, PIECE), lambda i: (0, 0, 0)),
        ],
        out_shape=[pieces_shape] * 2,
        scratch_shapes=[
            pltpu.VMEM((length, head_dim), BF16),
            pltpu.VMEM((head_dim, length), F32),
        ],
        compiler_params=pltpu.CompilerParams(vmem_limit_bytes=VMEM_BYTES),
        cost_estimate=lasting(40),
    )(query, key, value, grad, slopes)


def short_forward(reach, ids_row, ids_col, pack, lines):
    _, heads, head_dim, length = pack.shape
    blocks = length // PIECE

    def body(
        reach_ref, row_ref, col_ref, q_ref, k_ref, v_ref, line_ref,
        o_ref, w_ref, s_ref, key_rows, total, taps,
    ):
        block = pl.program_id(0)

        @pl.when(block == 0)
        def _():
            taps[...] = jnp.zeros_like(taps)
            for h in range(heads):
                rows_of(key_rows.at[h], k_ref.at[h], length)
                taps[h, pl.ds(length - REACH, BAND_ROWS), :] = banded(line_ref[h])

        total[...] = jnp.zeros_like(total)
        own_ids = row_ref[...]

        def turn(step, carry):
            at = pl.multiple_of(step * PIECE, PIECE)
            same = col_ref[pl.ds(REACH + at, PIECE), :] == own_ids
            same_low = same.astype(F32).astype(BF16)
            near = pl.multiple_of(length + at - block * PIECE, PIECE)
            for h in range(heads):
                dots = contract(key_rows[h, pl.ds(at, PIECE), :], q_ref[h], 1, 0)
                weights, slopes = pair_terms(dots, same)
                weights = weights + taps[h, pl.ds(near, PIECE), :] * same_low
                w_ref[h, pl.ds(at, PIECE), :] = weights
                s_ref[h, pl.ds(at, PIECE), :] = slopes
                total[h] += contract(v_ref[h, :, pl.ds(at, PIECE)], weights, 1, 0)
            return carry

        lax.fori_loop(reach_ref[0, block], reach_ref[1, block], turn, 0)
        o_ref[...] = total[...].astype(BF16)

    def packed(which):
        return pl.BlockSpec((None, heads, head_dim, length), lambda i: (which, 0, 0, 0))

    block_spec = pl.BlockSpec((heads, head_dim, PIECE), lambda i: (0, 0, i))
    large = pl.BlockSpec((None, heads, length, PIECE), lambda i: (i, 0, 0, 0))
    large_shape = jax.ShapeDtypeStruct((blocks, heads, length, PIECE), BF16)
    return pl.pallas_call(
        body,
        grid=(blocks,),
        in_specs=[
            pl.BlockSpec(memory_space=pltpu.SMEM),
            pl.BlockSpec((1, PIECE), lambda i: (0, i)),
            pl.BlockSpec(ids_col.shape, lambda i: (0, 0)),
            pl.BlockSpec((None, heads, head_dim, PIECE), lambda i: (0, 0, 0, i)),
            packed(1),
            packed(2),
            pl.BlockSpec((heads, 1, LINE), lambda i: (0, 0, 0)),
        ],
        out_specs=[block_spec, large, large],
        out_shape=[jax.ShapeDtypeStruct((heads, head_dim, length), BF16), large_shape, large_shape],
        scratch_shapes=[
            pltpu.VMEM((heads, length, head_dim), BF16),
            pltpu.VMEM((heads, head_dim, PIECE), F32),
            pltpu.VMEM((heads, 2 * length, PIECE), BF16),
        ],
        compiler_params=pltpu.CompilerParams(vmem_limit_bytes=VMEM_BYTES),
        cost_estimate=lasting(28),
    )(reach, ids_row, ids_col, pack, pack, pack, lines)


def short_backward(reach, ids_row, ids_col, pack, grad, weights, slopes):
    _, heads, head_dim, length = pack.shape
    blocks = length // PIECE

    def body(
        reach_ref, row_ref, col_ref, q_ref, k_ref, v_ref, g_ref, w_ref, s_ref,
        dq_ref, dk_ref, dv_ref, taps_ref, value_rows, products,
    ):
        block = pl.program_id(0)

        @pl.when(block == 0)
        def _():
            for h in range(heads):
                padded_rows(value_rows.at[h], v_ref.at[h], length)
            dk_ref[...] = jnp.zeros_like(dk_ref)
            dv_ref[...] = jnp.zeros_like(dv_ref)
            products[...] = jnp.zeros_like(products)

        start = pl.multiple_of(block * PIECE, PIECE)
        near = (col_ref[pl.ds(start, BAND_ROWS), :] == row_ref[...]).astype(F32)
        for h in range(heads):
            products[h] += (
                contract(value_rows[h, pl.ds(start, BAND_ROWS), :], g_ref[h], 1, 0) * near
            )
        dq_ref[...] = jnp.zeros_like(dq_ref)

        def turn(step, carry):
            at = pl.multiple_of(step * PIECE, PIECE)
            for h in range(heads):
                own = g_ref[h]
                grad_weights = contract(value_rows[h, pl.ds(REACH + at, PIECE), :], own, 1, 0)
                terms = grad_weights.astype(BF16) * s_ref[h, pl.ds(at, PIECE), :]
                dq_ref[h] += contract(k_ref[h, :, pl.ds(at, PIECE)], terms, 1, 0) * SLOPE_SCALE
                dk_ref[h, :, pl.ds(at, PIECE)] += contract(q_ref[h], terms, 1, 1) * SLOPE_SCALE
                dv_ref[h, :, pl.ds(at, PIECE)] += contract(own, w_ref[h, pl.ds(at, PIECE), :], 1, 1)
            return carry

        lax.fori_loop(reach_ref[0, block], reach_ref[1, block], turn, 0)

        @pl.when(block == blocks - 1)
        def _():
            for h in range(heads):
                taps_ref[h] = unbanded(products[h])

    def packed(which):
        return pl.BlockSpec((None, heads, head_dim, length), lambda i: (which, 0, 0, 0))

    block_spec = pl.BlockSpec((heads, head_dim, PIECE), lambda i: (0, 0, i))
    whole = pl.BlockSpec((heads, head_dim, length), lambda i: (0, 0, 0))
    large = pl.BlockSpec((None, heads, length, PIECE), lambda i: (i, 0, 0, 0))
    whole_shape = jax.ShapeDtypeStruct((heads, head_dim, length), F32)
    return pl.pallas_call(
        body,
        grid=(blocks,),
        in_specs=[
            pl.BlockSpec(memory_space=pltpu.SMEM),
            pl.BlockSpec((1, PIECE), lambda i: (0, i)),
            pl.BlockSpec(ids_col.shape, lambda i: (0, 0)),
            pl.BlockSpec((None, heads, head_dim, PIECE), lambda i: (0, 0, 0, i)),
            packed(1),
            packed(2),
            block_spec,
            large,
            large,
        ],
        out_specs=[block_spec, whole, whole, pl.BlockSpec((heads, 1, LINE), lambda i: (0, 0, 0))],
        out_shape=[whole_shape] * 3 + [jax.ShapeDtypeStruct((heads, 1, LINE), F32)],
        scratch_shapes=[
            pltpu.VMEM((heads, length + 2 * REACH, head_dim), BF16),
            pltpu.VMEM((heads, BAND_ROWS, PIECE), F32),
        ],
        compiler_params=pltpu.CompilerParams(vmem_limit_bytes=VMEM_BYTES),
        cost_estimate=lasting(28),
    )(reach, ids_row, ids_col, pack, pack, pack, grad, weights, slopes)


def project_in(tokens, query_weight, key_weight, value_weight, heads):
    row_total, width = tokens.shape
    cols = query_weight.shape[1]
    head_dim = cols // heads
    blocks = row_total // PIECE
    long_rows = ITEMS * PIECE

    def body(t_ref, wq_ref, wk_ref, wv_ref, long_ref, short_ref, unit_ref, inv_ref, turned, rows):
        block = pl.program_id(0)

        @pl.when(block == 0)
        def _():
            for index, ref in enumerate((wq_ref, wk_ref, wv_ref)):
                turned[pl.ds(index * cols, cols), :] = ref[...].T
            long_ref[pl.ds(ITEMS * heads, GROUP - ITEMS * heads)] = jnp.zeros(
                (GROUP - ITEMS * heads, 3 * head_dim, PIECE), BF16
            )

        @pl.when(block < ITEMS)
        def _():
            item_at = lax.broadcasted_iota(jnp.int32, (PIECE, long_rows), 0)
            place_at = lax.broadcasted_iota(jnp.int32, (PIECE, long_rows), 1)
            pick = jnp.where(place_at == ITEMS * item_at + block, 1.0, 0.0).astype(BF16)
            rows[...] = contract(pick, t_ref[pl.ds(0, long_rows), :], 1, 0).astype(BF16)

        @pl.when(block >= ITEMS)
        def _():
            rows[...] = t_ref[pl.ds(pl.multiple_of(block * PIECE, PIECE), PIECE), :]

        parts = contract(turned[...], rows[...], 1, 1).reshape(3, heads, head_dim, PIECE)
        raw = parts[:2]
        inverse = lax.rsqrt(jnp.sum(raw * raw, axis=2, keepdims=True) + EPS_UNIT)
        unit = raw * inverse
        unit_ref[...] = unit
        inv_ref[...] = inverse
        low = unit.astype(BF16)
        short_ref[:2] = low
        short_ref[2] = parts[2].astype(BF16)

        @pl.when(block < ITEMS)
        def _():
            for h in range(heads):
                unit_at = block * heads + h
                long_ref[unit_at, pl.ds(0, head_dim), :] = low[0, h]
                long_ref[unit_at, pl.ds(head_dim, head_dim), :] = low[1, h]
                long_ref[unit_at, pl.ds(2 * head_dim, head_dim), :] = parts[2, h].astype(BF16)

    weight = pl.BlockSpec((width, cols), lambda i: (0, 0))
    return pl.pallas_call(
        body,
        grid=(blocks,),
        in_specs=[pl.BlockSpec((row_total, width), lambda i: (0, 0)), weight, weight, weight],
        out_specs=[
            pl.BlockSpec((GROUP, 3 * head_dim, PIECE), lambda i: (0, 0, 0)),
            pl.BlockSpec(
                (3, heads, head_dim, PIECE), lambda i: (0, 0, 0, jnp.maximum(i - ITEMS, 0))
            ),
            pl.BlockSpec((2, heads, head_dim, PIECE), lambda i: (0, 0, 0, i)),
            pl.BlockSpec((2, heads, 1, PIECE), lambda i: (0, 0, 0, i)),
        ],
        out_shape=[
            jax.ShapeDtypeStruct((GROUP, 3 * head_dim, PIECE), BF16),
            jax.ShapeDtypeStruct((3, heads, head_dim, row_total - long_rows), BF16),
            jax.ShapeDtypeStruct((2, heads, head_dim, row_total), F32),
            jax.ShapeDtypeStruct((2, heads, 1, row_total), F32),
        ],
        scratch_shapes=[pltpu.VMEM((3 * cols, width), BF16), pltpu.VMEM((PIECE, width), BF16)],
        compiler_params=pltpu.CompilerParams(vmem_limit_bytes=VMEM_BYTES),
        cost_estimate=lasting(10),
    )(tokens, query_weight, key_weight, value_weight)


def row_blocks(first, count, cols, span=PIECE):
    return pl.BlockSpec((span, cols), lambda i: (i + first, 0))


ANYWHERE = pl.BlockSpec(memory_space=pl.ANY)


def project_out_short(short_att, out_weight, row_total):
    heads, head_dim, short_rows = short_att.shape
    cols, width = out_weight.shape
    span = ITEMS * PIECE

    def body(a_ref, w_ref, mixed_ref, part_ref):
        mixed = a_ref[...].reshape(cols, span)
        mixed_ref[...] = mixed
        part_ref[...] = contract(mixed, w_ref[...], 0, 0).astype(BF16)

    return pl.pallas_call(
        body,
        grid=(short_rows // span,),
        in_specs=[
            pl.BlockSpec((heads, head_dim, span), lambda i: (0, 0, i)),
            pl.BlockSpec((cols, width), lambda i: (0, 0)),
        ],
        out_specs=[
            pl.BlockSpec((cols, span), lambda i: (0, i + 1)),
            pl.BlockSpec((span, width), lambda i: (i, 0)),
        ],
        out_shape=[
            jax.ShapeDtypeStruct((cols, row_total), BF16),
            jax.ShapeDtypeStruct((short_rows, width), BF16),
        ],
        compiler_params=pltpu.CompilerParams(vmem_limit_bytes=VMEM_BYTES),
        cost_estimate=lasting(4),
    )(short_att, out_weight)


def project_out_long(moved, out_weight, mixed):
    cols, width = out_weight.shape
    head_dim = moved.shape[1]
    heads = cols // head_dim
    span = ITEMS * PIECE

    def body(m_ref, w_ref, old_ref, mixed_ref, part_ref, items):
        for h in range(heads):
            for item in range(ITEMS):
                items[pl.ds(h * head_dim, head_dim), pl.ds(item * PIECE, PIECE)] = m_ref[
                    item * heads + h
                ]
        placed = contract(items[...], place_of_item(span), 1, 0).astype(BF16)
        mixed_ref[...] = placed
        part_ref[...] = contract(placed, w_ref[...], 0, 0).astype(BF16)

    return pl.pallas_call(
        body,
        grid=(1,),
        in_specs=[
            pl.BlockSpec((GROUP, head_dim, PIECE), lambda i: (0, 0, 0)),
            pl.BlockSpec((cols, width), lambda i: (0, 0)),
            ANYWHERE,
        ],
        out_specs=[
            pl.BlockSpec((cols, span), lambda i: (0, 0)),
            pl.BlockSpec((span, width), lambda i: (0, 0)),
        ],
        out_shape=[
            jax.ShapeDtypeStruct(mixed.shape, BF16),
            jax.ShapeDtypeStruct((span, width), BF16),
        ],
        scratch_shapes=[pltpu.VMEM((cols, span), BF16)],
        input_output_aliases={2: 0},
        compiler_params=pltpu.CompilerParams(vmem_limit_bytes=VMEM_BYTES),
        cost_estimate=lasting(3),
    )(moved, out_weight, mixed)


def feed_forward(first, tokens, own, other, gain, bias, inner_weight, outer_weight, into=()):
    row_total, width = tokens.shape
    count = own.shape[0] // PIECE
    hidden_units = inner_weight.shape[1]

    def body(t_ref, own_ref, other_ref, gain_ref, bias_ref, inner_ref, outer_ref, *rest):
        unit_ref, inv_ref, low_ref, act_ref, slope_ref, part_ref = rest[len(into) :]
        hidden = t_ref[...].astype(F32) + (
            own_ref[...].astype(F32) + other_ref[...].astype(F32)
        )
        unit, inverse = norm_terms(hidden)
        unit_ref[...] = unit
        inv_ref[...] = inverse
        low = (unit * gain_ref[...] + bias_ref[...]).astype(BF16)
        low_ref[...] = low
        act, slope = gelu_terms(contract(low, inner_ref[...], 1, 0))
        act = act.astype(BF16)
        act_ref[...] = act
        slope_ref[...] = slope.astype(BF16)
        part_ref[...] = contract(act, outer_ref[...], 1, 0).astype(BF16)

    own_rows = row_blocks(0, count, width)
    rows = row_blocks(first, count, width)
    units = row_blocks(first, count, hidden_units)
    line = pl.BlockSpec((1, width), lambda i: (0, 0))
    return pl.pallas_call(
        body,
        grid=(count,),
        in_specs=[
            rows, own_rows, own_rows, line, line,
            pl.BlockSpec((width, hidden_units), lambda i: (0, 0)),
            pl.BlockSpec((hidden_units, width), lambda i: (0, 0)),
        ]
        + [ANYWHERE] * len(into),
        out_specs=[rows, row_blocks(first, count, 1), rows, units, units, own_rows],
        out_shape=[
            jax.ShapeDtypeStruct((row_total, width), F32),
            jax.ShapeDtypeStruct((row_total, 1), F32),
            jax.ShapeDtypeStruct((row_total, width), BF16),
            jax.ShapeDtypeStruct((row_total, hidden_units), BF16),
            jax.ShapeDtypeStruct((row_total, hidden_units), BF16),
            jax.ShapeDtypeStruct((count * PIECE, width), BF16),
        ],
        input_output_aliases={7 + at: at for at in range(len(into))},
        compiler_params=pltpu.CompilerParams(vmem_limit_bytes=VMEM_BYTES),
        cost_estimate=lasting(3 * count),
    )(tokens, own, other, gain, bias, inner_weight, outer_weight, *into)


def feed_back(
    first, unit_one, own, other, gain_one, bias_one, gain_two, bias_two, cotangent, slope,
    inner_weight, outer_weight, into=(),
):
    row_total, width = unit_one.shape
    count = own.shape[0] // PIECE
    hidden_units = inner_weight.shape[1]

    def body(
        unit_ref, own_ref, other_ref, gain_one_ref, bias_one_ref, gain_ref, bias_ref, g_ref,
        slope_ref, inner_ref, outer_ref, *rest,
    ):
        out_ref, sum_ref, low_ref, pre_ref, part_ref, gain_grad_ref, bias_grad_ref = rest[
            len(into) :
        ]

        @pl.when(pl.program_id(0) == 0)
        def _():
            gain_grad_ref[...] = jnp.zeros_like(gain_grad_ref)
            bias_grad_ref[...] = jnp.zeros_like(bias_grad_ref)

        normed = unit_ref[...] * gain_one_ref[...] + bias_one_ref[...]
        unit, inverse = norm_terms(
            normed + (own_ref[...].astype(F32) + other_ref[...].astype(F32))
        )
        out_ref[...] = (unit * gain_ref[...] + bias_ref[...]).astype(BF16)
        g = g_ref[...].astype(F32)
        gain_grad_ref[...] += jnp.sum(g * unit, axis=0, keepdims=True)
        bias_grad_ref[...] += jnp.sum(g, axis=0, keepdims=True)
        grad_sum = norm_back(g * gain_ref[...], unit, inverse)
        sum_ref[...] = grad_sum
        low = grad_sum.astype(BF16)
        low_ref[...] = low
        pre = contract(low, outer_ref[...], 1, 1) * slope_ref[...].astype(F32)
        pre = pre.astype(BF16)
        pre_ref[...] = pre
        part_ref[...] = contract(pre, inner_ref[...], 1, 1).astype(BF16)

    own_rows = row_blocks(0, count, width)
    rows = row_blocks(first, count, width)
    units = row_blocks(first, count, hidden_units)
    line = pl.BlockSpec((1, width), lambda i: (0, 0))
    return pl.pallas_call(
        body,
        grid=(count,),
        in_specs=[
            rows, own_rows, own_rows, line, line, line, line, rows, units,
            pl.BlockSpec((width, hidden_units), lambda i: (0, 0)),
            pl.BlockSpec((hidden_units, width), lambda i: (0, 0)),
        ]
        + [ANYWHERE] * len(into),
        out_specs=[rows, rows, rows, units, own_rows, line, line],
        out_shape=[
            jax.ShapeDtypeStruct((row_total, width), BF16),
            jax.ShapeDtypeStruct((row_total, width), F32),
            jax.ShapeDtypeStruct((row_total, width), BF16),
            jax.ShapeDtypeStruct((row_total, hidden_units), BF16),
            jax.ShapeDtypeStruct((count * PIECE, width), BF16),
            jax.ShapeDtypeStruct((1, width), F32),
            jax.ShapeDtypeStruct((1, width), F32),
        ],
        input_output_aliases={11 + at: at for at in range(len(into))},
        compiler_params=pltpu.CompilerParams(vmem_limit_bytes=VMEM_BYTES),
        cost_estimate=lasting(3 * count),
    )(
        unit_one, own, other, gain_one, bias_one, gain_two, bias_two, cotangent, slope,
        inner_weight, outer_weight, *into,
    )


def project_back(first, unit, inverse, grad_sum, own, other, gain, out_weight, heads, into=()):
    row_total, width = unit.shape
    cols = out_weight.shape[0]
    head_dim = cols // heads
    span = ITEMS * PIECE
    count = own.shape[0] // span
    is_long = first == 0

    def body(unit_ref, inv_ref, sum_ref, own_ref, other_ref, gain_ref, w_ref, *rest):
        hidden_ref, low_ref, att_ref, gain_grad_ref, bias_grad_ref = rest[len(into) :]

        @pl.when(pl.program_id(0) == 0)
        def _():
            gain_grad_ref[...] = jnp.zeros_like(gain_grad_ref)
            bias_grad_ref[...] = jnp.zeros_like(bias_grad_ref)

        unit = unit_ref[...]
        grad = sum_ref[...] + (own_ref[...].astype(F32) + other_ref[...].astype(F32))
        gain_grad_ref[...] += jnp.sum(grad * unit, axis=0, keepdims=True)
        bias_grad_ref[...] += jnp.sum(grad, axis=0, keepdims=True)
        hidden = norm_back(grad * gain_ref[...], unit, inv_ref[...])
        hidden_ref[...] = hidden
        low = hidden.astype(BF16)
        low_ref[...] = low
        att = contract(w_ref[...], low, 1, 1).astype(BF16)
        if is_long:
            items = contract(att, place_of_item(span), 1, 1).astype(BF16)
            for h in range(heads):
                for item in range(ITEMS):
                    att_ref[item * heads + h] = items[
                        h * head_dim : (h + 1) * head_dim, item * PIECE : (item + 1) * PIECE
                    ]
            att_ref[pl.ds(ITEMS * heads, GROUP - ITEMS * heads)] = jnp.zeros(
                (GROUP - ITEMS * heads, head_dim, PIECE), BF16
            )
        else:
            att_ref[...] = att.reshape(heads, head_dim, span)

    own_rows = row_blocks(0, count, width, span)
    rows = row_blocks(first, count, width, span)
    line = pl.BlockSpec((1, width), lambda i: (0, 0))
    if is_long:
        att_spec = pl.BlockSpec((GROUP, head_dim, PIECE), lambda i: (0, 0, 0))
        att_shape = (GROUP, head_dim, PIECE)
    else:
        att_spec = pl.BlockSpec((heads, head_dim, span), lambda i: (0, 0, i))
        att_shape = (heads, head_dim, count * span)
    return pl.pallas_call(
        body,
        grid=(count,),
        in_specs=[
            rows, row_blocks(first, count, 1, span), rows, own_rows, own_rows, line,
            pl.BlockSpec((cols, width), lambda i: (0, 0)),
        ]
        + [ANYWHERE] * len(into),
        out_specs=[rows, rows, att_spec, line, line],
        out_shape=[
            jax.ShapeDtypeStruct((row_total, width), F32),
            jax.ShapeDtypeStruct((row_total, width), BF16),
            jax.ShapeDtypeStruct(att_shape, BF16),
            jax.ShapeDtypeStruct((1, width), F32),
            jax.ShapeDtypeStruct((1, width), F32),
        ],
        input_output_aliases={7 + at: at for at in range(len(into))},
        compiler_params=pltpu.CompilerParams(vmem_limit_bytes=VMEM_BYTES),
        cost_estimate=lasting(4 * count),
    )(unit, inverse, grad_sum, own, other, gain, out_weight, *into)


SLOT = 8


def first_rows(source, mine_ref, away, second, count):
    first = lax.bitwise_xor(mine_ref[0], away)
    return source[pl.ds(pl.multiple_of((first * 4 + second) * count, count), count), :]


def terms_call(body, mine, rows, columns, lines, counts, width, scratch, microseconds):
    span = ITEMS * PIECE
    shape = (4, sum(counts), width)
    return counts, pl.pallas_call(
        body,
        grid=(rows[0].shape[0] // span,),
        in_specs=[pl.BlockSpec(memory_space=pltpu.SMEM)]
        + [pl.BlockSpec((span, array.shape[1]), lambda i: (i, 0)) for array in rows]
        + [pl.BlockSpec((array.shape[0], span), lambda i: (0, i)) for array in columns]
        + [pl.BlockSpec(array.shape, lambda i: (0, 0)) for array in lines],
        out_specs=[pl.BlockSpec(shape, lambda i: (0, 0, 0))] * 4,
        out_shape=[jax.ShapeDtypeStruct(shape, BF16)] * 4,
        scratch_shapes=[pltpu.VMEM(dims, F32) for dims in scratch],
        compiler_params=pltpu.CompilerParams(vmem_limit_bytes=VMEM_BYTES),
        cost_estimate=lasting(microseconds),
    )(mine, *rows, *columns, *lines)


def outer_terms(mine, act, grad_ffn):
    units, width = act.shape[1], grad_ffn.shape[1]
    counts = [units // 16]

    def body(mine_ref, act_ref, ffn_ref, *rest):
        outs, (outer,) = rest[:4], rest[4:]

        @pl.when(pl.program_id(0) == 0)
        def _():
            outer[...] = jnp.zeros_like(outer)

        outer[...] += contract(act_ref[...], ffn_ref[...], 0, 0)

        @pl.when(pl.program_id(0) == pl.num_programs(0) - 1)
        def _():
            for away, ref in enumerate(outs):
                for second in range(4):
                    rows = first_rows(outer, mine_ref, away, second, counts[0])
                    ref[second] = rows.astype(BF16)

    return terms_call(body, mine, [act, grad_ffn], [], [], counts, width, [(units, width)], 9)


def inner_terms(mine, normed, grad_pre, mixed, grad_proj, norm_lines):
    units, width, cols = grad_pre.shape[1], normed.shape[1], mixed.shape[0]
    counts = [width // 16, width // 16, cols // 16, SLOT]

    def body(mine_ref, low_ref, pre_ref, proj_ref, mixed_ref, norm_ref, *rest):
        outs, (inner, out) = rest[:4], rest[4:]

        @pl.when(pl.program_id(0) == 0)
        def _():
            inner[...] = jnp.zeros_like(inner)
            out[...] = jnp.zeros_like(out)

        inner[...] += contract(low_ref[...], pre_ref[...], 0, 0)
        out[...] += contract(mixed_ref[...], proj_ref[...], 1, 0)

        @pl.when(pl.program_id(0) == pl.num_programs(0) - 1)
        def _():
            slot = lax.broadcasted_iota(jnp.int32, (SLOT, width), 0) == 0
            for away, ref in enumerate(outs):
                line = norm_ref[pl.ds(lax.bitwise_xor(mine_ref[0], away), 1), :]
                for second in range(4):
                    both = first_rows(inner, mine_ref, away, second, counts[0]).astype(BF16)
                    ref[second, pl.ds(0, counts[0]), :] = both[:, :width]
                    ref[second, pl.ds(counts[0], counts[1]), :] = both[:, width:]
                    tail = jnp.concatenate(
                        [
                            first_rows(out, mine_ref, away, second, counts[2]),
                            jnp.where(slot, line if second == 0 else 0.0, 0.0),
                        ],
                        axis=0,
                    )
                    ref[second, pl.ds(counts[0] + counts[1], counts[2] + SLOT), :] = (
                        tail.astype(BF16)
                    )

    return terms_call(
        body, mine, [normed, grad_pre, grad_proj], [mixed], [norm_lines], counts, width,
        [(width, units), (cols, width)], 9,
    )


def next_terms(part, counts, bits):
    places, at, pieces = 1 << len(bits), 0, []
    for index, count in enumerate(counts):
        pieces.append(part[at : at + count].reshape(places, -1, part.shape[1]))
        at, counts[index] = at + count, count // places
    return terms_for(jnp.concatenate(pieces, axis=1), bits)


def lay_out(piece, counts, order, first, is_line, outs):
    width = piece.shape[1]
    rows = piece[...].astype(F32)

    def at(count):
        return pl.ds(order * count if isinstance(order, int) else pl.multiple_of(order * count, count), count)

    if len(counts) == 1:
        outs[0][at(counts[0]), :] = rows
        return
    inner, out, norm, taps = outs
    marks = [sum(counts[:index]) for index in range(len(counts))]
    inner[at(counts[0]), pl.ds(0, width)] = rows[: marks[1]]
    inner[at(counts[1]), pl.ds(width, width)] = rows[marks[1] : marks[2]]
    out[at(counts[2]), :] = rows[marks[2] : marks[3]]
    taps[pl.ds(order, 1), :] = rows[marks[3] + 1 : marks[3] + 2]

    @pl.when(is_line)
    def _():
        norm[pl.ds(first, 1), :] = rows[marks[3] : marks[3] + 1]


def gathered_sums(gathered, counts, shapes):
    peers = gathered.shape[0]
    groups = bit_groups(peers)

    def body(in_ref, *outs):
        for at_place in range(peers):
            order = 0
            for bits in groups:
                size = 1 << len(bits)
                order = order * size + ((at_place >> bits[0]) & (size - 1))
            share = peers // 4
            lay_out(in_ref.at[at_place], counts, order, order // share, order % share == 0, outs)

    return sums_call(body, [], [gathered], shapes)


def placed_sums(mine, arrays, aways, counts, shapes):
    def body(mine_ref, *refs):
        ins, outs = refs[: len(arrays)], refs[len(arrays) :]
        for ref, pairs in zip(ins, aways):
            for piece, (first_away, second_away) in enumerate(pairs):
                first = lax.bitwise_xor(mine_ref[0], first_away)
                second = lax.bitwise_xor(mine_ref[1], second_away)
                lay_out(ref.at[piece], counts, first * 4 + second, first, second == 0, outs)

    return sums_call(body, [mine], arrays, shapes)


def sums_call(body, scalars, arrays, shapes):
    def whole(shape):
        return pl.BlockSpec(shape, lambda: (0,) * len(shape))

    return pl.pallas_call(
        body,
        in_specs=[pl.BlockSpec(memory_space=pltpu.SMEM)] * len(scalars)
        + [whole(array.shape) for array in arrays],
        out_specs=[whole(shape) for shape in shapes],
        out_shape=[jax.ShapeDtypeStruct(shape, F32) for shape in shapes],
        compiler_params=pltpu.CompilerParams(vmem_limit_bytes=VMEM_BYTES),
        cost_estimate=lasting(4),
    )(*scalars, *arrays)


def by_twos(steps):
    return len(steps) == 2 and all(len(bits) == 2 for bits in steps)


def across(array, mask):
    peers = lax.axis_size("seq")
    return lax.ppermute(array, "seq", [(i, i ^ mask) for i in range(peers)])


def gather_second(part, steps):
    if not by_twos(steps):
        return part
    came = [came[None] for came in terms_sent([part] * 4, steps[1])]
    return jnp.concatenate([part[None]] + came, axis=0)


def gather_near(own, steps):
    return (across(own[:2], 1), across(own[2:], 2)) if by_twos(steps) else ()


def gather_far(own, near, steps):
    if not near:
        return ()
    return (
        across(jnp.concatenate([own[:2], near[0]], axis=0), 2),
        across(jnp.concatenate([own[2:], near[1]], axis=0), 1),
    )


def placed(own, near, far, counts, shapes):
    place = lax.axis_index("seq")
    if not near:
        return gathered_sums(lax.all_gather(own, "seq", axis=0), counts, shapes)
    mine = jnp.stack([place & 3, (place >> 2) & 3]).astype(jnp.int32)
    aways = [
        [(0, 0), (0, 1), (0, 2), (0, 3)],
        [(1, 0), (1, 1)],
        [(2, 2), (2, 3)],
        [(2, 0), (2, 1), (3, 0), (3, 1)],
        [(1, 2), (1, 3), (3, 2), (3, 3)],
    ]
    return placed_sums(mine, [own, *near, *far], aways, counts, shapes)


def unit_back(moved_pairs, moved_values, short_parts, unit, inverse):
    heads, head_dim = unit.shape[1:3]
    short_heads, _, short_rows = short_parts[0][0].shape
    count = len(short_parts)
    span = ITEMS * PIECE
    blocks = 1 + short_rows // span
    cols = heads * head_dim

    def body(*refs):
        pairs_ref, values_ref = refs[:2]
        short_refs = refs[2 : 2 + 3 * count]
        unit_ref, inv_ref, out_ref, items = refs[2 + 3 * count :]
        block = pl.program_id(0)

        def short_part(which):
            return jnp.concatenate([short_refs[3 * at + which][...] for at in range(count)], axis=0)

        def back(which, grad):
            unit = unit_ref[which]
            along = jnp.sum(unit * grad, axis=1, keepdims=True)
            return ((grad - unit * along) * inv_ref[which]).astype(BF16).reshape(cols, span)

        @pl.when(block == 0)
        def _():
            def long_part(ref, at):
                part = pl.ds(at, head_dim)
                heads_of = [
                    jnp.concatenate([ref[h, part, :], ref[heads + h, part, :]], axis=1)
                    for h in range(heads)
                ]
                return jnp.stack(heads_of, axis=0)

            for which in range(2):
                items[pl.ds(which * cols, cols), :] = back(
                    which, long_part(pairs_ref, which * head_dim).astype(F32)
                )
            items[pl.ds(2 * cols, cols), :] = long_part(values_ref, 0).reshape(cols, span)
            out_ref[...] = contract(items[...], place_of_item(span), 1, 0).astype(BF16)

        @pl.when(block > 0)
        def _():
            out_ref[pl.ds(0, cols), :] = back(0, short_part(0))
            out_ref[pl.ds(cols, cols), :] = back(1, short_part(1))
            out_ref[pl.ds(2 * cols, cols), :] = short_part(2).astype(BF16).reshape(
                cols, span
            )

    short = pl.BlockSpec(
        (short_heads, head_dim, span), lambda i: (0, 0, jnp.maximum(i - 1, 0))
    )
    return pl.pallas_call(
        body,
        grid=(blocks,),
        in_specs=[
            pl.BlockSpec((GROUP, moved_pairs.shape[1], PIECE), lambda i: (0, 0, 0)),
            pl.BlockSpec((GROUP, head_dim, PIECE), lambda i: (0, 0, 0)),
        ]
        + [short] * (3 * count)
        + [
            pl.BlockSpec((2, heads, head_dim, span), lambda i: (0, 0, 0, i)),
            pl.BlockSpec((2, heads, 1, span), lambda i: (0, 0, 0, i)),
        ],
        out_specs=pl.BlockSpec((3 * cols, span), lambda i: (0, i)),
        out_shape=jax.ShapeDtypeStruct((3 * cols, span * blocks), BF16),
        scratch_shapes=[pltpu.VMEM((3 * cols, span), BF16)],
        compiler_params=pltpu.CompilerParams(vmem_limit_bytes=VMEM_BYTES),
        cost_estimate=lasting(8),
    )(moved_pairs, moved_values, *sum(map(tuple, short_parts), ()), unit, inverse)


def other_half(part):
    return lax.ppermute(part, "tp", [(0, 1), (1, 0)])


def bit_groups(peers):
    bits = peers.bit_length() - 1
    return [list(range(low, min(low + 2, bits))) for low in range(0, bits, 2)]


def terms_for(part, bits):
    mine = (lax.axis_index("seq") >> bits[0]) & ((1 << len(bits)) - 1)
    return [
        lax.dynamic_index_in_dim(part, mine ^ away, 0, False) for away in range(1 << len(bits))
    ]


def in_order(gathered, peers):
    sizes = [1 << len(bits) for bits in reversed(bit_groups(peers))]
    count = len(sizes)
    array = gathered.reshape(sizes + list(gathered.shape[1:]))
    array = jnp.transpose(array, list(range(count))[::-1] + [count, count + 1])
    return array.reshape(-1, gathered.shape[-1])


def terms_sent(terms, bits, first=1):
    peers = lax.axis_size("seq")
    terms = terms if first > 1 else terms[1:]
    return [
        lax.ppermute(term, "seq", [(i, i ^ (away << bits[0])) for i in range(peers)])
        for away, term in enumerate(terms, first)
    ]


def terms_gathered(own, bits):
    mine = (lax.axis_index("seq") >> bits[0]) & ((1 << len(bits)) - 1)
    every = jnp.stack([own] + terms_sent([own] * (1 << len(bits)), bits), axis=0)
    return jnp.stack(
        [
            lax.dynamic_index_in_dim(every, mine ^ place, 0, False)
            for place in range(1 << len(bits))
        ],
        axis=0,
    )


def terms_summed(own, came):
    total = own.astype(F32)
    for term in came:
        total = total + term.astype(F32)
    return total.astype(BF16)


def after(first, second):
    return lax.optimization_barrier((first, second))


def shards(
    tokens,
    short_lengths,
    query_weight,
    key_weight,
    value_weight,
    conv_kernel,
    out_weight,
    gain_one,
    bias_one,
    inner_weight,
    outer_weight,
    gain_two,
    bias_two,
    cotangent,
):
    row_total, width = tokens.shape
    heads_dev = conv_kernel.shape[0]
    head_cols = query_weight.shape[1]
    head_dim = head_cols // heads_dev
    short_rows = row_total - ITEMS * PIECE
    units = ITEMS * heads_dev
    place = lax.axis_index("seq") % GROUP
    groups = [
        [first + i for i in range(GROUP)] for first in range(0, lax.axis_size("seq"), GROUP)
    ]

    def exchange(pieces):
        return lax.all_to_all(pieces, "seq", 0, 0, axis_index_groups=groups)

    def by_position(moved, count):
        return jnp.transpose(moved, (1, 0, 2)).reshape(count, head_dim, GROUP * PIECE)

    item_ends = jnp.cumsum(short_lengths[0])
    positions = jnp.arange(short_rows, dtype=jnp.int32)
    item_ids = jnp.sum((positions[:, None] >= item_ends[None, :]).astype(jnp.int32), axis=1)
    ids_row = item_ids[None, :]
    ids_col = jnp.pad(item_ids, (REACH, REACH), constant_values=-1)[:, None]
    item_starts = jnp.concatenate([jnp.zeros((1,), jnp.int32), item_ends[:-1]])
    block_first = jnp.arange(0, short_rows, PIECE, dtype=jnp.int32)
    block_last = block_first + (PIECE - 1)
    inside = (item_starts[None, :] <= block_last[:, None]) & (
        item_ends[None, :] > block_first[:, None]
    )
    lowest = jnp.min(jnp.where(inside, item_starts[None, :], short_rows), axis=1)
    highest = jnp.max(jnp.where(inside, item_ends[None, :], 0), axis=1)
    reach = jnp.stack([lowest // PIECE, (highest + PIECE - 1) // PIECE]).astype(jnp.int32)

    last_tap = LINE - REACH - HALF_WIDTH
    lines = jnp.pad(
        conv_kernel[:, ::-1], ((0, 0), (last_tap, LINE - last_tap - CONV_WIDTH))
    )[:, None, :]
    unit_head = place % heads_dev
    long_line = lax.dynamic_index_in_dim(lines, unit_head, 0, False)

    long_send, short_pack, unit, inverse = project_in(
        tokens, query_weight, key_weight, value_weight, heads_dev
    )
    lines_of = [line[None, :] for line in (gain_one, bias_one, gain_two, bias_two)]
    gain_one, bias_one, gain_two, bias_two = lines_of

    long_moved = exchange(long_send)
    short_att, short_w, short_s = short_forward(reach, ids_row, ids_col, short_pack, lines)
    long_moved, short_att = after(long_moved, short_att)
    long_pack = by_position(long_moved, 3)
    long_att, long_w, long_s = long_forward(long_pack[0], long_pack[1], long_pack[2], long_line)

    long_att, short_att = after(long_att, short_att)
    long_att = exchange(long_att)
    mixed, short_proj = project_out_short(short_att, out_weight, row_total)
    *forward, short_ffn = feed_forward(
        ITEMS, tokens, short_proj, other_half(short_proj), gain_one, bias_one, inner_weight,
        outer_weight,
    )
    long_att, short_ffn = after(long_att, short_ffn)
    short_ffn_other = other_half(short_ffn)

    mixed, long_proj = project_out_long(long_att, out_weight, mixed)
    *forward, long_ffn = feed_forward(
        0, tokens, long_proj, other_half(long_proj), gain_one, bias_one, inner_weight,
        outer_weight, forward,
    )
    norm_unit, norm_inverse, normed_low, act_low, act_slope = forward
    *backward, long_back, long_gain_two, long_bias_two = feed_back(
        0, norm_unit, long_ffn, other_half(long_ffn), gain_one, bias_one, gain_two, bias_two,
        cotangent, act_slope, inner_weight, outer_weight,
    )
    grad_hidden, grad_proj_low, long_grad, long_gain_one, long_bias_one = project_back(
        0, norm_unit, norm_inverse, backward[1], long_back, other_half(long_back), gain_one,
        out_weight, heads_dev,
    )
    long_grad, backward, short_ffn, short_ffn_other = lax.optimization_barrier(
        (long_grad, backward, short_ffn, short_ffn_other)
    )
    long_grad = exchange(long_grad)
    *backward, short_back, short_gain_two, short_bias_two = feed_back(
        ITEMS, norm_unit, short_ffn, short_ffn_other, gain_one, bias_one, gain_two, bias_two,
        cotangent, act_slope, inner_weight, outer_weight, backward,
    )
    output, grad_sum, grad_ffn_low, grad_pre_low = backward
    grad_hidden, grad_proj_low, short_grad, short_gain_one, short_bias_one = project_back(
        1, norm_unit, norm_inverse, grad_sum, short_back, other_half(short_back), gain_one,
        out_weight, heads_dev, (grad_hidden, grad_proj_low),
    )
    norm_lines = jnp.concatenate(
        [
            long_gain_one + short_gain_one,
            long_bias_one + short_bias_one,
            long_gain_two + short_gain_two,
            long_bias_two + short_bias_two,
        ],
        axis=0,
    )

    peers = lax.axis_size("seq")
    steps = bit_groups(peers)
    mine = (lax.axis_index("seq") & 3).astype(jnp.int32)[None]
    outer_counts, outer_terms_now = outer_terms(mine, act_low, grad_ffn_low)
    outer_terms_now, grad_pre_low = after(outer_terms_now, grad_pre_low)
    outer_came = terms_sent(outer_terms_now, steps[0])
    inner_counts, inner_terms_now = inner_terms(
        mine, normed_low, grad_pre_low, mixed, grad_proj_low, norm_lines
    )
    inner_terms_now, long_grad = after(inner_terms_now, long_grad)
    long_grad = by_position(long_grad, 1)[0]
    long_dv, long_taps = long_back_values(long_pack[2], long_grad, long_w)
    outer_came, own, inner_terms_now, long_dv, long_grad = lax.optimization_barrier(
        (outer_came, outer_terms_now[0], inner_terms_now, long_dv, long_grad)
    )
    outer_part = terms_summed(own, outer_came)
    inner_came = terms_sent(inner_terms_now, steps[0])
    outer_terms_now, long_dv, long_grad = lax.optimization_barrier(
        (terms_for(outer_part, steps[1]), long_dv, long_grad)
    )
    outer_came = terms_sent(outer_terms_now, steps[1])
    long_dv = exchange(long_dv)
    long_dq, long_dk = long_back_pairs(
        long_pack[0], long_pack[1], long_pack[2], long_grad, long_s
    )
    outer_came, outer_own, inner_came, inner_own, long_dv, long_dq, long_dk, short_grad = (
        lax.optimization_barrier(
            (
                outer_came, outer_terms_now[0], inner_came, inner_terms_now[0], long_dv, long_dq,
                long_dk, short_grad,
            )
        )
    )
    outer_part = terms_summed(outer_own, outer_came)
    for bits in steps[2:]:
        terms = next_terms(outer_part, outer_counts, bits)
        outer_part = terms_summed(terms[0], terms_sent(terms, bits))
    inner_part = terms_summed(inner_own, inner_came)
    long_back = jnp.concatenate([long_dq, long_dk], axis=1)
    inner_terms_now, outer_part, long_back, short_grad = lax.optimization_barrier(
        (terms_for(inner_part, steps[1]), outer_part, long_back, short_grad)
    )
    outer_own = gather_second(outer_part, steps)
    long_back = exchange(long_back)
    inner_came = terms_sent(inner_terms_now, steps[1])
    outer_own, short_grad = after(outer_own, short_grad)
    outer_near = gather_near(outer_own, steps)
    *short_parts, short_taps = short_backward(
        reach, ids_row, ids_col, short_pack, short_grad, short_w, short_s
    )
    long_back, short_parts, short_taps, outer_own, outer_near = lax.optimization_barrier(
        (long_back, short_parts, short_taps, outer_own, outer_near)
    )
    outer_far = gather_far(outer_own, outer_near, steps)
    grads_low = unit_back(long_back, long_dv, [short_parts], unit, inverse)
    own, grads_low, outer_far = lax.optimization_barrier(
        (inner_terms_now[0], grads_low, outer_far)
    )
    inner_part = terms_summed(own, inner_came)
    for bits in steps[2:]:
        terms = next_terms(inner_part, inner_counts, bits)
        inner_part = terms_summed(terms[0], terms_sent(terms, bits))

    first_tap = BAND_ROWS - 1 - REACH + HALF_WIDTH
    taps = slice(first_tap, first_tap - CONV_WIDTH, -1)
    owner = (jnp.arange(heads_dev) == unit_head) & (place < units)
    kernel_part = short_taps[:, 0, taps] + jnp.where(owner[:, None], long_taps[:, taps], 0.0)
    taps_line = kernel_part.reshape(1, -1)
    taps_line = jnp.pad(taps_line, ((0, 0), (0, width - taps_line.shape[1]))).astype(BF16)
    (outer_sum,) = placed(
        outer_own, outer_near, outer_far, outer_counts, [outer_weight.shape]
    )
    taps_at = sum(inner_counts[:-1]) + 1
    inner_part = jnp.concatenate(
        [inner_part[:taps_at], taps_line, inner_part[taps_at + 1 :]], axis=0
    )
    inner_own = gather_second(inner_part, steps)
    inner_near = gather_near(inner_own, steps)
    inner_far = gather_far(inner_own, inner_near, steps)

    weight_part = contract(tokens, grads_low, 0, 1).astype(BF16)
    terms = terms_for(weight_part.reshape(1 << len(steps[0]), -1, 3 * head_cols), steps[0])
    terms, grads_low = after(terms, grads_low)
    came = terms_sent(terms, steps[0])
    weight_all = jnp.concatenate([query_weight, key_weight, value_weight], axis=1)
    token_own = contract(grads_low, weight_all, 0, 1).astype(BF16)
    own, token_own = after(terms[0], token_own)
    weight_part = terms_summed(own, came)
    for bits in steps[1:]:
        terms = terms_for(weight_part.reshape(1 << len(bits), -1, 3 * head_cols), bits)
        weight_part = terms_summed(terms[0], terms_sent(terms, bits))
    for bits in reversed(steps):
        weight_part = terms_gathered(weight_part, bits).reshape(-1, 3 * head_cols)
    weight_sum = weight_part.astype(F32)
    token_grad = grad_hidden + (token_own.astype(F32) + other_half(token_own).astype(F32))
    inner_sum, out_sum, norm_sums, tap_lines = placed(
        inner_own, inner_near, inner_far, inner_counts,
        [inner_weight.shape, out_weight.shape, (4, width), (peers, width)],
    )
    kernel_sum = jnp.sum(tap_lines[:, : heads_dev * CONV_WIDTH], axis=0).reshape(
        heads_dev, CONV_WIDTH
    )
    return (
        output,
        token_grad,
        weight_sum[:, :head_cols],
        weight_sum[:, head_cols : 2 * head_cols],
        weight_sum[:, 2 * head_cols :],
        kernel_sum,
        out_sum,
        norm_sums[0],
        norm_sums[1],
        inner_sum,
        outer_sum,
        norm_sums[2],
        norm_sums[3],
    )


def solution(mesh):
    rows = P("seq", None)
    columns = P(None, "tp")
    split_rows = P("tp", None)
    return jax.shard_map(
        shards,
        mesh=mesh,
        in_specs=(
            rows, rows, columns, columns, columns, split_rows, split_rows,
            P(), P(), columns, split_rows, P(), P(), rows,
        ),
        out_specs=(
            rows, rows, columns, columns, columns, split_rows, split_rows,
            P(), P(), columns, split_rows, P(), P(),
        ),
        check_vma=False,
    )
```
